32 devices in a mesh: dp: 16 (over z, x, core), fsdp: 2 (over y).
Axes of the slice: x: 2, y: 2, z: 4, core: 2. Of those that a mesh axis runs over, the one named last changes fastest.
Arguments:
- tokens: bfloat16 [8192, 1024], P(('dp', 'fsdp')), may hold values from -6 to 6
- head_grad: bfloat16 [8192, 1024], P(('dp', 'fsdp')), may hold values from -6 to 6
- w_qkv: bfloat16 [1024, 3072], P(('dp', 'fsdp')), may hold values from -0.1875 to 0.1875
- w_out: bfloat16 [1024, 1024], P(('dp', 'fsdp')), may hold values from -0.75 to 0.75
- w_up: bfloat16 [1024, 4096], P(('dp', 'fsdp')), may hold values from -0.1875 to 0.1875
- w_down: bfloat16 [4096, 1024], P(('dp', 'fsdp')), may hold values from -0.09375 to 0.09375
- gains: bfloat16 [3, 1024], P(None, ('dp', 'fsdp')), may hold values from 0.25 to 1.75
- shifts: bfloat16 [3, 1024], P(None, ('dp', 'fsdp')), may hold values from -1 to 1
- biases: bfloat16 [4, 1024], P(None, ('dp', 'fsdp')), may hold values from -1 to 1
- up_bias: bfloat16 [4096], P(('dp', 'fsdp')), may hold values from -1 to 1
- seq_lengths: int32 [16, 3], P('dp'), may hold values from 1 to 510, as said below
- neigh_keys: bfloat16 [512, 128, 1024], P(('dp', 'fsdp')), may hold values from -6 to 6
- neigh_ids: int32 [512, 128], P(('dp', 'fsdp')), may hold values from 0 to 267743, as said below
- neigh_counts: int32 [512], P(('dp', 'fsdp')), may hold values from 1 to 128
- targets: int32 [8192], P(('dp', 'fsdp')), may hold values from 0 to 267743, as said below
- p_lm: float32 [8192], P(('dp', 'fsdp')), may hold values from 0.001 to 0.5
Outputs:
- state: bfloat16 [8192, 1024], P(('dp', 'fsdp'))
- token_loss: float32 [8192], P(('dp', 'fsdp'))
- grad_input: bfloat16 [8192, 1024], P(('dp', 'fsdp'))
- grad_w_qkv: float32 [1024, 3072], P(('dp', 'fsdp'))
- grad_w_out: float32 [1024, 1024], P(('dp', 'fsdp'))
- grad_w_up: float32 [1024, 4096], P(('dp', 'fsdp'))
- grad_w_down: float32 [4096, 1024], P(('dp', 'fsdp'))
- grad_gains: float32 [3, 1024], P(None, ('dp', 'fsdp'))
- grad_shifts: float32 [3, 1024], P(None, ('dp', 'fsdp'))
- grad_biases: float32 [4, 1024], P(None, ('dp', 'fsdp'))
- grad_up_bias: float32 [4096], P(('dp', 'fsdp'))
The draws below stay inside these ranges and needn't reach their ends.
Inputs may be any that keep to these rules, and one draw needn't show every extreme that they name: `seq_lengths`: each row holds the lengths of a group's three sequences in order; they sum to 512, the first and the last lie between 1 and 32. `neigh_ids`: token ids of the vocabulary; common tokens recur, and many neighbours store a target of their own span. `targets`: token ids of the vocabulary.
All inputs are finite; a program needn't handle non-finite values.
Results may differ from the reference program's by a relative error of at most 0.013.
Values may be sent and summed in bfloat16 or wider, within the bound.
A program may use at most 192 MiB of HBM per device.

```python
import math
import jax
import jax.numpy as jnp
import numpy as np
from jax import lax

D = 1024
HEADS = 16
HEAD_DIM = 64
FF = 4096
VOCAB = 267744
NEIGH = 128
SPAN = 16
TOK_DEV = 256
GROUP = 512
GROUPS = 16
TOKENS = 8192
SPANS = 512
N_DP = 16


zipf_terms = np.arange(1, 4097, dtype=np.float32) ** np.float32(-1.1)


zipf_edges = np.floor(np.cumsum(zipf_terms, dtype=np.float32) / np.sum(zipf_terms, dtype=np.float32) * np.float32(1048576.0)).astype(np.int32)[:-1]


def token_draws(key):
    shared = jax.random.fold_in(key, 101)
    key_offset, key_targets, key_free, key_pick, key_copy = jax.random.split(shared, 5)
    offset = jax.random.randint(key_offset, (), 0, VOCAB)
    edges = jnp.asarray(zipf_edges)

    def ids_of(sub_key, shape):
        uniform_int = jax.random.randint(sub_key, shape, 0, 1048576)
        rank = jnp.searchsorted(edges, uniform_int, side='right').astype(jnp.int32)
        return (rank * 65519 + offset) % VOCAB
    target_ids = ids_of(key_targets, (TOKENS,))
    span_count = TOKENS // SPAN
    free_ids = ids_of(key_free, (span_count, NEIGH))
    pick = jax.random.randint(key_pick, (span_count, NEIGH), 0, SPAN)
    copy_flag = jax.random.randint(key_copy, (span_count, NEIGH), 0, 2)
    chosen = jnp.take_along_axis(target_ids.reshape(span_count, SPAN), pick, axis=1)
    stored = jnp.where(copy_flag == 1, chosen, free_ids)
    return (target_ids.astype(jnp.int32), stored.astype(jnp.int32))


def draw_targets(key, part):
    target_ids, stored = token_draws(key)
    return target_ids


def draw_neigh_ids(key, part):
    target_ids, stored = token_draws(key)
    return stored


def draw_seq_lengths(key, part):
    key = jax.random.fold_in(key, 11)
    key_first, key_last = jax.random.split(key)
    first_len = jax.random.randint(key_first, (GROUPS, 1), 1, TOK_DEV // 8 + 1)
    last_len = jax.random.randint(key_last, (GROUPS, 1), 1, TOK_DEV // 8 + 1)
    middle_len = GROUP - first_len - last_len
    return jnp.concatenate([first_len, middle_len, last_len], 1).astype(jnp.int32)


def place_ends(array, stream_key, low, top_value):
    longest = array.shape.index(max(array.shape))
    spots = []
    for shift in (0, 1):
        where = [jax.random.randint(jax.random.fold_in(stream_key, axis), (), 0, length) for axis, length in enumerate(array.shape)]
        where[longest] = (where[longest] + shift) % array.shape[longest]
        spots.append(tuple(where))
    return array.at[spots[0]].set(low).at[spots[1]].set(top_value)


def block_levels(stream_key, dims, cuts, smallest, top_value):
    def one(dim, shards_of):
        steps = jax.random.uniform(jax.random.fold_in(jax.random.fold_in(stream_key, 6), dim), (shards_of,), jnp.float32, smallest / len(cuts), top_value / len(cuts))
        return jnp.repeat(jnp.exp(steps), dims[dim] // shards_of).reshape((-1,) + (1,) * (len(dims) - dim - 1))

    factor_of = one(*cuts[0])
    for cut in cuts[1:]:
        factor_of = factor_of * one(*cut)
    return factor_of


def normal_values(own_key, shape, scale, bound, shards=(), kind=jnp.bfloat16):
    factor_of = block_levels(own_key, shape, shards, -0.22, 0.18) if shards else 1.0
    array = jax.random.normal(own_key, shape, jnp.float32) * scale * factor_of
    return jnp.minimum(jnp.maximum(array, -bound), bound).astype(kind)


def setup_inputs(seed: int = 0) -> dict:
    key_list = jax.random.split(jax.random.key(seed), 17)
    return {
        "tokens": normal_values(key_list[0], (TOKENS, D), 1.0, 6.0, ((0, 32),)),
        "head_grad": normal_values(key_list[1], (TOKENS, D), 1.0, 6.0, ((0, 32),)),
        "w_qkv": normal_values(key_list[2], (D, 3 * D), D ** -0.5, 0.1875, ((0, 32),)),
        "w_out": normal_values(key_list[3], (D, D), (D // 16) ** -0.5, 0.75, ((0, 32),)),
        "w_up": normal_values(key_list[4], (D, FF), D ** -0.5, 0.1875, ((0, 32),)),
        "w_down": normal_values(key_list[5], (FF, D), FF ** -0.5, 0.09375, ((0, 32),)),
        "gains": jnp.clip(1.0 + 0.15 * jax.random.normal(key_list[6], (3, D), jnp.float32), 0.25, 1.75).astype(jnp.bfloat16),
        "shifts": normal_values(key_list[7], (3, D), 0.2, 1.0, ((1, 32),)),
        "biases": normal_values(key_list[8], (4, D), 0.2, 1.0, ((1, 32),)),
        "up_bias": normal_values(key_list[9], (FF,), 0.2, 1.0, ((0, 32),)),
        "seq_lengths": draw_seq_lengths(jax.random.fold_in(key_list[16], 71), 0),
        "neigh_keys": normal_values(key_list[11], (SPANS, NEIGH, D), 1.0, 6.0, ((0, 32),)),
        "neigh_ids": draw_neigh_ids(jax.random.fold_in(key_list[16], 71), 0),
        "neigh_counts": place_ends(jax.random.randint(key_list[13], (SPANS,), 1, NEIGH + 1), jax.random.fold_in(key_list[13], 1), 1, NEIGH).astype(jnp.int32),
        "targets": draw_targets(jax.random.fold_in(key_list[16], 71), 0),
        "p_lm": jnp.clip(jnp.exp(math.log(0.5) - 6.214608 * jax.random.uniform(key_list[15], (TOKENS,), jnp.float32) ** block_levels(key_list[15], (TOKENS,), ((0, 32),), -0.2, 0.2)), 0.001, 0.5),
    }


EPSILON = 1e-05
MIX_WEIGHT = 0.25
PRECISION_HIGH = lax.Precision.HIGHEST

@jax.custom_vjp
def low(v):
    return lax.optimization_barrier(v.astype(jnp.bfloat16)).astype(jnp.float32)

@jax.custom_vjp
def low_back(v):
    return v

def low_keep(v):
    return (low(v), None)

def low_pass(kept, grad):
    return (grad,)

def back_keep(v):
    return (v, None)

def back_low(kept, grad):
    return (low(grad),)
low.defvjp(low_keep, low_pass)
low_back.defvjp(back_keep, back_low)

def norm_rows(values, gain_row, shift_row):
    center = values - lax.optimization_barrier(jnp.mean(values, -1, keepdims=True))
    inverse = lax.rsqrt(lax.optimization_barrier(jnp.mean(center * center, -1, keepdims=True)) + EPSILON)
    return center * inverse * gain_row + shift_row

def matmul_high(left, right):
    return jnp.dot(left, right, precision=PRECISION_HIGH)

def segment_of(lengths, positions):
    first_end = lengths[0]
    second_end = lengths[0] + lengths[1]
    return (positions >= first_end).astype(jnp.int32) + (positions >= second_end).astype(jnp.int32)

def group_attention(packed):
    queries, key_rows, value_rows, lengths = packed
    group_size = queries.shape[0]
    positions = jnp.arange(group_size, dtype=jnp.int32)
    segment = segment_of(lengths, positions)
    allowed = (segment[:, None] == segment[None, :]) & (positions[None, :] <= positions[:, None])
    query_heads = queries.reshape(group_size, HEADS, HEAD_DIM)
    key_heads = key_rows.reshape(group_size, HEADS, HEAD_DIM)
    value_heads = value_rows.reshape(group_size, HEADS, HEAD_DIM)
    raw_scores = low_back(jnp.einsum('qhe,khe->hqk', query_heads, key_heads, precision=PRECISION_HIGH) / math.sqrt(HEAD_DIM))
    masked = jnp.where(allowed[None], raw_scores, -jnp.inf)
    row_top = lax.optimization_barrier(jnp.max(masked, -1, keepdims=True))
    exp_values = jnp.exp(masked - row_top)
    prob_values = low(exp_values / lax.optimization_barrier(jnp.sum(exp_values, -1, keepdims=True)))
    output = jnp.einsum('hqk,khe->qhe', prob_values, value_heads, precision=PRECISION_HIGH)
    return output.reshape(group_size, HEADS * HEAD_DIM)

def knn_loss(query, keys_f32, neigh_ids, neigh_counts, targets, p_lm):
    span_count = keys_f32.shape[0]
    query_low = low(query).reshape(span_count, -1, D)
    key_square = lax.optimization_barrier(jnp.sum(keys_f32 * keys_f32, -1))
    raw_logits = jnp.einsum('sqd,snd->sqn', query_low, keys_f32, precision=PRECISION_HIGH)
    logits = low_back((2.0 * raw_logits - key_square[:, None, :]) * (0.5 / math.sqrt(D)))
    slot_valid = jnp.arange(NEIGH, dtype=jnp.int32)[None, :] < neigh_counts[:, None]
    masked = jnp.where(slot_valid[:, None, :], logits, -jnp.inf)
    exp_values = jnp.exp(masked - lax.optimization_barrier(jnp.max(masked, -1, keepdims=True)))
    weights = exp_values / lax.optimization_barrier(jnp.sum(exp_values, -1, keepdims=True))
    id_match = neigh_ids[:, None, :] == targets.reshape(span_count, -1)[:, :, None]
    knn_prob = lax.optimization_barrier(jnp.sum(jnp.where(id_match, weights, 0.0), -1))
    mixture = MIX_WEIGHT * knn_prob + (1.0 - MIX_WEIGHT) * p_lm.reshape(span_count, -1)
    return -jnp.log(mixture).reshape(-1)

def forward(tokens_f32, w_qkv, w_out, w_up, w_down, gains, shifts, biases, up_bias, seq_lengths, keys_f32, neigh_ids, neigh_counts, targets, p_lm):
    normed_in = low(norm_rows(tokens_f32, gains[0], shifts[0]))
    qkv_bias = jnp.concatenate([biases[0], jnp.zeros_like(biases[0]), biases[1]])
    qkv = low(low_back(matmul_high(normed_in, w_qkv) + qkv_bias))
    query_part = qkv[:, :D].reshape(N_DP, -1, D)
    key_part = qkv[:, D:2 * D].reshape(N_DP, -1, D)
    value_part = qkv[:, 2 * D:].reshape(N_DP, -1, D)
    attended = lax.map(jax.checkpoint(group_attention), (query_part, key_part, value_part, seq_lengths))
    attended = low(low_back(attended.reshape(-1, D)))
    hidden_one = tokens_f32 + low_back(matmul_high(attended, w_out) + biases[2])
    normed_mid = low(norm_rows(hidden_one, gains[1], shifts[1]))
    pre_act = low_back(matmul_high(normed_mid, w_up) + up_bias)
    gelu_out = low(jax.nn.gelu(pre_act))
    state_f32 = hidden_one + low_back(matmul_high(gelu_out, w_down) + biases[3])
    query = norm_rows(state_f32, gains[2], shifts[2])
    token_loss = knn_loss(query, keys_f32, neigh_ids, neigh_counts, targets, p_lm)
    return (state_f32, query, token_loss)

def reference(tokens, head_grad, w_qkv, w_out, w_up, w_down, gains, shifts, biases, up_bias, seq_lengths, neigh_keys, neigh_ids, neigh_counts, targets, p_lm):
    keys_f32 = neigh_keys.astype(jnp.float32)

    def wrapped(tokens_f32, qkv_w, out_w, up_w, down_w, gain_rows, shift_rows, bias_rows, hidden_bias):
        return forward(tokens_f32, qkv_w, out_w, up_w, down_w, gain_rows, shift_rows, bias_rows, hidden_bias, seq_lengths, keys_f32, neigh_ids, neigh_counts, targets, p_lm)
    outputs, pull = jax.vjp(wrapped, tokens.astype(jnp.float32), w_qkv.astype(jnp.float32), w_out.astype(jnp.float32), w_up.astype(jnp.float32), w_down.astype(jnp.float32), gains.astype(jnp.float32), shifts.astype(jnp.float32), biases.astype(jnp.float32), up_bias.astype(jnp.float32))
    state_f32, query, token_loss = outputs
    grads = pull((jnp.zeros_like(state_f32), head_grad.astype(jnp.float32), jnp.ones_like(token_loss)))
    return (state_f32.astype(jnp.bfloat16), token_loss, grads[0].astype(jnp.bfloat16), grads[1], grads[2], grads[3], grads[4], grads[5], grads[6], grads[7], grads[8])
```

```python
import math

import jax
import jax.numpy as jnp
from jax import lax
from jax.experimental import pallas as pl
from jax.experimental.pallas import tpu as pltpu
from jax.sharding import PartitionSpec as P

HEADS = 16


EPSILON = 1e-05
MIX_WEIGHT = 0.25


def norm_rows(values, gain_row, shift_row):
    center = values - jnp.mean(values, -1, keepdims=True)
    inverse = lax.rsqrt(jnp.mean(center * center, -1, keepdims=True) + EPSILON)
    unit_rows = center * inverse
    return (unit_rows * gain_row + shift_row, unit_rows, inverse)


def norm_back(grad_rows, unit_rows, inverse, gain_row):
    scaled = grad_rows * gain_row
    first_mean = jnp.mean(scaled, -1, keepdims=True)
    second_mean = jnp.mean(scaled * unit_rows, -1, keepdims=True)
    grad_values = inverse * (scaled - first_mean - unit_rows * second_mean)
    return (grad_values, jnp.sum(grad_rows * unit_rows, 0), jnp.sum(grad_rows, 0))


def contract_rows(left, right):
    return lax.dot_general(
        left, right, (((0,), (0,)), ((), ())), preferred_element_type=jnp.float32
    )


def times_transposed(left, right):
    return lax.dot_general(
        left, right, (((1,), (1,)), ((), ())), preferred_element_type=jnp.float32
    )


def segment_of(lengths, positions):
    first_end = lengths[0]
    second_end = lengths[0] + lengths[1]
    return (positions >= first_end).astype(jnp.int32) + (positions >= second_end).astype(jnp.int32)


def on_device(
    tokens,
    head_grad,
    w_qkv,
    w_out,
    w_up,
    w_down,
    gains,
    shifts,
    biases,
    up_bias,
    seq_lengths,
    neigh_keys,
    neigh_ids,
    neigh_counts,
    targets,
    p_lm,
):
    gathered = (
        lax.all_gather(w_qkv, ("dp", "fsdp"), axis=0, tiled=True),
        lax.all_gather(w_out, ("dp", "fsdp"), axis=0, tiled=True),
        lax.all_gather(w_up, ("dp", "fsdp"), axis=0, tiled=True),
        lax.all_gather(w_down, ("dp", "fsdp"), axis=0, tiled=True),
        lax.all_gather(gains, ("dp", "fsdp"), axis=1, tiled=True),
        lax.all_gather(shifts, ("dp", "fsdp"), axis=1, tiled=True),
        lax.all_gather(biases, ("dp", "fsdp"), axis=1, tiled=True),
        lax.all_gather(up_bias, ("dp", "fsdp"), axis=0, tiled=True),
    )
    row_count, feature_width = tokens.shape
    head_count = HEADS
    head_depth = feature_width // head_count
    score_scale = 1.0 / math.sqrt(head_depth)
    gain_rows = gathered[4].astype(jnp.float32)
    shift_rows = gathered[5].astype(jnp.float32)
    bias_rows = gathered[6].astype(jnp.float32)
    tokens_f32 = tokens.astype(jnp.float32)
    normed_in, unit_in, inverse_in = norm_rows(tokens_f32, gain_rows[0], shift_rows[0])
    normed_in_low = normed_in.astype(jnp.bfloat16)
    qkv_bias = jnp.concatenate([bias_rows[0], jnp.zeros_like(bias_rows[0]), bias_rows[1]])
    qkv = (
        jnp.dot(normed_in_low, gathered[0], preferred_element_type=jnp.float32) + qkv_bias
    ).astype(jnp.bfloat16)
    query_heads = qkv[:, :feature_width].reshape(row_count, head_count, head_depth)
    kv_local = qkv[:, feature_width:]
    kv_group = lax.all_gather(kv_local, "fsdp", axis=0, tiled=True)
    group_size = kv_group.shape[0]
    part_count = lax.axis_size("fsdp")
    block_rows = row_count * min(part_count, max(1, 512 // row_count))
    block_count = group_size // block_rows
    first_row = lax.axis_index("fsdp") * row_count
    last_row = first_row + row_count - 1
    lengths = seq_lengths[0]
    query_pos = first_row + jnp.arange(row_count, dtype=jnp.int32)
    query_seg = segment_of(lengths, query_pos)

    def scores_of(source, block_start):
        key_piece = lax.dynamic_slice_in_dim(source, block_start, block_rows, 0)
        key_heads = key_piece[:, :feature_width].reshape(block_rows, head_count, head_depth)
        value_heads = key_piece[:, feature_width:].reshape(block_rows, head_count, head_depth)
        key_pos = block_start + jnp.arange(block_rows, dtype=jnp.int32)
        allowed = (segment_of(lengths, key_pos)[None, :] == query_seg[:, None]) & (
            key_pos[None, :] <= query_pos[:, None]
        )
        raw_scores = (
            jnp.einsum("qhe,khe->hqk", query_heads, key_heads, preferred_element_type=jnp.float32)
            * score_scale
        )
        return (jnp.where(allowed[None], raw_scores, -jnp.inf), key_heads, value_heads)

    def keep_same(kept_value):
        return kept_value

    def stats_step(block_index, stats):
        block_start = block_index * block_rows

        def stats_block_work(pair):
            row_top, row_total = pair
            masked, key_heads, value_heads = scores_of(kv_group, block_start)
            new_top = jnp.maximum(row_top, jnp.max(masked, -1))
            safe_top = jnp.where(new_top > -jnp.inf, new_top, 0.0)
            row_total = row_total * jnp.exp(row_top - safe_top) + jnp.sum(
                jnp.exp(masked - safe_top[..., None]), -1
            )
            return (new_top, row_total)

        return lax.cond(block_start <= last_row, stats_block_work, keep_same, stats)

    start_stats = (
        jnp.full((head_count, row_count), -jnp.inf, jnp.float32),
        jnp.zeros((head_count, row_count), jnp.float32),
    )
    row_top, row_total = lax.fori_loop(0, block_count, stats_step, start_stats)
    log_total = row_top + jnp.log(row_total)

    def value_step(block_index, value_acc):
        block_start = block_index * block_rows

        def value_block_work(value_sum):
            masked, key_heads, value_heads = scores_of(kv_group, block_start)
            prob_low = jnp.exp(masked - log_total[..., None]).astype(jnp.bfloat16)
            return value_sum + jnp.einsum(
                "hqk,khe->qhe", prob_low, value_heads, preferred_element_type=jnp.float32
            )

        return lax.cond(block_start <= last_row, value_block_work, keep_same, value_acc)

    attended = lax.fori_loop(
        0, block_count, value_step, jnp.zeros((row_count, head_count, head_depth), jnp.float32)
    )
    attended = attended.reshape(row_count, feature_width)
    attended_low = attended.astype(jnp.bfloat16)
    hidden_one = tokens_f32 + (
        jnp.dot(attended_low, gathered[1], preferred_element_type=jnp.float32) + bias_rows[2]
    )
    normed_mid, unit_mid, inverse_mid = norm_rows(hidden_one, gain_rows[1], shift_rows[1])
    normed_mid_low = normed_mid.astype(jnp.bfloat16)
    pre_act = jnp.dot(normed_mid_low, gathered[2], preferred_element_type=jnp.float32) + gathered[
        7
    ].astype(jnp.float32)
    gelu_low = jax.nn.gelu(pre_act).astype(jnp.bfloat16)
    state_f32 = hidden_one + (
        jnp.dot(gelu_low, gathered[3], preferred_element_type=jnp.float32) + bias_rows[3]
    )
    query, unit_out, inverse_out = norm_rows(state_f32, gain_rows[2], shift_rows[2])
    span_count = neigh_keys.shape[0]
    slot_count = neigh_keys.shape[1]
    knn_scale = 0.5 / math.sqrt(feature_width)
    query_low = query.astype(jnp.bfloat16).reshape(span_count, -1, feature_width)
    key_square = jnp.einsum(
        "snd,snd->sn", neigh_keys, neigh_keys, preferred_element_type=jnp.float32
    )
    raw_logits = jnp.einsum(
        "sqd,snd->sqn", query_low, neigh_keys, preferred_element_type=jnp.float32
    )
    logits = (2.0 * raw_logits - key_square[:, None, :]) * knn_scale
    slot_valid = jnp.arange(slot_count, dtype=jnp.int32)[None, :] < neigh_counts[:, None]
    masked_logits = jnp.where(slot_valid[:, None, :], logits, -jnp.inf)
    exp_values = jnp.exp(masked_logits - jnp.max(masked_logits, -1, keepdims=True))
    weights = exp_values / jnp.sum(exp_values, -1, keepdims=True)
    id_match = neigh_ids[:, None, :] == targets.reshape(span_count, -1)[:, :, None]
    knn_prob = jnp.sum(jnp.where(id_match, weights, 0.0), -1)
    mixture = MIX_WEIGHT * knn_prob + (1.0 - MIX_WEIGHT) * p_lm.reshape(span_count, -1)
    token_loss = -jnp.log(mixture).reshape(row_count)
    match_f32 = jnp.where(id_match, 1.0, 0.0)
    dlogits = (
        -(MIX_WEIGHT / mixture)[..., None] * weights * (match_f32 - knn_prob[..., None])
    ).astype(jnp.bfloat16)
    knn_grad = jnp.einsum(
        "sqn,snd->sqd", dlogits, neigh_keys, preferred_element_type=jnp.float32
    ) * (2.0 * knn_scale)
    dquery = head_grad.astype(jnp.float32) + knn_grad.reshape(row_count, feature_width)
    back_params = (
        lax.all_gather(w_qkv, ("dp", "fsdp"), axis=0, tiled=True),
        lax.all_gather(w_out, ("dp", "fsdp"), axis=0, tiled=True),
        lax.all_gather(w_up, ("dp", "fsdp"), axis=0, tiled=True),
        lax.all_gather(w_down, ("dp", "fsdp"), axis=0, tiled=True),
        lax.all_gather(gains, ("dp", "fsdp"), axis=1, tiled=True),
        lax.all_gather(shifts, ("dp", "fsdp"), axis=1, tiled=True),
        lax.all_gather(biases, ("dp", "fsdp"), axis=1, tiled=True),
        lax.all_gather(up_bias, ("dp", "fsdp"), axis=0, tiled=True),
    )
    kv_back = lax.all_gather(kv_local, "fsdp", axis=0, tiled=True)
    gain_back = back_params[4].astype(jnp.float32)
    dstate, gain_grad_out, shift_grad_out = norm_back(dquery, unit_out, inverse_out, gain_back[2])
    dstate_low = dstate.astype(jnp.bfloat16)
    grad_w_down = contract_rows(gelu_low, dstate_low)
    bias_grad_down = jnp.sum(dstate_low.astype(jnp.float32), 0)
    dgelu = times_transposed(dstate_low, back_params[3])
    gelu_value, gelu_pull = jax.vjp(jax.nn.gelu, pre_act)
    dpre_low = gelu_pull(dgelu)[0].astype(jnp.bfloat16)
    grad_w_up = contract_rows(normed_mid_low, dpre_low)
    grad_up_bias = jnp.sum(dpre_low.astype(jnp.float32), 0)
    dnormed_mid = times_transposed(dpre_low, back_params[2])
    dhidden_part, gain_grad_mid, shift_grad_mid = norm_back(
        dnormed_mid, unit_mid, inverse_mid, gain_back[1]
    )
    dhidden_one = dstate + dhidden_part
    dhidden_low = dhidden_one.astype(jnp.bfloat16)
    grad_w_out = contract_rows(attended_low, dhidden_low)
    bias_grad_out = jnp.sum(dhidden_low.astype(jnp.float32), 0)
    dattended_low = times_transposed(dhidden_low, back_params[1]).astype(jnp.bfloat16)
    dattended_heads = dattended_low.reshape(row_count, head_count, head_depth)
    delta_rows = jnp.sum(
        dattended_heads.astype(jnp.float32) * attended.reshape(row_count, head_count, head_depth),
        -1,
    ).T

    def both_grad_step(block_index, grad_pair):
        block_start = block_index * block_rows

        def both_block_work(pair):
            dquery_acc, dkv_group = pair
            masked, key_heads, value_heads = scores_of(kv_back, block_start)
            prob_values = jnp.exp(masked - log_total[..., None])
            prob_low = prob_values.astype(jnp.bfloat16)
            dprob = jnp.einsum(
                "qhe,khe->hqk", dattended_heads, value_heads, preferred_element_type=jnp.float32
            )
            dscores = (prob_values * (dprob - delta_rows[..., None])).astype(jnp.bfloat16)
            dquery_acc = dquery_acc + jnp.einsum(
                "hqk,khe->qhe", dscores, key_heads, preferred_element_type=jnp.float32
            )
            dkey_heads = (
                jnp.einsum("hqk,qhe->khe", dscores, query_heads, preferred_element_type=jnp.float32)
                * score_scale
            )
            dvalue_heads = jnp.einsum(
                "hqk,qhe->khe", prob_low, dattended_heads, preferred_element_type=jnp.float32
            )
            block_grad = jnp.concatenate(
                [
                    dkey_heads.reshape(block_rows, feature_width),
                    dvalue_heads.reshape(block_rows, feature_width),
                ],
                1,
            )
            current = lax.dynamic_slice_in_dim(dkv_group, block_start, block_rows, 0)
            return (
                dquery_acc,
                lax.dynamic_update_slice_in_dim(dkv_group, current + block_grad, block_start, 0),
            )

        return lax.cond(block_start <= last_row, both_block_work, keep_same, grad_pair)

    zero_dquery = jnp.zeros((row_count, head_count, head_depth), jnp.float32)
    start_grads = (zero_dquery, jnp.zeros((group_size, 2 * feature_width), jnp.float32))
    dquery_acc, dkv_group = lax.fori_loop(0, block_count, both_grad_step, start_grads)
    dkv_mine = lax.psum_scatter(
        dkv_group.astype(jnp.bfloat16), "fsdp", scatter_dimension=0, tiled=True
    ).astype(jnp.float32)
    dqkv_low = jnp.concatenate(
        [(dquery_acc * score_scale).reshape(row_count, feature_width), dkv_mine], 1
    ).astype(jnp.bfloat16)
    grad_w_qkv = contract_rows(normed_in_low, dqkv_low)
    column_sums = jnp.sum(dqkv_low.astype(jnp.float32), 0)
    dnormed_in = times_transposed(dqkv_low, back_params[0])
    dinput_part, gain_grad_in, shift_grad_in = norm_back(
        dnormed_in, unit_in, inverse_in, gain_back[0]
    )
    grad_input = (dhidden_one + dinput_part).astype(jnp.bfloat16)
    grad_gains = jnp.stack([gain_grad_in, gain_grad_mid, gain_grad_out])
    grad_shifts = jnp.stack([shift_grad_in, shift_grad_mid, shift_grad_out])
    grad_biases = jnp.stack(
        [
            column_sums[:feature_width],
            column_sums[2 * feature_width :],
            bias_grad_out,
            bias_grad_down,
        ]
    )
    summed = (
        lax.psum_scatter(grad_w_qkv, ("dp", "fsdp"), scatter_dimension=0, tiled=True),
        lax.psum_scatter(grad_w_out, ("dp", "fsdp"), scatter_dimension=0, tiled=True),
        lax.psum_scatter(grad_w_up, ("dp", "fsdp"), scatter_dimension=0, tiled=True),
        lax.psum_scatter(grad_w_down, ("dp", "fsdp"), scatter_dimension=0, tiled=True),
        lax.psum_scatter(grad_gains, ("dp", "fsdp"), scatter_dimension=1, tiled=True),
        lax.psum_scatter(grad_shifts, ("dp", "fsdp"), scatter_dimension=1, tiled=True),
        lax.psum_scatter(grad_biases, ("dp", "fsdp"), scatter_dimension=1, tiled=True),
        lax.psum_scatter(grad_up_bias, ("dp", "fsdp"), scatter_dimension=0, tiled=True),
    )
    return (
        state_f32.astype(jnp.bfloat16),
        token_loss,
        grad_input,
        summed[0],
        summed[1],
        summed[2],
        summed[3],
        summed[4],
        summed[5],
        summed[6],
        summed[7],
    )


VMEM_LIMIT = 63 << 20
BF = jnp.bfloat16
F32 = jnp.float32
MESH = pl.DeviceIdType.MESH
NEG = -1e30


def dot(left, right, left_dim=1, right_dim=0):
    return lax.dot_general(
        left, right, (((left_dim,), (right_dim,)), ((), ())), preferred_element_type=F32
    )


def unit_of(values):
    center = values - jnp.mean(values, -1, keepdims=True)
    inverse = lax.rsqrt(jnp.mean(center * center, -1, keepdims=True) + EPSILON)
    return center * inverse, inverse


def ln_back(grad_rows, unit_rows, inverse, gain_row):
    scaled = grad_rows * gain_row
    first_mean = jnp.mean(scaled, -1, keepdims=True)
    second_mean = jnp.mean(scaled * unit_rows, -1, keepdims=True)
    return inverse * (scaled - first_mean - unit_rows * second_mean)


def col_sum(values):
    return jnp.sum(values, 0, keepdims=True)


def gelu_pair(u):
    k0 = math.sqrt(2.0 / math.pi)
    square = u * u
    t = jnp.tanh(u * (k0 + (k0 * 0.044715) * square))
    half = 0.5 * (1.0 + t)
    slope = half + (0.5 * u) * (1.0 - t * t) * (k0 + (3.0 * k0 * 0.044715) * square)
    return u * half, slope


def block_kernel(
    tokens, head_grad, w_qkv, w_out, w_up, w_down, packet, seq, keys_in, ids, counts, targets, p_lm,
    state_out, loss_out, gin_out, gqkv_out, gout_out, gup_out, gdown_out, gpk_out,
    wA, wD, wO, pk, prm, ubias, tokg, ni, qkv, mask, att_h, att_f, h1, nmg, gelu, slope, st, prec,
    hgrad, ksq, match, dsg, dnm, dnr, dattg, dqkv, dnr2, sendb, lowb, gA, gD, gO, gP, dRA, xRA, zRA,
    dRD, xRD, zRD, dRO, yRO, xRO, zRO, dRP, yRP, xRP, zRP, finA, finD, finO, pg, dub, lossb, lsem,
    ysend, yrecv, zsend, zrecv, xsend, xrecv, csend, crecv, osem, msend, mrecv, rcs, rcr, rxs, rxr, rzs,
    rzr, rys, ryr, rfl, kn_sem,
):
    dp = lax.axis_index("dp")
    y = lax.axis_index("fsdp")
    z = dp // 4
    x = (dp // 2) % 2
    c = dp % 2
    oy = 1 - y
    ox = 1 - x
    oc = 1 - c

    def dev(zz, xx, cc, yy):
        return ((zz * 2 + xx) * 2 + cc, yy)

    zs = [(z + j) % 4 for j in (1, 2, 3)]
    zdev = [dev(zz, x, c, y) for zz in zs]
    xdev = dev(z, ox, c, y)
    ydev = dev(z, x, c, oy)
    cdev = dev(z, x, oc, y)

    def rc(src, dst_ref, ss, rs, to):
        return pltpu.make_async_remote_copy(
            src_ref=src, dst_ref=dst_ref, send_sem=ss, recv_sem=rs, device_id=to, device_id_type=MESH
        )

    def lc(src, dst_ref, sem):
        return pltpu.make_async_copy(src, dst_ref, sem)

    pending = []

    my_rows = pl.ds(pl.multiple_of(y * 32, 32), 32)

    def up_cols(j, i, yy):
        return pl.ds(pl.multiple_of((8 * j + 2 * i + yy) * 128, 128), 128)

    def part_cols(part, yy):
        return pl.ds(pl.multiple_of(part * 1024 + yy * 512, 512), 512)

    lc(packet, pk.at[z, x, c, y], lsem.at[12]).start()
    for s in range(3):
        lc(w_qkv.at[:, part_cols(s, y)], wA.at[s, z, x, c, my_rows], lsem.at[s]).start()
    lc(tokens, tokg.at[y], lsem.at[13]).start()
    for j in range(4):
        for i in range(4):
            lc(w_up.at[:, up_cols(j, i, y)], wA.at[3 + j, z, x, c, my_rows, pl.ds(i * 128, 128)],
               lsem.at[3 + j]).start()
    lc(w_out, wO.at[z, x, c, y], lsem.at[11]).start()
    for j in range(4):
        lc(w_down.at[:, pl.ds(j * 256, 256)], wD.at[j, z, x, c], lsem.at[7 + j]).start()
    kcopies = []
    for j in range(4):
        kcopies.append(lc(keys_in.at[:, :, :, :, pl.ds(j * 256, 256)], gD.at[j], kn_sem.at[0]))
        kcopies[-1].start()
    kcopy = lc(gD, gD, kn_sem.at[0])

    def keys_of(s):
        return jnp.concatenate([gD[j, s // 4, (s // 2) % 2, s % 2] for j in range(4)], 1)

    hcopy = lc(head_grad, hgrad, kn_sem.at[1])
    hcopy.start()

    barrier = pltpu.get_barrier_semaphore()
    for to in (*zdev, xdev, ydev, cdev):
        pl.semaphore_signal(barrier, inc=1, device_id=to, device_id_type=MESH)
    pl.semaphore_wait(barrier, 6)

    def own_view(t):
        if t < 7:
            return wA.at[t, z, x, c]
        if t < 11:
            return wD.at[t - 7, z, x, c]
        return wO.at[z, x, c, y] if t == 11 else pk.at[z, x, c, y]

    def x_view(t):
        if t < 7:
            return wA.at[t, :, x, c]
        if t < 11:
            return wD.at[t - 7, :, x, c]
        return wO.at[:, x, c, y] if t == 11 else pk.at[:, x, c, y]

    def y_view(t):
        return wO.at[:, :, c, y] if t == 11 else pk.at[:, :, c, y]

    def c_view(t):
        if t < 7:
            return wA.at[t, :, :, c]
        if t < 11:
            return wD.at[t - 7, :, :, c]
        return wO.at[:, :, c] if t == 11 else pk.at[:, :, c]

    def y0_full(t):
        view = wA.at[t, z, x, c, my_rows]
        return rc(view, view, ysend.at[t], yrecv.at[t], ydev)

    def start_y0(t):
        if t < 3:
            rc(w_qkv.at[:, part_cols(t, oy)], wA.at[t, z, x, c, my_rows], ysend.at[t], yrecv.at[t], ydev).start()
        else:
            for i in range(4):
                rc(w_up.at[:, up_cols(t - 3, i, oy)], wA.at[t, z, x, c, my_rows, pl.ds(i * 128, 128)],
                   ysend.at[t], yrecv.at[t], ydev).start()
        pending.append(y0_full(t))

    def local_wait(t):
        if t < 7:
            view = wA.at[t, z, x, c, my_rows]
        else:
            view = own_view(t)
        lc(view, view, lsem.at[t]).wait()

    def start_z(t):
        local_wait(t)
        if t < 7:
            y0_full(t).wait_recv()
        for j in range(3):
            cp = rc(own_view(t), own_view(t), zsend.at[t, j], zrecv.at[t, j], zdev[j])
            cp.start()
            pending.append(cp)

    def start_x(t):
        for j in range(3):
            rc(own_view(t), own_view(t), zsend.at[t, j], zrecv.at[t, j], zdev[j]).wait_recv()
        cp = rc(x_view(t), x_view(t), xsend.at[t], xrecv.at[t], xdev)
        cp.start()
        pending.append(cp)

    def y_copy(t):
        return rc(y_view(t), y_view(t), ysend.at[t - 4], yrecv.at[t - 4], ydev)

    def start_y(t):
        rc(x_view(t), x_view(t), xsend.at[t], xrecv.at[t], xdev).wait_recv()
        cp = y_copy(t)
        cp.start()
        pending.append(cp)

    def c_copy(t):
        return rc(c_view(t), c_view(t), csend.at[t], crecv.at[t], cdev)

    def start_c(t):
        if t < 11:
            rc(x_view(t), x_view(t), xsend.at[t], xrecv.at[t], xdev).wait_recv()
        else:
            y_copy(t).wait_recv()
        cp = c_copy(t)
        cp.start()
        pending.append(cp)

    def ready(t):
        c_copy(t).wait_recv()

    order = [0, 1, 2, 11, 3, 4, 5, 6, 7, 8, 9, 10]

    def tick(n):
        if n < 12:
            start_x(order[n])
        if n + 2 < 12:
            start_z(order[n + 2])
        if 1 <= n <= 12:
            t = order[n - 1]
            if t == 11:
                start_y(t)
            else:
                start_c(t)
        if n == 5:
            start_c(11)

    start_y0(0)
    start_y0(1)
    start_y0(2)
    start_z(12)
    start_z(0)
    tok_copy = rc(tokens, tokg.at[y], msend.at[0], mrecv.at[0], ydev)
    tok_copy.start()
    pending.append(tok_copy)
    for t in range(3, 7):
        start_y0(t)
    start_x(12)
    start_z(1)
    start_y(12)

    first_end = seq[0, 0]
    second_end = first_end + seq[0, 1]

    def segment(pos):
        return (pos >= first_end).astype(jnp.int32) + (pos >= second_end).astype(jnp.int32)

    def mask_rows(i, _):
        rows = pl.ds(pl.multiple_of(i * 128, 128), 128)
        qpos = i * 128 + lax.broadcasted_iota(jnp.int32, (128, 512), 0)
        kpos = lax.broadcasted_iota(jnp.int32, (128, 512), 1)
        good = (segment(qpos) == segment(kpos)) & (kpos <= qpos)
        mask[rows, :] = jnp.where(good, 0.0, NEG)
        return 0

    lax.fori_loop(0, 4, mask_rows, 0)
    start_c(12)
    tick(0)
    c_copy(12).wait_recv()

    for g in range(8):
        total = None
        for i in range(4):
            piece = pk[g // 2, g % 2, i // 2, i % 2].astype(F32)
            total = piece if total is None else total + piece
        prm[:, g * 128 : (g + 1) * 128] = total
    for d in range(16):
        piece = pk[d // 4, (d // 2) % 2, d % 2, y].astype(F32)
        ubias[0:1, d * 128 : (d + 1) * 128] = piece[10:11, :]

    def row(r):
        return prm[r : r + 1, :]

    lc(tokens, tokg.at[y], lsem.at[13]).wait()
    rc(tokens, tokg.at[y], msend.at[0], mrecv.at[0], ydev).wait_recv()

    def norm_in(i, _):
        half = i // 4
        rows = pl.ds(pl.multiple_of((i % 4) * 64, 64), 64)
        unit, _inv = unit_of(tokg[half, rows, :].astype(F32))
        ni[half, rows, :] = (unit * row(0) + row(3)).astype(BF)
        return 0

    lax.fori_loop(0, 8, norm_in, 0)
    tick(1)

    head_cols = pl.ds(pl.multiple_of(y * 512, 512), 512)
    tick(2)
    for s in range(3):
        ready(s)
        bias = prm[6:7, head_cols] if s == 0 else (prm[7:8, head_cols] if s == 2 else None)
        for half in range(2):
            value = dot(ni[half], wA[s].reshape(1024, 512))
            if bias is not None:
                value = value + bias
            qkv[s, half] = value.astype(BF)
        tick(3 + s)

    lane = lax.broadcasted_iota(jnp.int32, (1, 128), 1)
    in_head = [lane < 64, lane >= 64]

    def probs_of(qe, k2, half):
        nk = 256 * (half + 1)
        s = dot(qe, k2[:nk], 1, 1) * 0.125 + mask[half * 256 : half * 256 + 256, :nk]
        ex = jnp.exp(s - jnp.max(s, -1, keepdims=True))
        return ex * (1.0 / jnp.sum(ex, -1, keepdims=True))

    def attend(p, _):
        cols = pl.ds(pl.multiple_of(p * 128, 128), 128)
        q2 = qkv[0, :, :, cols]
        k2 = qkv[1, :, :, cols].reshape(512, 128)
        v2 = qkv[2, :, :, cols].reshape(512, 128)
        for half in range(2):
            nk = 256 * (half + 1)
            outs = []
            for e in range(2):
                qe = jnp.where(in_head[e], q2[half], jnp.zeros_like(q2[half]))
                outs.append(dot(probs_of(qe, k2, half).astype(BF), v2[:nk]))
            att_h[half, :, cols] = jnp.where(in_head[0], outs[0], outs[1]).astype(BF)
        return 0

    lax.fori_loop(0, 2, attend, 0)
    tick(6)
    lax.fori_loop(2, 4, attend, 0)
    own_att = lc(att_h.at[y], att_f.at[:, head_cols], lsem.at[14])
    own_att.start()
    att_copy = rc(att_h.at[oy], att_f.at[:, head_cols], msend.at[1], mrecv.at[1], ydev)
    att_copy.start()
    pending.append(att_copy)
    tick(7)

    kcopy.wait()
    hcopy.wait()
    eye = lax.broadcasted_iota(jnp.int32, (128, 128), 0) == lax.broadcasted_iota(jnp.int32, (128, 128), 1)

    def tables(s, _):
        rows = pl.ds(pl.multiple_of(s * 16, 16), 16)
        kk = keys_of(s)
        ksq[rows, :] = jnp.broadcast_to(col_sum(jnp.where(eye, dot(kk, kk, 1, 1), 0.0)), (16, 128))
        match[rows, :] = jnp.where(ids[pl.ds(s, 1), :] == targets[rows, :], 1.0, 0.0)
        return 0

    lax.fori_loop(0, 16, tables, 0)

    own_att.wait()
    att_copy.wait_recv()
    ready(11)
    h1[...] = dot(att_f[...], wO[...].reshape(1024, 1024)) + row(8)

    def norm_mid(i, _):
        rows = pl.ds(pl.multiple_of(i * 64, 64), 64)
        value = h1[rows, :] + tokg[y, rows, :].astype(F32)
        h1[rows, :] = value
        unit, _inv = unit_of(value)
        nmg[y, rows, :] = (unit * row(1) + row(4)).astype(BF)
        return 0

    lax.fori_loop(0, 4, norm_mid, 0)
    nm_copy = rc(nmg.at[y], nmg.at[y], msend.at[2], mrecv.at[2], ydev)
    nm_copy.start()
    pending.append(nm_copy)
    tick(8)
    nm_copy.wait_recv()

    for j in range(4):
        ready(3 + j)
        cols = slice(j * 512, (j + 1) * 512)
        for half in range(2):
            u = dot(nmg[half], wA[3 + j].reshape(1024, 512)) + ubias[0:1, cols]
            value, dvalue = gelu_pair(u)
            gelu[half, :, cols] = value.astype(BF)
            slope[half, :, cols] = dvalue.astype(BF)
        tick(9 + j)
    part_copies = []
    for j in range(4):
        ready(7 + j)
        cols = slice(j * 256, (j + 1) * 256)
        weight = wD[j].reshape(2048, 256)
        sendb[0, :, cols] = dot(gelu[oy], weight).astype(BF)
        cp = rc(sendb.at[0, :, pl.ds(j * 256, 256)], prec.at[:, pl.ds(j * 256, 256)], msend.at[3 + j], mrecv.at[3 + j], ydev)
        cp.start()
        pending.append(cp)
        part_copies.append(cp)
        st[:, cols] = dot(gelu[y], weight) + (h1[:, cols] + prm[9:10, cols])
    for cp in part_copies:
        cp.wait_recv()

    dsg_copies = []
    dg = jnp.zeros((1, 1024), F32)
    dsh = jnp.zeros((1, 1024), F32)
    db = jnp.zeros((1, 1024), F32)
    knn_scale = 0.5 / 32.0
    for b in range(4):
        rows = slice(b * 64, b * 64 + 64)
        value = st[rows, :] + prec[rows, :].astype(F32)
        lowb[rows, :] = value.astype(BF)
        unit, inv = unit_of(value)
        query = (unit * row(2) + row(5)).astype(BF)
        raw = jnp.concatenate(
            [dot(query[i * 16 : i * 16 + 16], keys_of(b * 4 + i), 1, 1) for i in range(4)], 0
        )
        logits = (2.0 * raw - ksq[rows, :]) * knn_scale
        slot = lax.broadcasted_iota(jnp.int32, (64, 128), 1)
        logits = jnp.where(slot < counts[rows, :], logits, NEG)
        ex = jnp.exp(logits - jnp.max(logits, -1, keepdims=True))
        weights = ex / jnp.sum(ex, -1, keepdims=True)
        same = match[rows, :]
        knn_prob = jnp.sum(same * weights, -1, keepdims=True)
        mixture = MIX_WEIGHT * knn_prob + (1.0 - MIX_WEIGHT) * p_lm[rows, :]
        lossb[rows, :] = -jnp.log(mixture)
        dlog = (-(MIX_WEIGHT / mixture) * weights * (same - knn_prob)).astype(BF)
        kgrad = jnp.concatenate(
            [dot(dlog[i * 16 : i * 16 + 16], keys_of(b * 4 + i)) for i in range(4)], 0
        )
        dquery = hgrad[rows, :].astype(F32) + kgrad * (2.0 * knn_scale)
        dg = dg + col_sum(dquery * unit)
        dsh = dsh + col_sum(dquery)
        dvalue = ln_back(dquery, unit, inv, row(2))
        st[rows, :] = dvalue
        low = dvalue.astype(BF)
        db = db + col_sum(low.astype(F32))
        dsg[y, rows, :] = low
        view = dsg.at[y, pl.ds(b * 64, 64)]
        cp = rc(view, view, msend.at[7 + b], mrecv.at[7 + b], ydev)
        cp.start()
        pending.append(cp)
        dsg_copies.append(cp)
    pg[...] = jnp.zeros_like(pg)
    pg[2:3, :] = dg
    pg[5:6, :] = dsh
    pg[9:10, :] = db
    out_state = lc(lowb, state_out, osem.at[0])
    out_state.start()
    out_loss = lc(lossb, loss_out, osem.at[1])
    out_loss.start()
    finals = [out_loss]
    for cp in dsg_copies:
        cp.wait_recv()

    slot_of = {3: 0, 4: 1, 5: 2, 6: 3, 0: 0, 1: 1, 2: 2}

    def g_ref(t):
        if t < 7:
            return gA.at[slot_of[t]]
        if t < 11:
            return gD.at[t - 7]
        return gO if t == 11 else gP

    def recv_refs(t):
        if t < 7:
            return dRA.at[t], xRA.at[t], zRA.at[t]
        if t < 11:
            return dRD.at[t - 7], xRD.at[t - 7], zRD.at[t - 7]
        return (dRO, xRO, zRO) if t == 11 else (dRP, xRP, zRP)

    def rs_c(t):
        return rc(g_ref(t).at[:, :, oc], recv_refs(t)[0], rcs.at[t], rcr.at[t], cdev)

    def rs_y(t):
        dest = yRO if t == 11 else yRP
        return rc(g_ref(t).at[:, :, c, oy], dest, rys.at[t], ryr.at[t], ydev)

    def rs_x(t):
        g = g_ref(t)
        src = g.at[:, ox, c] if t < 11 else g.at[:, ox, c, y]
        return rc(src, recv_refs(t)[1], rxs.at[t], rxr.at[t], xdev)

    def rs_z(t, j):
        g = g_ref(t)
        src = g.at[zs[j], x, c] if t < 11 else g.at[zs[j], x, c, y]
        return rc(src, recv_refs(t)[2].at[j], rzs.at[t, j], rzr.at[t, j], zdev[j])

    def rs_start(t):
        rs_c(t).start()

    def rs_after_c(t):
        rs_c(t).wait_recv()
        g, r = g_ref(t), recv_refs(t)[0]
        for i in range(4):
            g[i, :, c] = (g[i, :, c].astype(F32) + r[i].astype(F32)).astype(g.dtype)
        (rs_y(t) if t >= 11 else rs_x(t)).start()

    def rs_after_y(t):
        rs_y(t).wait_recv()
        g, r = g_ref(t), (yRO if t == 11 else yRP)
        for i in range(4):
            g[i, :, c, y] = (g[i, :, c, y].astype(F32) + r[i].astype(F32)).astype(g.dtype)
        rs_x(t).start()

    def rs_after_x(t):
        rs_x(t).wait_recv()
        g, r = g_ref(t), recv_refs(t)[1]
        for i in range(4):
            if t < 11:
                g[i, x, c] = (g[i, x, c].astype(F32) + r[i].astype(F32)).astype(g.dtype)
            else:
                g[i, x, c, y] = (g[i, x, c, y].astype(F32) + r[i].astype(F32)).astype(g.dtype)
        for j in range(3):
            rs_z(t, j).start()

    def rs_sends_done(t):
        rs_c(t).wait_send()
        if t >= 11:
            rs_y(t).wait_send()
        rs_x(t).wait_send()
        for j in range(3):
            rs_z(t, j).wait_send()

    def out_cols(t, yy):
        if t < 3:
            return [(gqkv_out, part_cols(t, yy), slice(0, 512))]
        return [(gup_out, up_cols(t - 3, i, yy), slice(i * 128, (i + 1) * 128)) for i in range(4)]

    def fin_view(t, yy):
        return finA.at[t, yy]

    def rs_finish(t):
        for j in range(3):
            rs_z(t, j).wait_recv()
        g, r = g_ref(t), recv_refs(t)[2]
        own = g[z, x, c] if t < 11 else g[z, x, c, y]
        total = own.astype(F32) + r[0].astype(F32) + r[1].astype(F32) + r[2].astype(F32)
        rs_sends_done(t)
        if t < 7:
            finA[t, 0] = total[:32]
            finA[t, 1] = total[32:]
            for ref, cols, inner in out_cols(t, y):
                lc(finA.at[t, y, :, pl.ds(inner.start, inner.stop - inner.start)], ref.at[:, cols], rfl.at[t]).start()
                rc(finA.at[t, oy, :, pl.ds(inner.start, inner.stop - inner.start)], ref.at[:, cols],
                   rys.at[t], ryr.at[t], ydev).start()
            full = finA.at[t, y]
            finals.append(lc(full, full, rfl.at[t]))
            both = rc(full, full, rys.at[t], ryr.at[t], ydev)
            pending.append(both)
            late_recv.append(both)
        elif t < 11:
            finD[t - 7] = total
            cp = lc(finD.at[t - 7], gdown_out.at[:, pl.ds((t - 7) * 256, 256)], rfl.at[t])
            cp.start()
            finals.append(cp)
        elif t == 11:
            finO[...] = total
            cp = lc(finO, gout_out, rfl.at[t])
            cp.start()
            finals.append(cp)
        else:
            return total

    late_recv = []

    def make_down(j):
        ds_cols = dsg[:, :, j * 256 : (j + 1) * 256].reshape(512, 256)
        for i in range(4):
            part = gelu[:, :, i * 512 : (i + 1) * 512].reshape(512, 512)
            gD[j, i] = dot(part, ds_cols, 0, 0).astype(BF).reshape(2, 2, 128, 256)
        rs_start(7 + j)

    def make_a(t, right):
        left = nmg if t >= 3 else ni
        for i in range(4):
            part = left[:, :, i * 256 : (i + 1) * 256].reshape(512, 256)
            gA[slot_of[t], i] = dot(part, right, 0, 0).astype(BF).reshape(2, 2, 64, 512)
        rs_start(t)

    def make_dpre(i):
        cols = slice(i * 512, (i + 1) * 512)
        acc = None
        for j in range(4):
            part = dot(
                dsg[:, :, j * 256 : (j + 1) * 256].reshape(512, 256), wD[j, i].reshape(512, 256), 1, 1
            )
            acc = part if acc is None else acc + part
        low = (acc * slope[:, :, cols].reshape(512, 512).astype(F32)).astype(BF)
        slope[:, :, cols] = low.reshape(2, 256, 512)
        dub[0:1, cols] = col_sum(low.astype(F32))

    def up_grad(j):
        make_a(3 + j, slope[:, :, j * 512 : (j + 1) * 512].reshape(512, 512))

    make_down(0)
    make_down(1)
    make_dpre(0)
    rs_after_c(7)
    make_dpre(1)
    rs_after_c(8)
    make_dpre(2)
    make_dpre(3)

    def dnorm_mid(half, n):
        acc = None
        for j in range(4):
            part = dot(slope[half, :, j * 512 : (j + 1) * 512], wA[3 + j, n].reshape(256, 512), 1, 1)
            acc = part if acc is None else acc + part
        return acc

    def dnorm_in(half, n):
        acc = None
        for s in range(3):
            part = dot(dqkv[s, half], wA[s, n].reshape(256, 512), 1, 1)
            acc = part if acc is None else acc + part
        return acc

    def share(fn, slot, recv, sem0):
        copies = []
        for n in range(4):
            cols = pl.ds(n * 256, 256)
            sendb[slot, :, n * 256 : (n + 1) * 256] = fn(oy, n).astype(BF)
            cp = rc(sendb.at[slot, :, cols], recv.at[:, cols], msend.at[sem0 + n], mrecv.at[sem0 + n], ydev)
            cp.start()
            pending.append(cp)
            copies.append(cp)
        for n in range(4):
            dnm[:, n * 256 : (n + 1) * 256] = fn(y, n)
        return copies

    dn_copies = share(dnorm_mid, 1, dnr, 11)
    make_down(2)
    make_down(3)
    rs_after_c(9)
    rs_after_c(10)
    up_grad(0)
    up_grad(1)
    rs_after_c(3)
    rs_after_x(7)
    for cp in dn_copies:
        cp.wait_recv()

    out_state.wait()
    zero_row = jnp.zeros((1, 1024), F32)

    def back_mid(i, carry):
        a, b, d = carry
        rows = pl.ds(pl.multiple_of(i * 64, 64), 64)
        dy = dnm[rows, :] + dnr[rows, :].astype(F32)
        unit, inv = unit_of(h1[rows, :])
        total = st[rows, :] + ln_back(dy, unit, inv, row(1))
        st[rows, :] = total
        low = total.astype(BF)
        lowb[rows, :] = low
        return a + col_sum(dy * unit), b + col_sum(dy), d + col_sum(low.astype(F32))

    dg, dsh, db = lax.fori_loop(0, 4, back_mid, (zero_row, zero_row, zero_row))
    pg[1:2, :] = dg
    pg[4:5, :] = dsh
    pg[8:9, :] = db

    def datt(yy):
        weight = wO[pl.ds(2 * yy, 2)].reshape(512, 1024)
        return dot(lowb[...], weight, 1, 1).astype(BF)

    sendb[2, :, :512] = datt(oy)
    da_copy = rc(sendb.at[2, :, pl.ds(0, 512)], dattg.at[y], msend.at[15], mrecv.at[15], ydev)
    da_copy.start()
    pending.append(da_copy)
    dattg[y] = datt(y)
    up_grad(2)
    up_grad(3)
    rs_after_c(4)
    for i in range(4):
        part = att_f[:, i * 256 : (i + 1) * 256]
        gO[i] = dot(part, lowb[...], 0, 0).astype(BF).reshape(2, 2, 2, 32, 1024)
    rs_start(11)
    rs_after_x(8)
    rs_after_c(5)
    rs_after_c(6)
    rs_after_x(9)
    rs_finish(7)
    rs_after_c(11)
    da_copy.wait_recv()

    def attend_back(p, _):
        cols = pl.ds(pl.multiple_of(p * 128, 128), 128)
        q2 = qkv[0, :, :, cols]
        k2 = qkv[1, :, :, cols].reshape(512, 128)
        v2 = qkv[2, :, :, cols].reshape(512, 128)
        do2 = dattg[:, :, cols]
        zero = jnp.zeros((512, 128), BF)
        dks = [None, None]
        dvs = [None, None]
        for half in range(2):
            nk = 256 * (half + 1)
            dq = None
            for e in range(2):
                qe = jnp.where(in_head[e], q2[half], zero[:256])
                doe = jnp.where(in_head[e], do2[half], zero[:256])
                ke = jnp.where(in_head[e], k2[:nk], zero[:nk])
                probs = probs_of(qe, k2, half)
                dprob = dot(doe, v2[:nk], 1, 1)
                delta = jnp.sum(probs * dprob, -1, keepdims=True)
                ds = (probs * (dprob - delta)).astype(BF)
                part = dot(ds, ke)
                dq = part if dq is None else dq + part
                dk = dot(ds, qe, 0, 0)
                dv = dot(probs.astype(BF), doe, 0, 0)
                for kb in range(half + 1):
                    rows = slice(kb * 256, kb * 256 + 256)
                    dks[kb] = dk[rows] if dks[kb] is None else dks[kb] + dk[rows]
                    dvs[kb] = dv[rows] if dvs[kb] is None else dvs[kb] + dv[rows]
            dqkv[0, half, :, cols] = (dq * 0.125).astype(BF)
        for kb in range(2):
            dqkv[1, kb, :, cols] = (dks[kb] * 0.125).astype(BF)
            dqkv[2, kb, :, cols] = dvs[kb].astype(BF)
        return 0

    lax.fori_loop(0, 2, attend_back, 0)
    rs_after_x(10)
    rs_after_y(11)
    lax.fori_loop(2, 4, attend_back, 0)
    rs_finish(8)
    rs_after_x(3)

    dn2_copies = share(dnorm_in, 3, dnr2, 16)
    pg[6:7, head_cols] = col_sum(dqkv[0].reshape(512, 512).astype(F32))
    pg[7:8, head_cols] = col_sum(dqkv[2].reshape(512, 512).astype(F32))
    rs_finish(9)
    rs_after_x(4)
    rs_finish(3)
    make_a(0, dqkv[0].reshape(512, 512))
    rs_finish(10)
    rs_after_x(5)
    rs_finish(4)
    rs_after_c(0)
    make_a(1, dqkv[1].reshape(512, 512))
    for cp in dn2_copies:
        cp.wait_recv()

    def back_in(i, carry):
        a, b = carry
        rows = pl.ds(pl.multiple_of(i * 64, 64), 64)
        dy = dnm[rows, :] + dnr2[rows, :].astype(F32)
        unit, inv = unit_of(tokg[y, rows, :].astype(F32))
        hgrad[rows, :] = (st[rows, :] + ln_back(dy, unit, inv, row(0))).astype(BF)
        return a + col_sum(dy * unit), b + col_sum(dy)

    dg, dsh = lax.fori_loop(0, 4, back_in, (zero_row, zero_row))
    pg[0:1, :] = dg
    pg[3:4, :] = dsh
    out_gin = lc(hgrad, gin_out, osem.at[2])
    out_gin.start()
    finals.append(out_gin)
    row_id = lax.broadcasted_iota(jnp.int32, (16, 128), 0)
    for d in range(32):
        piece = pg[:, (d // 4) * 128 : (d // 4) * 128 + 128]
        mine = jnp.where(y == d % 2, dub[0:1, (d // 2) * 128 : (d // 2) * 128 + 128], 0.0)
        gP[d // 8, (d // 4) % 2, (d // 2) % 2, d % 2] = jnp.where(row_id == 10, mine, piece)
    rs_start(12)
    rs_after_c(1)
    rs_after_x(6)
    rs_finish(5)
    make_a(2, dqkv[2].reshape(512, 512))
    rs_after_c(12)
    rs_after_x(11)
    rs_after_c(2)
    rs_after_y(12)
    rs_finish(6)
    rs_after_x(0)
    rs_after_x(12)
    rs_finish(11)
    rs_after_x(1)
    rs_finish(0)
    packet_sum = rs_finish(12)
    pg[:, 0:128] = packet_sum
    out_pk = lc(pg.at[:, pl.ds(0, 128)], gpk_out, osem.at[3])
    out_pk.start()
    finals.append(out_pk)
    rs_after_x(2)
    rs_finish(1)
    rs_finish(2)
    for cp in late_recv:
        cp.wait_recv()
    for cp in pending:
        cp.wait_send()
    for cp in finals:
        cp.wait()


SCRATCH = dict(
    wA=((7, 4, 2, 2, 64, 512), BF), wD=((4, 4, 2, 2, 128, 256), BF), wO=((4, 2, 2, 2, 32, 1024), BF),
    pk=((4, 2, 2, 2, 16, 128), BF), prm=((16, 1024), F32), ubias=((8, 2048), F32),
    tokg=((2, 256, 1024), BF), ni=((2, 256, 1024), BF), qkv=((3, 2, 256, 512), BF), mask=((512, 512), F32),
    att_h=((2, 256, 512), BF), att_f=((256, 1024), BF), h1=((256, 1024), F32), nmg=((2, 256, 1024), BF),
    gelu=((2, 256, 2048), BF), slope=((2, 256, 2048), BF), st=((256, 1024), F32), prec=((256, 1024), BF),
    hgrad=((256, 1024), BF), ksq=((256, 128), F32), match=((256, 128), F32), dsg=((2, 256, 1024), BF),
    dnm=((256, 1024), F32), dnr=((256, 1024), BF), dattg=((2, 256, 512), BF), dqkv=((3, 2, 256, 512), BF),
    dnr2=((256, 1024), BF), sendb=((4, 256, 1024), BF), lowb=((256, 1024), BF),
    gA=((4, 4, 2, 2, 64, 512), BF), gD=((4, 4, 2, 2, 128, 256), BF), gO=((4, 2, 2, 2, 32, 1024), BF),
    gP=((4, 2, 2, 2, 16, 128), F32),
    dRA=((7, 4, 2, 64, 512), BF), xRA=((7, 4, 64, 512), BF), zRA=((7, 3, 64, 512), BF),
    dRD=((4, 4, 2, 128, 256), BF), xRD=((4, 4, 128, 256), BF), zRD=((4, 3, 128, 256), BF),
    dRO=((4, 2, 2, 32, 1024), BF), yRO=((4, 2, 32, 1024), BF), xRO=((4, 32, 1024), BF), zRO=((3, 32, 1024), BF),
    dRP=((4, 2, 2, 16, 128), F32), yRP=((4, 2, 16, 128), F32), xRP=((4, 16, 128), F32), zRP=((3, 16, 128), F32),
    finA=((7, 2, 32, 512), F32), finD=((4, 128, 256), F32), finO=((32, 1024), F32),
    pg=((16, 1024), F32), dub=((8, 2048), F32), lossb=((256, 1), F32),
)
SEMS = dict(
    lsem=(15,), ysend=(9,), yrecv=(9,), zsend=(13, 3), zrecv=(13, 3), xsend=(13,), xrecv=(13,),
    csend=(13,), crecv=(13,), osem=(4,), msend=(20,), mrecv=(20,), rcs=(13,), rcr=(13,), rxs=(13,),
    rxr=(13,), rzs=(13, 3), rzr=(13, 3), rys=(13,), ryr=(13,), rfl=(13,), kn_sem=(2,),
)


def on_device_fused(
    tokens, head_grad, w_qkv, w_out, w_up, w_down, gains, shifts, biases, up_bias, seq_lengths,
    neigh_keys, neigh_ids, neigh_counts, targets, p_lm,
):
    quarter = (2 * lax.axis_index("dp") + lax.axis_index("fsdp")) % 4
    small = jnp.tile(jnp.concatenate([gains, shifts, biases], 0), (1, 4))
    lane = lax.broadcasted_iota(jnp.int32, (10, 128), 1)
    small = jnp.where(lane // 32 == quarter, small, jnp.zeros_like(small))
    packet = jnp.concatenate([small, up_bias[None, :], jnp.zeros((5, 128), BF)], 0)
    counts_col = jnp.repeat(neigh_counts, 16)[:, None]
    keys = neigh_keys.reshape(4, 2, 2, 128, 1024)
    anywhere = pl.BlockSpec(memory_space=pl.ANY)
    vmem = pl.BlockSpec(memory_space=pltpu.VMEM)
    smem = pl.BlockSpec(memory_space=pltpu.SMEM)
    outs = [
        jax.ShapeDtypeStruct((256, 1024), BF),
        jax.ShapeDtypeStruct((256, 1), F32),
        jax.ShapeDtypeStruct((256, 1024), BF),
        jax.ShapeDtypeStruct((32, 3072), F32),
        jax.ShapeDtypeStruct((32, 1024), F32),
        jax.ShapeDtypeStruct((32, 4096), F32),
        jax.ShapeDtypeStruct((128, 1024), F32),
        jax.ShapeDtypeStruct((16, 128), F32),
    ]
    res = pl.pallas_call(
        block_kernel,
        out_shape=outs,
        in_specs=[anywhere] * 7 + [smem, anywhere, vmem, vmem, vmem, vmem],
        out_specs=[anywhere] * 8,
        scratch_shapes=[pltpu.VMEM(*SCRATCH[k]) for k in SCRATCH]
        + [pltpu.SemaphoreType.DMA(SEMS[k]) for k in SEMS],
        compiler_params=pltpu.CompilerParams(
            collective_id=0, has_side_effects=True, vmem_limit_bytes=VMEM_LIMIT
        ),
        name="block",
    )(
        tokens, head_grad, w_qkv, w_out, w_up, w_down, packet, seq_lengths, keys, neigh_ids,
        counts_col, targets[:, None], p_lm[:, None],
    )
    state, loss, gin, gqkv, gout, gup, gdown, packet_sum = res
    mine = lax.dynamic_slice(packet_sum, (0, quarter * 32), (10, 32))
    return (
        state, loss.reshape(256), gin, gqkv, gout, gup, gdown,
        mine[0:3], mine[3:6], mine[6:10], packet_sum[10],
    )


def solution(mesh):
    in_specs = (
        P(("dp", "fsdp"), None),
        P(("dp", "fsdp"), None),
        P(("dp", "fsdp"), None),
        P(("dp", "fsdp"), None),
        P(("dp", "fsdp"), None),
        P(("dp", "fsdp"), None),
        P(None, ("dp", "fsdp")),
        P(None, ("dp", "fsdp")),
        P(None, ("dp", "fsdp")),
        P(("dp", "fsdp")),
        P("dp", None),
        P(("dp", "fsdp"), None, None),
        P(("dp", "fsdp"), None),
        P(("dp", "fsdp")),
        P(("dp", "fsdp")),
        P(("dp", "fsdp")),
    )
    out_specs = (
        P(("dp", "fsdp"), None),
        P(("dp", "fsdp")),
        P(("dp", "fsdp"), None),
        P(("dp", "fsdp"), None),
        P(("dp", "fsdp"), None),
        P(("dp", "fsdp"), None),
        P(("dp", "fsdp"), None),
        P(None, ("dp", "fsdp")),
        P(None, ("dp", "fsdp")),
        P(None, ("dp", "fsdp")),
        P(("dp", "fsdp")),
    )
    fused = mesh.shape["dp"] == 16 and mesh.shape["fsdp"] == 2
    return jax.shard_map(
        on_device_fused if fused else on_device, mesh=mesh, in_specs=in_specs, out_specs=out_specs, check_vma=False
    )
```

```python
import functools
import math

import jax
import jax.numpy as jnp
from jax import lax
from jax.experimental import pallas as pl
from jax.experimental.pallas import tpu as pltpu
from jax.sharding import PartitionSpec as P

HEADS = 16


EPSILON = 1e-05
MIX_WEIGHT = 0.25


def norm_rows(values, gain_row, shift_row):
    center = values - jnp.mean(values, -1, keepdims=True)
    inverse = lax.rsqrt(jnp.mean(center * center, -1, keepdims=True) + EPSILON)
    unit_rows = center * inverse
    return (unit_rows * gain_row + shift_row, unit_rows, inverse)


def norm_back(grad_rows, unit_rows, inverse, gain_row):
    scaled = grad_rows * gain_row
    first_mean = jnp.mean(scaled, -1, keepdims=True)
    second_mean = jnp.mean(scaled * unit_rows, -1, keepdims=True)
    grad_values = inverse * (scaled - first_mean - unit_rows * second_mean)
    return (grad_values, jnp.sum(grad_rows * unit_rows, 0), jnp.sum(grad_rows, 0))


def contract_rows(left, right):
    return lax.dot_general(
        left, right, (((0,), (0,)), ((), ())), preferred_element_type=jnp.float32
    )


def times_transposed(left, right):
    return lax.dot_general(
        left, right, (((1,), (1,)), ((), ())), preferred_element_type=jnp.float32
    )


def segment_of(lengths, positions):
    first_end = lengths[0]
    second_end = lengths[0] + lengths[1]
    return (positions >= first_end).astype(jnp.int32) + (positions >= second_end).astype(jnp.int32)


def on_device(
    tokens,
    head_grad,
    w_qkv,
    w_out,
    w_up,
    w_down,
    gains,
    shifts,
    biases,
    up_bias,
    seq_lengths,
    neigh_keys,
    neigh_ids,
    neigh_counts,
    targets,
    p_lm,
):
    gathered = (
        lax.all_gather(w_qkv, ("dp", "fsdp"), axis=0, tiled=True),
        lax.all_gather(w_out, ("dp", "fsdp"), axis=0, tiled=True),
        lax.all_gather(w_up, ("dp", "fsdp"), axis=0, tiled=True),
        lax.all_gather(w_down, ("dp", "fsdp"), axis=0, tiled=True),
        lax.all_gather(gains, ("dp", "fsdp"), axis=1, tiled=True),
        lax.all_gather(shifts, ("dp", "fsdp"), axis=1, tiled=True),
        lax.all_gather(biases, ("dp", "fsdp"), axis=1, tiled=True),
        lax.all_gather(up_bias, ("dp", "fsdp"), axis=0, tiled=True),
    )
    row_count, feature_width = tokens.shape
    head_count = HEADS
    head_depth = feature_width // head_count
    score_scale = 1.0 / math.sqrt(head_depth)
    gain_rows = gathered[4].astype(jnp.float32)
    shift_rows = gathered[5].astype(jnp.float32)
    bias_rows = gathered[6].astype(jnp.float32)
    tokens_f32 = tokens.astype(jnp.float32)
    normed_in, unit_in, inverse_in = norm_rows(tokens_f32, gain_rows[0], shift_rows[0])
    normed_in_low = normed_in.astype(jnp.bfloat16)
    qkv_bias = jnp.concatenate([bias_rows[0], jnp.zeros_like(bias_rows[0]), bias_rows[1]])
    qkv = (
        jnp.dot(normed_in_low, gathered[0], preferred_element_type=jnp.float32) + qkv_bias
    ).astype(jnp.bfloat16)
    query_heads = qkv[:, :feature_width].reshape(row_count, head_count, head_depth)
    kv_local = qkv[:, feature_width:]
    kv_group = lax.all_gather(kv_local, "fsdp", axis=0, tiled=True)
    group_size = kv_group.shape[0]
    part_count = lax.axis_size("fsdp")
    block_rows = row_count * min(part_count, max(1, 512 // row_count))
    block_count = group_size // block_rows
    first_row = lax.axis_index("fsdp") * row_count
    last_row = first_row + row_count - 1
    lengths = seq_lengths[0]
    query_pos = first_row + jnp.arange(row_count, dtype=jnp.int32)
    query_seg = segment_of(lengths, query_pos)

    def scores_of(source, block_start):
        key_piece = lax.dynamic_slice_in_dim(source, block_start, block_rows, 0)
        key_heads = key_piece[:, :feature_width].reshape(block_rows, head_count, head_depth)
        value_heads = key_piece[:, feature_width:].reshape(block_rows, head_count, head_depth)
        key_pos = block_start + jnp.arange(block_rows, dtype=jnp.int32)
        allowed = (segment_of(lengths, key_pos)[None, :] == query_seg[:, None]) & (
            key_pos[None, :] <= query_pos[:, None]
        )
        raw_scores = (
            jnp.einsum("qhe,khe->hqk", query_heads, key_heads, preferred_element_type=jnp.float32)
            * score_scale
        )
        return (jnp.where(allowed[None], raw_scores, -jnp.inf), key_heads, value_heads)

    def keep_same(kept_value):
        return kept_value

    def stats_step(block_index, stats):
        block_start = block_index * block_rows

        def stats_block_work(pair):
            row_top, row_total = pair
            masked, key_heads, value_heads = scores_of(kv_group, block_start)
            new_top = jnp.maximum(row_top, jnp.max(masked, -1))
            safe_top = jnp.where(new_top > -jnp.inf, new_top, 0.0)
            row_total = row_total * jnp.exp(row_top - safe_top) + jnp.sum(
                jnp.exp(masked - safe_top[..., None]), -1
            )
            return (new_top, row_total)

        return lax.cond(block_start <= last_row, stats_block_work, keep_same, stats)

    start_stats = (
        jnp.full((head_count, row_count), -jnp.inf, jnp.float32),
        jnp.zeros((head_count, row_count), jnp.float32),
    )
    row_top, row_total = lax.fori_loop(0, block_count, stats_step, start_stats)
    log_total = row_top + jnp.log(row_total)

    def value_step(block_index, value_acc):
        block_start = block_index * block_rows

        def value_block_work(value_sum):
            masked, key_heads, value_heads = scores_of(kv_group, block_start)
            prob_low = jnp.exp(masked - log_total[..., None]).astype(jnp.bfloat16)
            return value_sum + jnp.einsum(
                "hqk,khe->qhe", prob_low, value_heads, preferred_element_type=jnp.float32
            )

        return lax.cond(block_start <= last_row, value_block_work, keep_same, value_acc)

    attended = lax.fori_loop(
        0, block_count, value_step, jnp.zeros((row_count, head_count, head_depth), jnp.float32)
    )
    attended = attended.reshape(row_count, feature_width)
    attended_low = attended.astype(jnp.bfloat16)
    hidden_one = tokens_f32 + (
        jnp.dot(attended_low, gathered[1], preferred_element_type=jnp.float32) + bias_rows[2]
    )
    normed_mid, unit_mid, inverse_mid = norm_rows(hidden_one, gain_rows[1], shift_rows[1])
    normed_mid_low = normed_mid.astype(jnp.bfloat16)
    pre_act = jnp.dot(normed_mid_low, gathered[2], preferred_element_type=jnp.float32) + gathered[
        7
    ].astype(jnp.float32)
    gelu_low = jax.nn.gelu(pre_act).astype(jnp.bfloat16)
    state_f32 = hidden_one + (
        jnp.dot(gelu_low, gathered[3], preferred_element_type=jnp.float32) + bias_rows[3]
    )
    query, unit_out, inverse_out = norm_rows(state_f32, gain_rows[2], shift_rows[2])
    span_count = neigh_keys.shape[0]
    slot_count = neigh_keys.shape[1]
    knn_scale = 0.5 / math.sqrt(feature_width)
    query_low = query.astype(jnp.bfloat16).reshape(span_count, -1, feature_width)
    key_square = jnp.einsum(
        "snd,snd->sn", neigh_keys, neigh_keys, preferred_element_type=jnp.float32
    )
    raw_logits = jnp.einsum(
        "sqd,snd->sqn", query_low, neigh_keys, preferred_element_type=jnp.float32
    )
    logits = (2.0 * raw_logits - key_square[:, None, :]) * knn_scale
    slot_valid = jnp.arange(slot_count, dtype=jnp.int32)[None, :] < neigh_counts[:, None]
    masked_logits = jnp.where(slot_valid[:, None, :], logits, -jnp.inf)
    exp_values = jnp.exp(masked_logits - jnp.max(masked_logits, -1, keepdims=True))
    weights = exp_values / jnp.sum(exp_values, -1, keepdims=True)
    id_match = neigh_ids[:, None, :] == targets.reshape(span_count, -1)[:, :, None]
    knn_prob = jnp.sum(jnp.where(id_match, weights, 0.0), -1)
    mixture = MIX_WEIGHT * knn_prob + (1.0 - MIX_WEIGHT) * p_lm.reshape(span_count, -1)
    token_loss = -jnp.log(mixture).reshape(row_count)
    match_f32 = jnp.where(id_match, 1.0, 0.0)
    dlogits = (
        -(MIX_WEIGHT / mixture)[..., None] * weights * (match_f32 - knn_prob[..., None])
    ).astype(jnp.bfloat16)
    knn_grad = jnp.einsum(
        "sqn,snd->sqd", dlogits, neigh_keys, preferred_element_type=jnp.float32
    ) * (2.0 * knn_scale)
    dquery = head_grad.astype(jnp.float32) + knn_grad.reshape(row_count, feature_width)
    back_params = (
        lax.all_gather(w_qkv, ("dp", "fsdp"), axis=0, tiled=True),
        lax.all_gather(w_out, ("dp", "fsdp"), axis=0, tiled=True),
        lax.all_gather(w_up, ("dp", "fsdp"), axis=0, tiled=True),
        lax.all_gather(w_down, ("dp", "fsdp"), axis=0, tiled=True),
        lax.all_gather(gains, ("dp", "fsdp"), axis=1, tiled=True),
        lax.all_gather(shifts, ("dp", "fsdp"), axis=1, tiled=True),
        lax.all_gather(biases, ("dp", "fsdp"), axis=1, tiled=True),
        lax.all_gather(up_bias, ("dp", "fsdp"), axis=0, tiled=True),
    )
    kv_back = lax.all_gather(kv_local, "fsdp", axis=0, tiled=True)
    gain_back = back_params[4].astype(jnp.float32)
    dstate, gain_grad_out, shift_grad_out = norm_back(dquery, unit_out, inverse_out, gain_back[2])
    dstate_low = dstate.astype(jnp.bfloat16)
    grad_w_down = contract_rows(gelu_low, dstate_low)
    bias_grad_down = jnp.sum(dstate_low.astype(jnp.float32), 0)
    dgelu = times_transposed(dstate_low, back_params[3])
    gelu_value, gelu_pull = jax.vjp(jax.nn.gelu, pre_act)
    dpre_low = gelu_pull(dgelu)[0].astype(jnp.bfloat16)
    grad_w_up = contract_rows(normed_mid_low, dpre_low)
    grad_up_bias = jnp.sum(dpre_low.astype(jnp.float32), 0)
    dnormed_mid = times_transposed(dpre_low, back_params[2])
    dhidden_part, gain_grad_mid, shift_grad_mid = norm_back(
        dnormed_mid, unit_mid, inverse_mid, gain_back[1]
    )
    dhidden_one = dstate + dhidden_part
    dhidden_low = dhidden_one.astype(jnp.bfloat16)
    grad_w_out = contract_rows(attended_low, dhidden_low)
    bias_grad_out = jnp.sum(dhidden_low.astype(jnp.float32), 0)
    dattended_low = times_transposed(dhidden_low, back_params[1]).astype(jnp.bfloat16)
    dattended_heads = dattended_low.reshape(row_count, head_count, head_depth)
    delta_rows = jnp.sum(
        dattended_heads.astype(jnp.float32) * attended.reshape(row_count, head_count, head_depth),
        -1,
    ).T

    def both_grad_step(block_index, grad_pair):
        block_start = block_index * block_rows

        def both_block_work(pair):
            dquery_acc, dkv_group = pair
            masked, key_heads, value_heads = scores_of(kv_back, block_start)
            prob_values = jnp.exp(masked - log_total[..., None])
            prob_low = prob_values.astype(jnp.bfloat16)
            dprob = jnp.einsum(
                "qhe,khe->hqk", dattended_heads, value_heads, preferred_element_type=jnp.float32
            )
            dscores = (prob_values * (dprob - delta_rows[..., None])).astype(jnp.bfloat16)
            dquery_acc = dquery_acc + jnp.einsum(
                "hqk,khe->qhe", dscores, key_heads, preferred_element_type=jnp.float32
            )
            dkey_heads = (
                jnp.einsum("hqk,qhe->khe", dscores, query_heads, preferred_element_type=jnp.float32)
                * score_scale
            )
            dvalue_heads = jnp.einsum(
                "hqk,qhe->khe", prob_low, dattended_heads, preferred_element_type=jnp.float32
            )
            block_grad = jnp.concatenate(
                [
                    dkey_heads.reshape(block_rows, feature_width),
                    dvalue_heads.reshape(block_rows, feature_width),
                ],
                1,
            )
            current = lax.dynamic_slice_in_dim(dkv_group, block_start, block_rows, 0)
            return (
                dquery_acc,
                lax.dynamic_update_slice_in_dim(dkv_group, current + block_grad, block_start, 0),
            )

        return lax.cond(block_start <= last_row, both_block_work, keep_same, grad_pair)

    zero_dquery = jnp.zeros((row_count, head_count, head_depth), jnp.float32)
    start_grads = (zero_dquery, jnp.zeros((group_size, 2 * feature_width), jnp.float32))
    dquery_acc, dkv_group = lax.fori_loop(0, block_count, both_grad_step, start_grads)
    dkv_mine = lax.psum_scatter(
        dkv_group.astype(jnp.bfloat16), "fsdp", scatter_dimension=0, tiled=True
    ).astype(jnp.float32)
    dqkv_low = jnp.concatenate(
        [(dquery_acc * score_scale).reshape(row_count, feature_width), dkv_mine], 1
    ).astype(jnp.bfloat16)
    grad_w_qkv = contract_rows(normed_in_low, dqkv_low)
    column_sums = jnp.sum(dqkv_low.astype(jnp.float32), 0)
    dnormed_in = times_transposed(dqkv_low, back_params[0])
    dinput_part, gain_grad_in, shift_grad_in = norm_back(
        dnormed_in, unit_in, inverse_in, gain_back[0]
    )
    grad_input = (dhidden_one + dinput_part).astype(jnp.bfloat16)
    grad_gains = jnp.stack([gain_grad_in, gain_grad_mid, gain_grad_out])
    grad_shifts = jnp.stack([shift_grad_in, shift_grad_mid, shift_grad_out])
    grad_biases = jnp.stack(
        [
            column_sums[:feature_width],
            column_sums[2 * feature_width :],
            bias_grad_out,
            bias_grad_down,
        ]
    )
    summed = (
        lax.psum_scatter(grad_w_qkv, ("dp", "fsdp"), scatter_dimension=0, tiled=True),
        lax.psum_scatter(grad_w_out, ("dp", "fsdp"), scatter_dimension=0, tiled=True),
        lax.psum_scatter(grad_w_up, ("dp", "fsdp"), scatter_dimension=0, tiled=True),
        lax.psum_scatter(grad_w_down, ("dp", "fsdp"), scatter_dimension=0, tiled=True),
        lax.psum_scatter(grad_gains, ("dp", "fsdp"), scatter_dimension=1, tiled=True),
        lax.psum_scatter(grad_shifts, ("dp", "fsdp"), scatter_dimension=1, tiled=True),
        lax.psum_scatter(grad_biases, ("dp", "fsdp"), scatter_dimension=1, tiled=True),
        lax.psum_scatter(grad_up_bias, ("dp", "fsdp"), scatter_dimension=0, tiled=True),
    )
    return (
        state_f32.astype(jnp.bfloat16),
        token_loss,
        grad_input,
        summed[0],
        summed[1],
        summed[2],
        summed[3],
        summed[4],
        summed[5],
        summed[6],
        summed[7],
    )


VMEM_LIMIT = 63 << 20
KNN_SCALE = 0.5 / 32.0
BF = jnp.bfloat16
F32 = jnp.float32
MESH = pl.DeviceIdType.MESH
NEG = -1e30


def dot(left, right, left_dim=1, right_dim=0):
    return lax.dot_general(
        left, right, (((left_dim,), (right_dim,)), ((), ())), preferred_element_type=F32
    )


def unit_of(values):
    center = values - jnp.mean(values, -1, keepdims=True)
    inverse = lax.rsqrt(jnp.mean(center * center, -1, keepdims=True) + EPSILON)
    return center * inverse, inverse


def ln_back(grad_rows, unit_rows, inverse, gain_row):
    scaled = grad_rows * gain_row
    first_mean = jnp.mean(scaled, -1, keepdims=True)
    second_mean = jnp.mean(scaled * unit_rows, -1, keepdims=True)
    return inverse * (scaled - first_mean - unit_rows * second_mean)


def col_sum(values):
    return jnp.sum(values, 0, keepdims=True)


def gelu_pair(u):
    k0 = math.sqrt(2.0 / math.pi)
    square = u * u
    t = jnp.tanh(u * (k0 + (k0 * 0.044715) * square))
    half = 0.5 * (1.0 + t)
    slope = half + (0.5 * u) * (1.0 - t * t) * (k0 + (3.0 * k0 * 0.044715) * square)
    return u * half, slope


GATHER_X_FIRST = (7, 3)
REDUCE_Z_FIRST = (5, 0, 7)
DOWN = {7: (0, 1), 13: (1, 1), 8: (2, 2), 9: (4, 2), 10: (6, 2)}

(
    DO_Y0, DO_Z, DO_F, DO_X, DO_Y, DO_C, DO_TOK, DO_MASK, DO_COLS, DO_TABLE, DO_UNPACK, DO_NORMOWN,
    DO_NORMOTHER, DO_PROJ, DO_ATTEND, DO_ATTOUT, DO_NORMMID, DO_UP, DO_DOWN, DO_KNN, DO_STATEOUT,
    DO_DSREST, DO_RC, DO_RY, DO_RX, DO_RF, DO_RZ, DO_GD, DO_DP, DO_GU, DO_DNO, DO_DNS, DO_DIO, DO_DIS,
    DO_BACKMID, DO_DAO, DO_DAS, DO_GO, DO_AB, DO_GQ, DO_BACKIN, DO_GP,
) = range(42)
ORDER = (
    (DO_Y0, 1), (DO_Y0, 0), (DO_Z, 12), (DO_Z, 11), (DO_Y0, 4), (DO_Y0, 6), (DO_Y0, 5), (DO_Y0, 2),
    (DO_TOK,), (DO_MASK,), (DO_Y0, 3), (DO_COLS,), (DO_TABLE, 2), (DO_TABLE, 0), (DO_TABLE, 3), (DO_F,
    12), (DO_Z, 0), (DO_Z, 1), (DO_TABLE, 1), (DO_X, 12), (DO_Z, 2), (DO_F, 11), (DO_Y, 12), (DO_X, 11),
    (DO_Z, 5), (DO_F, 0), (DO_X, 0), (DO_Z, 13), (DO_F, 1), (DO_Y, 11), (DO_C, 12), (DO_F, 2), (DO_X,
    1), (DO_Z, 4), (DO_UNPACK,), (DO_NORMOWN,), (DO_C, 0), (DO_NORMOTHER,), (DO_X, 2), (DO_Z, 3), (DO_F,
    5), (DO_PROJ, 0, 0), (DO_F, 13), (DO_PROJ, 0, 1), (DO_X, 5), (DO_Z, 6), (DO_C, 1), (DO_X, 13),
    (DO_Z, 8), (DO_C, 11), (DO_F, 4), (DO_PROJ, 1, 0), (DO_C, 2), (DO_PROJ, 1, 1), (DO_F, 3), (DO_X, 4),
    (DO_Z, 9), (DO_F, 6), (DO_PROJ, 2, 0), (DO_PROJ, 2, 1), (DO_ATTEND, 0), (DO_ATTEND, 1), (DO_C, 5),
    (DO_F, 8), (DO_ATTEND, 2), (DO_ATTEND, 3), (DO_C, 13), (DO_ATTOUT,), (DO_NORMMID, 0), (DO_NORMMID,
    1), (DO_UP, 2, 0), (DO_X, 3), (DO_Z, 7), (DO_X, 6), (DO_Z, 10), (DO_X, 8), (DO_C, 4), (DO_F, 9),
    (DO_F, 7), (DO_UP, 1, 0), (DO_C, 3), (DO_C, 6), (DO_X, 9), (DO_F, 10), (DO_UP, 0, 0), (DO_C, 8),
    (DO_UP, 3, 0), (DO_X, 7), (DO_X, 10), (DO_UP, 0, 1), (DO_UP, 2, 1), (DO_UP, 3, 1), (DO_UP, 1, 1),
    (DO_C, 9), (DO_DOWN, 13), (DO_DOWN, 8), (DO_C, 7), (DO_DOWN, 9), (DO_C, 10), (DO_DOWN, 7), (DO_DOWN,
    10), (DO_KNN, 0), (DO_KNN, 1), (DO_KNN, 2), (DO_KNN, 3), (DO_DSREST,), (DO_DP, 0, 0), (DO_DP, 1, 0),
    (DO_DP, 2, 0), (DO_DP, 3, 0), (DO_STATEOUT,), (DO_GD, 7), (DO_GD, 13), (DO_GD, 8), (DO_RC, 13),
    (DO_GD, 9), (DO_RC, 8), (DO_RC, 7), (DO_DP, 0, 1), (DO_DP, 3, 1), (DO_RX, 13), (DO_DP, 1, 1),
    (DO_RC, 9), (DO_DP, 2, 1), (DO_DNO, 2), (DO_DNO, 3), (DO_DNS, 1), (DO_DNO, 0), (DO_RF, 7), (DO_GD,
    10), (DO_GU, 0), (DO_DNS, 2), (DO_RF, 13), (DO_DNO, 1), (DO_GU, 1), (DO_GU, 2), (DO_RX, 8), (DO_GU,
    3), (DO_RX, 7), (DO_DNS, 3), (DO_RZ, 13), (DO_DNS, 0), (DO_RC, 3), (DO_RC, 4), (DO_RF, 8), (DO_RC,
    5), (DO_RX, 9), (DO_RZ, 7), (DO_RC, 6), (DO_RC, 10), (DO_RZ, 8), (DO_BACKMID,), (DO_GO,), (DO_DAO,
    1), (DO_DAS, 1), (DO_RF, 5), (DO_DAS, 0), (DO_RX, 3), (DO_DAO, 0), (DO_RF, 9), (DO_RC, 11), (DO_RF,
    3), (DO_AB, 2), (DO_RX, 4), (DO_AB, 0), (DO_RX, 5), (DO_AB, 1), (DO_RZ, 9), (DO_RX, 6), (DO_RZ, 3),
    (DO_RF, 4), (DO_AB, 3), (DO_DIO, 0), (DO_DIO, 2), (DO_DIO, 1), (DO_RX, 10), (DO_RF, 6), (DO_GQ, 0),
    (DO_DIO, 3), (DO_RY, 11), (DO_RZ, 5), (DO_DIS, 3), (DO_DIS, 0), (DO_DIS, 2), (DO_DIS, 1), (DO_RZ,
    4), (DO_GQ, 1), (DO_RF, 10), (DO_GQ, 2), (DO_RC, 0), (DO_RZ, 6), (DO_RC, 1), (DO_RZ, 10), (DO_RC,
    2), (DO_RX, 11), (DO_RF, 0), (DO_RF, 11), (DO_BACKIN,), (DO_GP,), (DO_RX, 1), (DO_RC, 12), (DO_RX,
    0), (DO_RF, 1), (DO_RY, 12), (DO_RX, 2), (DO_RZ, 11), (DO_RZ, 0), (DO_RX, 12), (DO_RZ, 1), (DO_RF,
    2), (DO_RF, 12), (DO_RZ, 2), (DO_RZ, 12),
)


def block_kernel(
    tokens, head_grad, w_qkv, w_out, w_up, w_down, gains, shifts, biases, up_bias, seq, counts, keys_in,
    ids, targets, p_lm, state_out, loss_out, gin_out, gqkv_out, gout_out, gup_out, gdown_out, gpk_out,
    wA, wD, wO, pk, prm, ubias, tokg, ni, qkv, mask, att_h, att_f, h1, nmg, gelu, slope, st, prec,
    hgrad, ksq, match, dsg, tcol, pcol, lcol, lossb, dnm, dnr, dattg, dqkv, dnr2, sendb, lowb, gA, gD,
    gO, gP, dRA, xRA, zRA, dRD, xRD, zRD, dRO, yRO, xRO, zRO, dRP, yRP, xRP, zRP, finA, finD, finO,
    finP, xOA, xOD, pg, dub, lsem, ysend, yrecv, zsend, zrecv, xsend, xrecv, csend, crecv, osem, msend,
    mrecv, asend, arecv, aloc, nsend, nrecv, dsend, drecv, psend, precv, rcs, rcr, rxs, rxr, rzs, rzr,
    rys, ryr, rfl, kn_sem,
):
    dp = lax.axis_index("dp")
    y = lax.axis_index("fsdp")
    z = dp // 4
    x = (dp // 2) % 2
    c = dp % 2
    oy = 1 - y
    ox = 1 - x
    oc = 1 - c

    def dev(zz, xx, cc, yy):
        return ((zz * 2 + xx) * 2 + cc, yy)

    z_to = [None] + [(z + j) % 4 for j in (1, 2, 3)]
    z_of = [z] + [(z - j) % 4 for j in (1, 2, 3)]
    zdev = [None] + [dev(zz, x, c, y) for zz in z_to[1:]]
    xdev = dev(z, ox, c, y)
    ydev = dev(z, x, c, oy)
    cdev = dev(z, x, oc, y)
    middle = (z == 1) | (z == 2)
    z_direct = {1: z != 3, 2: None, 3: z != 0}

    def when(cond, fn):
        if cond is None:
            fn()
        else:
            pl.when(cond)(fn)

    def rc(src, dst_ref, ss, rs, to):
        return pltpu.make_async_remote_copy(
            src_ref=src, dst_ref=dst_ref, send_sem=ss, recv_sem=rs, device_id=to, device_id_type=MESH
        )

    def lc(src, dst_ref, sem):
        return pltpu.make_async_copy(src, dst_ref, sem)

    pending = []
    finals = []
    late_recv = []
    tasks = {}

    def task(fn, name, *args):
        tasks[name] = functools.partial(fn, *args)

    def send(cp, cond=None):
        when(cond, cp.start)
        pending.append((cond, cp))

    my_rows = pl.ds(pl.multiple_of(y * 32, 32), 32)

    def up_cols(j, i, yy):
        return pl.ds(pl.multiple_of((8 * j + 2 * i + yy) * 128, 128), 128)

    def part_cols(part, yy):
        return pl.ds(pl.multiple_of(part * 1024 + yy * 512, 512), 512)

    for s in range(3):
        lc(w_qkv.at[:, part_cols(s, y)], wA.at[s, z, x, c, my_rows], lsem.at[s]).start()
    lc(w_out, wO.at[z, x, c, y], lsem.at[11]).start()
    lc(tokens, tokg.at[y], lsem.at[14]).start()
    for j in range(4):
        for i in range(4):
            lc(w_up.at[:, up_cols(j, i, y)], wA.at[3 + j, z, x, c, my_rows, pl.ds(i * 128, 128)],
               lsem.at[3 + j]).start()
    for t, (first, count) in DOWN.items():
        for h in range(first, first + count):
            lc(w_down.at[:, pl.ds(h * 128, 128)], wD.at[h, z, x, c], lsem.at[t]).start()
    for h in range(8):
        lc(keys_in.at[:, :, :, :, pl.ds(h * 128, 128)], gD.at[h], kn_sem.at[0]).start()
    lc(head_grad, hgrad, kn_sem.at[1]).start()

    quarter = (2 * dp + y) % 4
    pg[...] = jnp.zeros_like(pg)
    pg[0:3, 0:32] = gains[...].astype(F32)
    pg[3:6, 0:32] = shifts[...].astype(F32)
    pg[6:10, 0:32] = biases[...].astype(F32)
    small = pltpu.roll(pg[:, 0:128], quarter * 32, 1)
    pg[10:11, 0:128] = up_bias[...].astype(F32)
    row_id = lax.broadcasted_iota(jnp.int32, (16, 128), 0)
    pk[z, x, c, y] = jnp.where(row_id == 10, pg[:, 0:128], small).astype(BF)

    barrier = pltpu.get_barrier_semaphore()
    for to in (*zdev[1:], xdev, ydev, cdev):
        pl.semaphore_signal(barrier, inc=1, device_id=to, device_id_type=MESH)
    pl.semaphore_wait(barrier, 6)

    def weight(t, *index):
        if t < 7:
            return wA.at[(t, *index)]
        if t in DOWN:
            return wD.at[(pl.ds(*DOWN[t]), *index)]
        return (wO if t == 11 else pk).at[index]

    def z_view(t, zz):
        return weight(t, zz, x, c, y) if t in (11, 12) else weight(t, zz, x, c)

    def y_view(t):
        return wO.at[:, :, c, y] if t == 11 else pk.at[:, :, c, y]

    def c_view(t):
        return weight(t, slice(None), slice(None), c)

    def y0_full(t):
        view = wA.at[t, z, x, c, my_rows]
        return rc(view, view, ysend.at[t], yrecv.at[t], ydev)

    def start_y0(t):
        if t < 3:
            rc(w_qkv.at[:, part_cols(t, oy)], wA.at[t, z, x, c, my_rows], ysend.at[t], yrecv.at[t], ydev).start()
        else:
            for i in range(4):
                rc(w_up.at[:, up_cols(t - 3, i, oy)], wA.at[t, z, x, c, my_rows, pl.ds(i * 128, 128)],
                   ysend.at[t], yrecv.at[t], ydev).start()
        pending.append((None, y0_full(t)))

    def x_copy(t, j):
        view = z_view(t, z_of[j])
        return rc(view, view, xsend.at[t, j], xrecv.at[t, j], xdev)

    def pair_view(t, zz):
        return weight(t, zz, slice(None), c)

    def z_copy(t, j):
        view = pair_view(t, z) if t in GATHER_X_FIRST else z_view(t, z)
        return rc(view, view, zsend.at[t, j], zrecv.at[t, j], zdev[j])

    far = jnp.where(z == 1, 0, 3)
    far_sem = jnp.where(z == 1, 1, 3)

    def start_z(t):
        if t != 12:
            view = wA.at[t, z, x, c, my_rows] if t < 7 else z_view(t, z)
            lc(view, view, lsem.at[t]).wait()
        if t < 7:
            y0_full(t).wait_recv()
        if t not in GATHER_X_FIRST:
            for j in (2, 1, 3):
                send(z_copy(t, j), z_direct[j])
        send(x_copy(t, 0))

    def to_far(t, view):
        send(rc(view, view, zsend.at[t, 0], zrecv.at[t, far_sem], dev(far, x, c, y)), middle)

    def forward(t):
        if t in GATHER_X_FIRST:
            x_copy(t, 0).wait_recv()
            for j in (2, 1, 3):
                send(z_copy(t, j), z_direct[j])
        else:
            z_copy(t, 2).wait_recv()
            to_far(t, z_view(t, z_of[2]))
            send(x_copy(t, 2))

    def start_x(t):
        if t in GATHER_X_FIRST:
            z_copy(t, 2).wait_recv()
            to_far(t, pair_view(t, z_of[2]))
        else:
            for j in (1, 3):
                z_copy(t, j).wait_recv()
                send(x_copy(t, j))

    def x_done(t):
        if t in GATHER_X_FIRST:
            for j in (1, 3):
                z_copy(t, j).wait_recv()
        else:
            for j in range(4):
                x_copy(t, j).wait_recv()

    def y_copy(t):
        return rc(y_view(t), y_view(t), ysend.at[t - 4], yrecv.at[t - 4], ydev)

    def start_y(t):
        x_done(t)
        send(y_copy(t))

    def c_copy(t):
        return rc(c_view(t), c_view(t), csend.at[t], crecv.at[t], cdev)

    def start_c(t):
        if t not in (11, 12):
            x_done(t)
        else:
            y_copy(t).wait_recv()
        send(c_copy(t))

    def ready(t):
        c_copy(t).wait_recv()

    for t in range(14):
        if t < 7:
            task(start_y0, (DO_Y0, t), t)
        task(start_z, (DO_Z, t), t)
        task(forward, (DO_F, t), t)
        task(start_x, (DO_X, t), t)
        if t in (11, 12):
            task(start_y, (DO_Y, t), t)
        task(start_c, (DO_C, t), t)

    tok_copy = rc(tokens, tokg.at[y], msend.at[0], mrecv.at[0], ydev)
    task(send, (DO_TOK,), tok_copy)

    first_end = seq[0, 0]
    second_end = first_end + seq[0, 1]

    def segment(pos):
        return (pos >= first_end).astype(jnp.int32) + (pos >= second_end).astype(jnp.int32)

    def mask_rows(i, _):
        rows = pl.ds(pl.multiple_of(i * 128, 128), 128)
        qpos = i * 128 + lax.broadcasted_iota(jnp.int32, (128, 512), 0)
        kpos = lax.broadcasted_iota(jnp.int32, (128, 512), 1)
        good = (segment(qpos) == segment(kpos)) & (kpos <= qpos)
        mask[rows, :] = jnp.where(good, 0.0, NEG)
        return 0

    def make_mask():
        lax.fori_loop(0, 4, mask_rows, 0)

    task(make_mask, (DO_MASK,))

    def make_columns():
        wide = jnp.concatenate([targets[...].astype(F32), p_lm[...], jnp.zeros((6, 256), F32)], 0)
        cols = jnp.transpose(wide)
        tcol[...] = cols[:, 0:1]
        pcol[...] = cols[:, 1:2]
        lc(gD, gD, kn_sem.at[0]).wait()
        lc(head_grad, hgrad, kn_sem.at[1]).wait()

    task(make_columns, (DO_COLS,))

    def keys_of(s):
        return jnp.concatenate([gD[h, s // 4, (s // 2) % 2, s % 2] for h in range(8)], 1)

    def make_table(b):
        eye = lax.broadcasted_iota(jnp.int32, (128, 128), 0) == lax.broadcasted_iota(jnp.int32, (128, 128), 1)
        slot = lax.broadcasted_iota(jnp.int32, (16, 128), 1)
        for s in range(b * 4, b * 4 + 4):
            rows = slice(s * 16, s * 16 + 16)
            kk = keys_of(s)
            square = jnp.broadcast_to(col_sum(jnp.where(eye, dot(kk, kk, 1, 1), 0.0)), (16, 128))
            ksq[rows, :] = jnp.where(slot < counts[0, s], square * -KNN_SCALE, NEG)
            match[rows, :] = jnp.where(ids[s : s + 1, :].astype(F32) == tcol[rows, :], 1.0, 0.0)

    for b in range(4):
        task(make_table, (DO_TABLE, b), b)

    def unpack():
        ready(12)
        for g in range(8):
            total = None
            for i in range(4):
                piece = pk[g // 2, g % 2, i // 2, i % 2].astype(F32)
                total = piece if total is None else total + piece
            prm[:, g * 128 : (g + 1) * 128] = total
        for d in range(16):
            piece = pk[d // 4, (d // 2) % 2, d % 2, y].astype(F32)
            ubias[0:1, d * 128 : (d + 1) * 128] = piece[10:11, :]

    task(unpack, (DO_UNPACK,))

    def row(r):
        return prm[r : r + 1, :]

    def norm_in(half):
        def rows_of(i, _):
            rows = pl.ds(pl.multiple_of(i * 64, 64), 64)
            unit, _inv = unit_of(tokg[half, rows, :].astype(F32))
            ni[half, rows, :] = (unit * row(0) + row(3)).astype(BF)
            return 0

        lax.fori_loop(0, 4, rows_of, 0)

    def norm_own():
        lc(tokens, tokg.at[y], lsem.at[14]).wait()
        norm_in(y)

    def norm_other():
        tok_copy.wait_recv()
        norm_in(oy)

    task(norm_own, (DO_NORMOWN,))
    task(norm_other, (DO_NORMOTHER,))

    head_cols = pl.ds(pl.multiple_of(y * 512, 512), 512)

    def project(s, own):
        if own:
            ready(s)
        half = y if own else oy
        value = dot(ni[half], wA[s].reshape(1024, 512))
        if s != 1:
            value = value + prm[6 + s // 2 : 7 + s // 2, head_cols]
        qkv[s, half] = value.astype(BF)

    for s in range(3):
        task(project, (DO_PROJ, s, 0), s, True)
        task(project, (DO_PROJ, s, 1), s, False)

    lane = lax.broadcasted_iota(jnp.int32, (1, 128), 1)
    in_head = [lane < 64, lane >= 64]

    def probs_of(qe, k2, half):
        nk = 256 * (half + 1)
        s = dot(qe, k2[:nk], 1, 1) * 0.125 + mask[half * 256 : half * 256 + 256, :nk]
        ex = jnp.exp(s - jnp.max(s, -1, keepdims=True))
        return ex * (1.0 / jnp.sum(ex, -1, keepdims=True))

    def attend(p):
        cols = slice(p * 128, p * 128 + 128)
        q2 = qkv[0, :, :, cols]
        k2 = qkv[1, :, :, cols].reshape(512, 128)
        v2 = qkv[2, :, :, cols].reshape(512, 128)
        for half in range(2):
            nk = 256 * (half + 1)
            outs = []
            for e in range(2):
                qe = jnp.where(in_head[e], q2[half], jnp.zeros_like(q2[half]))
                outs.append(dot(probs_of(qe, k2, half).astype(BF), v2[:nk]))
            att_h[half, :, cols] = jnp.where(in_head[0], outs[0], outs[1]).astype(BF)
        send(att_copy(p))
        own_att(p).start()

    def pair_cols(p):
        return pl.ds(pl.multiple_of(y * 512 + p * 128, 128), 128)

    def att_copy(p):
        return rc(att_h.at[oy, :, pl.ds(p * 128, 128)], att_f.at[:, pair_cols(p)], asend.at[p], arecv.at[p], ydev)

    def own_att(p):
        return lc(att_h.at[y, :, pl.ds(p * 128, 128)], att_f.at[:, pair_cols(p)], aloc.at[p])

    for p in range(4):
        task(attend, (DO_ATTEND, p), p)

    def attention_out():
        for p in range(4):
            own_att(p).wait()
            att_copy(p).wait_recv()
        ready(11)
        h1[...] = dot(att_f[...], wO[...].reshape(1024, 1024)) + row(8)

    task(attention_out, (DO_ATTOUT,))

    def nm_copy(i):
        view = nmg.at[y, pl.ds(i * 128, 128)]
        return rc(view, view, nsend.at[i], nrecv.at[i], ydev)

    def norm_mid(i):
        def rows_of(k, _):
            rows = pl.ds(pl.multiple_of(k * 64, 64), 64)
            value = h1[rows, :] + tokg[y, rows, :].astype(F32)
            h1[rows, :] = value
            unit, _inv = unit_of(value)
            nmg[y, rows, :] = (unit * row(1) + row(4)).astype(BF)
            return 0

        lax.fori_loop(2 * i, 2 * i + 2, rows_of, 0)
        send(nm_copy(i))

    task(norm_mid, (DO_NORMMID, 0), 0)
    task(norm_mid, (DO_NORMMID, 1), 1)

    def up(j, own):
        if own:
            ready(3 + j)
        elif j == 0:
            nm_copy(0).wait_recv()
            nm_copy(1).wait_recv()
        half = y if own else oy
        cols = slice(j * 512, (j + 1) * 512)
        u = dot(nmg[half], wA[3 + j].reshape(1024, 512)) + ubias[0:1, cols]
        value, dvalue = gelu_pair(u)
        gelu[half, :, cols] = value.astype(BF)
        slope[half, :, cols] = dvalue.astype(BF)

    for j in range(4):
        task(up, (DO_UP, j, 0), j, True)
        task(up, (DO_UP, j, 1), j, False)

    def part_copy(t):
        cols = pl.ds(DOWN[t][0] * 128, DOWN[t][1] * 128)
        sem = list(DOWN).index(t)
        return rc(sendb.at[0, :, cols], prec.at[:, cols], psend.at[sem], precv.at[sem], ydev)

    def down_weight(first, count):
        return jnp.concatenate([wD[h].reshape(2048, 128) for h in range(first, first + count)], 1)

    def down(t):
        ready(t)
        first, count = DOWN[t]
        cols = slice(first * 128, (first + count) * 128)
        right = down_weight(first, count)
        sendb[0, :, cols] = dot(gelu[oy], right).astype(BF)
        send(part_copy(t))
        st[:, cols] = dot(gelu[y], right) + (h1[:, cols] + prm[9:10, cols])

    for t in DOWN:
        task(down, (DO_DOWN, t), t)

    def add_row(r, value):
        pg[r : r + 1, :] = pg[r : r + 1, :] + value

    def ds_copy(j, b):
        rows = pl.ds(b * 64, 64) if j < 2 else pl.ds(0, 256)
        cols = pl.ds(j * 128, 128) if j < 2 else pl.ds((j - 1) * 256, 256)
        view = dsg.at[y, rows, cols]
        sem = 4 * j + b if j < 2 else 6 + j
        return rc(view, view, dsend.at[sem], drecv.at[sem], ydev)

    ds_waited = []

    def need_ds(*columns):
        for j in columns:
            if j not in ds_waited:
                ds_waited.append(j)
                for b in range(4 if j < 2 else 1):
                    ds_copy(j, b).wait_recv()

    def neighbours(b):
        if b == 0:
            pg[...] = jnp.zeros_like(pg)
            for t in DOWN:
                part_copy(t).wait_recv()
        rows = slice(b * 64, b * 64 + 64)
        value = st[rows, :] + prec[rows, :].astype(F32)
        lowb[rows, :] = value.astype(BF)
        unit, inv = unit_of(value)
        query = (unit * row(2) + row(5)).astype(BF)
        raw = jnp.concatenate(
            [dot(query[i * 16 : i * 16 + 16], keys_of(b * 4 + i), 1, 1) for i in range(4)], 0
        )
        logits = (2.0 * KNN_SCALE) * raw + ksq[rows, :]
        ex = jnp.exp(logits - jnp.max(logits, -1, keepdims=True))
        weights = ex / jnp.sum(ex, -1, keepdims=True)
        same = match[rows, :]
        knn_prob = jnp.sum(same * weights, -1, keepdims=True)
        mixture = MIX_WEIGHT * knn_prob + (1.0 - MIX_WEIGHT) * pcol[rows, :]
        lcol[rows, :] = -jnp.log(mixture)
        dlog = (-(MIX_WEIGHT / mixture) * weights * (same - knn_prob)).astype(BF)
        kgrad = jnp.concatenate(
            [dot(dlog[i * 16 : i * 16 + 16], keys_of(b * 4 + i)) for i in range(4)], 0
        )
        dquery = hgrad[rows, :].astype(F32) + kgrad * (2.0 * KNN_SCALE)
        add_row(2, col_sum(dquery * unit))
        add_row(5, col_sum(dquery))
        dvalue = ln_back(dquery, unit, inv, row(2))
        st[rows, :] = dvalue
        low = dvalue.astype(BF)
        add_row(9, col_sum(low.astype(F32)))
        dsg[y, rows, :] = low
        send(ds_copy(0, b))
        send(ds_copy(1, b))

    for b in range(4):
        task(neighbours, (DO_KNN, b), b)

    out_state = lc(lowb, state_out, osem.at[0])

    def state_done():
        out_state.start()
        lossb[...] = jnp.transpose(jnp.broadcast_to(lcol[...], (256, 128)))[0:1, :]
        cp = lc(lossb, loss_out, osem.at[1])
        cp.start()
        finals.append(cp)

    task(state_done, (DO_STATEOUT,))

    def ds_rest():
        send(ds_copy(2, 0))
        send(ds_copy(3, 0))
        send(ds_copy(4, 0))

    task(ds_rest, (DO_DSREST,))

    slot_of = {3: 0, 4: 1, 5: 2, 6: 3, 0: 0, 1: 1, 2: 2}

    every = slice(None)

    def pick(refs, t, *index):
        if t < 7:
            return refs[0].at[(slot_of[t] if refs[0] is gA else t, *index)]
        if t in DOWN:
            return refs[1].at[(pl.ds(*DOWN[t]), *index)]
        return refs[2 if t == 11 else 3].at[index]

    g_refs = (gA, gD, gO, gP)
    c_refs = (dRA, dRD, dRO, dRP)
    y_refs = (None, None, yRO, yRP)
    x_refs = (xRA, xRD, xRO, xRP)
    z_refs = (zRA, zRD, zRO, zRP)

    def g_at(t, zz, xx):
        return pick(g_refs, t, zz, xx, c, y) if t in (11, 12) else pick(g_refs, t, zz, xx, c)

    def rs_c(t):
        return rc(pick(g_refs, t, every, every, oc), pick(c_refs, t, every), rcs.at[t], rcr.at[t], cdev)

    def rs_y(t):
        return rc(pick(g_refs, t, every, every, c, oy), pick(y_refs, t, every), rys.at[t], ryr.at[t], ydev)

    def x_one(t):
        k = REDUCE_Z_FIRST.index(t)
        return xOA.at[k] if t < 7 else xOD.at[k, pl.ds(0, DOWN[t][1])]

    def rs_x(t):
        if t in REDUCE_Z_FIRST:
            return rc(g_at(t, z, ox), x_one(t), rxs.at[t], rxr.at[t], xdev)
        return rc(g_at(t, every, ox), pick(x_refs, t, every), rxs.at[t], rxr.at[t], xdev)

    def z_block(t, zz):
        return g_at(t, zz, every if t in REDUCE_Z_FIRST else x)

    def z_slot(t, j):
        if t in REDUCE_Z_FIRST:
            return pick((x_refs, z_refs)[j // 2], t, pl.ds(2 * (j % 2), 2))
        return pick(z_refs, t, j)

    def rs_z(t, j):
        return rc(z_block(t, z_to[j]), z_slot(t, j), rzs.at[t, j], rzr.at[t, j], zdev[j])

    end_block = jnp.where(z == 0, 3, 0)
    end_to = dev(jnp.where(z == 0, 1, 2), x, c, y)
    is_end = (z == 0) | (z == 3)

    def rs_end(t):
        return rc(z_block(t, end_block), z_slot(t, 0), rzs.at[t, 0], rzr.at[t, 0], end_to)

    def add_to(ref, other):
        ref[...] = (ref[...].astype(F32) + other.astype(F32)).astype(ref.dtype)

    def rs_after_c(t):
        rs_c(t).wait_recv()
        for i in range(4):
            add_to(pick(g_refs, t, i, every, c), pick(c_refs, t, i)[...])
        if t in REDUCE_Z_FIRST:
            start_zs(t)
        else:
            (rs_y(t) if t in (11, 12) else rs_x(t)).start()

    def rs_after_y(t):
        rs_y(t).wait_recv()
        for i in range(4):
            add_to(pick(g_refs, t, i, every, c, y), pick(y_refs, t, i)[...])
        rs_x(t).start()

    def start_zs(t):
        when(is_end, rs_end(t).start)
        when(z_direct[1], rs_z(t, 1).start)
        when(z_direct[3], rs_z(t, 3).start)
        when(is_end, rs_z(t, 2).start)

    def z_arrived(t):
        rs_z(t, 2).wait_recv()
        pl.when(z != 0)(rs_z(t, 1).wait_recv)
        pl.when(z != 3)(rs_z(t, 3).wait_recv)

    def rs_after_x(t):
        if t in REDUCE_Z_FIRST:
            z_arrived(t)

            def add(*slots):
                total = g_at(t, z, every)[...].astype(F32)
                for j in slots:
                    total = total + z_slot(t, j)[...].astype(F32)
                g_at(t, z, every)[...] = total.astype(BF)

            pl.when(z == 0)(functools.partial(add, 2, 3))
            pl.when(z == 3)(functools.partial(add, 2, 1))
            pl.when(middle)(functools.partial(add, 2, 1, 3))
            rs_x(t).start()
        else:
            rs_x(t).wait_recv()
            for i in range(4):
                add_to(g_at(t, i, x), pick(x_refs, t, i)[...])
            start_zs(t)

    def rs_forward(t):
        def go():
            rs_end(t).wait_recv()
            add_to(z_block(t, z_to[2]), z_slot(t, 0)[...])
            rs_z(t, 2).start()

        pl.when(middle)(go)

    def rs_sends(t):
        out = [(None, rs_c(t)), (None, rs_x(t)), (None, rs_z(t, 2))]
        if t in (11, 12):
            out.append((None, rs_y(t)))
        return out + [(z_direct[1], rs_z(t, 1)), (z_direct[3], rs_z(t, 3)), (is_end, rs_end(t))]

    def out_cols(t, yy):
        if t < 3:
            return [(gqkv_out, part_cols(t, yy), pl.ds(0, 512))]
        return [(gup_out, up_cols(t - 3, i, yy), pl.ds(i * 128, 128)) for i in range(4)]

    def rs_finish(t):
        if t < 7:
            fin = finA.at[t]
        elif t in DOWN:
            fin = finD.at[pl.ds(*DOWN[t])]
        else:
            fin = finO if t == 11 else finP
        own = g_at(t, z, x)
        if t in REDUCE_Z_FIRST:
            rs_x(t).wait_recv()
            total = own[...].astype(F32) + x_one(t)[...].astype(F32)
            fin[...] = total.reshape(fin.shape)
        else:
            z_arrived(t)
            near = jnp.where(z == 0, 3, 1)
            total = own[...].astype(F32)
            for j in (2, near):
                total = total + pick(z_refs, t, j)[...].astype(F32)
            fin[...] = total.reshape(fin.shape)

            def third():
                fin[...] = fin[...] + pick(z_refs, t, 3)[...].astype(F32).reshape(fin.shape)

            pl.when(middle)(third)
        if t not in (3, 4, 5):
            pending.extend(rs_sends(t))
        if t < 7:
            for ref, cols, inner in out_cols(t, y):
                lc(finA.at[t, y, :, inner], ref.at[:, cols], rfl.at[t]).start()
                rc(finA.at[t, oy, :, inner], ref.at[:, cols], rys.at[t], ryr.at[t], ydev).start()
            full = finA.at[t, y]
            finals.append(lc(full, full, rfl.at[t]))
            both = rc(full, full, rys.at[t], ryr.at[t], ydev)
            pending.append((None, both))
            late_recv.append(both)
        else:
            if t in DOWN:
                for h in range(DOWN[t][0], sum(DOWN[t])):
                    lc(finD.at[h], gdown_out.at[:, pl.ds(h * 128, 128)], rfl.at[t]).start()
                finals.append(lc(fin, fin, rfl.at[t]))
            else:
                cp = lc(fin, gout_out if t == 11 else gpk_out, rfl.at[t])
                cp.start()
                finals.append(cp)

    for t in range(14):
        task(rs_after_c, (DO_RC, t), t)
        if t in (11, 12):
            task(rs_after_y, (DO_RY, t), t)
        task(rs_after_x, (DO_RX, t), t)
        task(rs_forward, (DO_RF, t), t)
        task(rs_finish, (DO_RZ, t), t)

    def make_down(t):
        first, count = DOWN[t]
        need_ds(first if first < 2 else first // 2 + 1)
        ds_cols = dsg[:, :, first * 128 : (first + count) * 128].reshape(512, count * 128)
        for i in range(4):
            part = gelu[:, :, i * 512 : (i + 1) * 512].reshape(512, 512)
            value = dot(part, ds_cols, 0, 0).astype(BF)
            for k in range(count):
                gD[first + k, i] = value[:, k * 128 : (k + 1) * 128].reshape(2, 2, 128, 128)
        rs_c(t).start()

    for t in DOWN:
        task(make_down, (DO_GD, t), t)

    def make_a(t, left, right):
        for i in range(4):
            part = left[:, :, i * 256 : (i + 1) * 256].reshape(512, 256)
            gA[slot_of[t], i] = dot(part, right, 0, 0).astype(BF).reshape(2, 2, 64, 512)
        rs_c(t).start()

    dub_started = []

    def make_dpre(i, own):
        if not own:
            need_ds(0, 1, 2, 3, 4)
        half = y if own else oy
        cols = slice(i * 512, (i + 1) * 512)
        acc = None
        for j in range(4):
            right = jnp.concatenate([wD[2 * j + k, i].reshape(512, 128) for k in range(2)], 1)
            part = dot(dsg[half, :, j * 256 : (j + 1) * 256], right, 1, 1)
            acc = part if acc is None else acc + part
        low = (acc * slope[half, :, cols].astype(F32)).astype(BF)
        slope[half, :, cols] = low
        total = col_sum(low.astype(F32))
        if i in dub_started:
            total = total + dub[0:1, cols]
        dub_started.append(i)
        dub[0:1, cols] = total

    def up_grad(j):
        make_a(3 + j, nmg, slope[:, :, j * 512 : (j + 1) * 512].reshape(512, 512))

    for j in range(4):
        task(make_dpre, (DO_DP, j, 0), j, True)
        task(make_dpre, (DO_DP, j, 1), j, False)
        task(up_grad, (DO_GU, j), j)

    def dnorm_mid(half, n):
        acc = None
        for j in range(4):
            part = dot(slope[half, :, j * 512 : (j + 1) * 512], wA[3 + j, n].reshape(256, 512), 1, 1)
            acc = part if acc is None else acc + part
        return acc

    def dnorm_in(half, n):
        acc = None
        for s in range(3):
            part = dot(dqkv[s, half], wA[s, n].reshape(256, 512), 1, 1)
            acc = part if acc is None else acc + part
        return acc

    def share_copy(slot, recv, sem0, n):
        cols = pl.ds(n * 256, 256)
        return rc(sendb.at[slot, :, cols], recv.at[:, cols], msend.at[sem0 + n], mrecv.at[sem0 + n], ydev)

    def share(fn, slot, recv, sem0, n):
        sendb[slot, :, n * 256 : (n + 1) * 256] = fn(oy, n).astype(BF)
        send(share_copy(slot, recv, sem0, n))

    def keep(fn, n):
        dnm[:, n * 256 : (n + 1) * 256] = fn(y, n)

    for n in range(4):
        task(share, (DO_DNO, n), dnorm_mid, 1, dnr, 11, n)
        task(keep, (DO_DNS, n), dnorm_mid, n)
        task(share, (DO_DIO, n), dnorm_in, 3, dnr2, 16, n)
        task(keep, (DO_DIS, n), dnorm_in, n)

    zero_row = jnp.zeros((1, 1024), F32)

    def back_mid():
        out_state.wait()
        for n in range(4):
            share_copy(1, dnr, 11, n).wait_recv()

        def rows_of(i, carry):
            a, b, d = carry
            rows = pl.ds(pl.multiple_of(i * 64, 64), 64)
            dy = dnm[rows, :] + dnr[rows, :].astype(F32)
            unit, inv = unit_of(h1[rows, :])
            total = st[rows, :] + ln_back(dy, unit, inv, row(1))
            st[rows, :] = total
            low = total.astype(BF)
            lowb[rows, :] = low
            return a + col_sum(dy * unit), b + col_sum(dy), d + col_sum(low.astype(F32))

        a, b, d = lax.fori_loop(0, 4, rows_of, (zero_row, zero_row, zero_row))
        pg[1:2, :] = a
        pg[4:5, :] = b
        pg[8:9, :] = d

    task(back_mid, (DO_BACKMID,))

    def datt(yy, k):
        return dot(lowb[...], wO[2 * yy + k].reshape(256, 1024), 1, 1).astype(BF)

    def da_copy(k):
        cols = pl.ds(k * 256, 256)
        return rc(sendb.at[2, :, cols], dattg.at[y, :, cols], dsend.at[11 + k], drecv.at[11 + k], ydev)

    def datt_other(k):
        sendb[2, :, k * 256 : (k + 1) * 256] = datt(oy, k)
        send(da_copy(k))

    def datt_own(k):
        dattg[y, :, k * 256 : (k + 1) * 256] = datt(y, k)

    for k in range(2):
        task(datt_other, (DO_DAO, k), k)
        task(datt_own, (DO_DAS, k), k)

    def out_grad():
        for i in range(4):
            part = att_f[:, i * 256 : (i + 1) * 256]
            gO[i] = dot(part, lowb[...], 0, 0).astype(BF).reshape(2, 2, 2, 32, 1024)
        rs_c(11).start()

    task(out_grad, (DO_GO,))

    def attend_back(p):
        if p % 2 == 0:
            da_copy(p // 2).wait_recv()
        cols = slice(p * 128, p * 128 + 128)
        q2 = qkv[0, :, :, cols]
        k2 = qkv[1, :, :, cols].reshape(512, 128)
        v2 = qkv[2, :, :, cols].reshape(512, 128)
        do2 = dattg[:, :, cols]
        zero = jnp.zeros((512, 128), BF)
        dks = [None, None]
        dvs = [None, None]
        for half in range(2):
            nk = 256 * (half + 1)
            dq = None
            for e in range(2):
                qe = jnp.where(in_head[e], q2[half], zero[:256])
                doe = jnp.where(in_head[e], do2[half], zero[:256])
                ke = jnp.where(in_head[e], k2[:nk], zero[:nk])
                probs = probs_of(qe, k2, half)
                dprob = dot(doe, v2[:nk], 1, 1)
                delta = jnp.sum(probs * dprob, -1, keepdims=True)
                ds = (probs * (dprob - delta)).astype(BF)
                part = dot(ds, ke)
                dq = part if dq is None else dq + part
                dk = dot(ds, qe, 0, 0)
                dv = dot(probs.astype(BF), doe, 0, 0)
                for kb in range(half + 1):
                    rows = slice(kb * 256, kb * 256 + 256)
                    dks[kb] = dk[rows] if dks[kb] is None else dks[kb] + dk[rows]
                    dvs[kb] = dv[rows] if dvs[kb] is None else dvs[kb] + dv[rows]
            dqkv[0, half, :, cols] = (dq * 0.125).astype(BF)
        for kb in range(2):
            dqkv[1, kb, :, cols] = (dks[kb] * 0.125).astype(BF)
            dqkv[2, kb, :, cols] = dvs[kb].astype(BF)

    for p in range(4):
        task(attend_back, (DO_AB, p), p)

    def qkv_grad(s):
        for cond, cp in rs_sends(3 + s):
            when(cond, cp.wait_send)
        make_a(s, ni, dqkv[s].reshape(512, 512))

    for s in range(3):
        task(qkv_grad, (DO_GQ, s), s)

    def back_in():
        for n in range(4):
            share_copy(3, dnr2, 16, n).wait_recv()

        def rows_of(i, carry):
            a, b = carry
            rows = pl.ds(pl.multiple_of(i * 64, 64), 64)
            dy = dnm[rows, :] + dnr2[rows, :].astype(F32)
            unit, inv = unit_of(tokg[y, rows, :].astype(F32))
            hgrad[rows, :] = (st[rows, :] + ln_back(dy, unit, inv, row(0))).astype(BF)
            return a + col_sum(dy * unit), b + col_sum(dy)

        a, b = lax.fori_loop(0, 4, rows_of, (zero_row, zero_row))
        pg[0:1, :] = a
        pg[3:4, :] = b
        cp = lc(hgrad, gin_out, osem.at[2])
        cp.start()
        finals.append(cp)

    task(back_in, (DO_BACKIN,))

    def small_grads():
        pg[6:7, head_cols] = col_sum(dqkv[0].reshape(512, 512).astype(F32))
        pg[7:8, head_cols] = col_sum(dqkv[2].reshape(512, 512).astype(F32))
        for d in range(32):
            piece = pg[:, (d // 4) * 128 : (d // 4) * 128 + 128]
            mine = jnp.where(y == d % 2, dub[0:1, (d // 2) * 128 : (d // 2) * 128 + 128], 0.0)
            gP[d // 8, (d // 4) % 2, (d // 2) % 2, d % 2] = jnp.where(row_id == 10, mine, piece)
        rs_c(12).start()

    task(small_grads, (DO_GP,))

    for name in ORDER:
        tasks.pop(name)()
    assert not tasks, sorted(tasks)
    for cp in late_recv:
        cp.wait_recv()
    for cond, cp in pending:
        when(cond, cp.wait_send)
    for cp in finals:
        cp.wait()


def finish_kernel(state, loss, gin, gqkv, gout, gup, gdown, gpk, *refs):
    outs, (sem,) = refs[:11], refs[11:]
    big = [(state, 0), (loss, 1), (gin, 2), (gqkv, 3), (gout, 4), (gup, 5), (gdown, 6)]
    copies = [pltpu.make_async_copy(src, outs[i], sem.at[i]) for src, i in big]
    for cp in copies:
        cp.start()
    quarter = (2 * lax.axis_index("dp") + lax.axis_index("fsdp")) % 4
    total = gpk[...]
    mine = pltpu.roll(total, ((4 - quarter) % 4) * 32, 1)
    outs[7][...] = mine[0:3, 0:32]
    outs[8][...] = mine[3:6, 0:32]
    outs[9][...] = mine[6:10, 0:32]
    outs[10][...] = total[10:11, :]
    for cp in copies:
        cp.wait()


SCRATCH = dict(
    wA=((7, 4, 2, 2, 64, 512), BF), wD=((8, 4, 2, 2, 128, 128), BF), wO=((4, 2, 2, 2, 32, 1024), BF),
    pk=((4, 2, 2, 2, 16, 128), BF), prm=((16, 1024), F32), ubias=((8, 2048), F32),
    tokg=((2, 256, 1024), BF), ni=((2, 256, 1024), BF), qkv=((3, 2, 256, 512), BF), mask=((512, 512), F32),
    att_h=((2, 256, 512), BF), att_f=((256, 1024), BF), h1=((256, 1024), F32), nmg=((2, 256, 1024), BF),
    gelu=((2, 256, 2048), BF), slope=((2, 256, 2048), BF), st=((256, 1024), F32), prec=((256, 1024), BF),
    hgrad=((256, 1024), BF), ksq=((256, 128), F32), match=((256, 128), F32), dsg=((2, 256, 1024), BF),
    tcol=((256, 1), F32), pcol=((256, 1), F32), lcol=((256, 1), F32), lossb=((1, 256), F32),
    dnm=((256, 1024), F32), dnr=((256, 1024), BF), dattg=((2, 256, 512), BF), dqkv=((3, 2, 256, 512), BF),
    dnr2=((256, 1024), BF), sendb=((4, 256, 1024), BF), lowb=((256, 1024), BF),
    gA=((4, 4, 2, 2, 64, 512), BF), gD=((8, 4, 2, 2, 128, 128), BF), gO=((4, 2, 2, 2, 32, 1024), BF),
    gP=((4, 2, 2, 2, 16, 128), F32),
    dRA=((7, 4, 2, 64, 512), BF), xRA=((7, 4, 64, 512), BF), zRA=((7, 4, 64, 512), BF),
    dRD=((8, 4, 2, 128, 128), BF), xRD=((8, 4, 128, 128), BF), zRD=((8, 4, 128, 128), BF),
    dRO=((4, 2, 2, 32, 1024), BF), yRO=((4, 2, 32, 1024), BF), xRO=((4, 32, 1024), BF), zRO=((4, 32, 1024), BF),
    dRP=((4, 2, 2, 16, 128), F32), yRP=((4, 2, 16, 128), F32), xRP=((4, 16, 128), F32), zRP=((4, 16, 128), F32),
    finA=((7, 2, 32, 512), F32), finD=((8, 128, 128), F32), finO=((32, 1024), F32), finP=((16, 128), F32),
    xOA=((3, 64, 512), BF), xOD=((3, 2, 128, 128), BF), pg=((16, 1024), F32), dub=((8, 2048), F32),
)
SEMS = dict(
    lsem=(15,), ysend=(9,), yrecv=(9,), zsend=(14, 4), zrecv=(14, 4), xsend=(14, 4), xrecv=(14, 4),
    csend=(14,), crecv=(14,), osem=(3,), msend=(20,), mrecv=(20,), asend=(4,), arecv=(4,), aloc=(4,),
    nsend=(2,), nrecv=(2,), dsend=(13,), drecv=(13,), psend=(5,), precv=(5,), rcs=(14,), rcr=(14,), rxs=(14,), rxr=(14,),
    rzs=(14, 4), rzr=(14, 4), rys=(14,), ryr=(14,), rfl=(14,), kn_sem=(2,),
)


def on_device_fused(
    tokens, head_grad, w_qkv, w_out, w_up, w_down, gains, shifts, biases, up_bias, seq_lengths,
    neigh_keys, neigh_ids, neigh_counts, targets, p_lm,
):
    keys = neigh_keys.reshape(4, 2, 2, 128, 1024)
    anywhere = pl.BlockSpec(memory_space=pl.ANY)
    vmem = pl.BlockSpec(memory_space=pltpu.VMEM)
    smem = pl.BlockSpec(memory_space=pltpu.SMEM)
    shape = jax.ShapeDtypeStruct
    results = [
        shape((256, 1024), BF),
        shape((1, 256), F32),
        shape((256, 1024), BF),
        shape((32, 3072), F32),
        shape((32, 1024), F32),
        shape((32, 4096), F32),
        shape((128, 1024), F32),
    ]
    held = pl.pallas_call(
        block_kernel,
        out_shape=results + [shape((16, 128), F32)],
        in_specs=[anywhere] * 6 + [vmem] * 4 + [smem, smem, anywhere, vmem, vmem, vmem],
        out_specs=[anywhere] * 8,
        scratch_shapes=[pltpu.VMEM(*SCRATCH[k]) for k in SCRATCH]
        + [pltpu.SemaphoreType.DMA(SEMS[k]) for k in SEMS],
        compiler_params=pltpu.CompilerParams(
            collective_id=0, has_side_effects=True, vmem_limit_bytes=VMEM_LIMIT
        ),
        name="block",
    )(
        tokens, head_grad, w_qkv, w_out, w_up, w_down, gains, shifts, biases, up_bias.reshape(1, 128),
        seq_lengths, neigh_counts.reshape(1, 16), keys, neigh_ids, targets.reshape(1, 256),
        p_lm.reshape(1, 256),
    )
    small = [shape((3, 32), F32), shape((3, 32), F32), shape((4, 32), F32), shape((1, 128), F32)]
    res = pl.pallas_call(
        finish_kernel,
        out_shape=results + small,
        in_specs=[anywhere] * 7 + [vmem],
        out_specs=[vmem] * 11,
        scratch_shapes=[pltpu.SemaphoreType.DMA((7,))],
        name="finish",
    )(*held)
    state, loss, gin, gqkv, gout, gup, gdown, dgains, dshifts, dbiases, dub = res
    return (
        state, loss.reshape(256), gin, gqkv, gout, gup, gdown, dgains, dshifts, dbiases, dub.reshape(128),
    )


def solution(mesh):
    in_specs = (
        P(("dp", "fsdp"), None),
        P(("dp", "fsdp"), None),
        P(("dp", "fsdp"), None),
        P(("dp", "fsdp"), None),
        P(("dp", "fsdp"), None),
        P(("dp", "fsdp"), None),
        P(None, ("dp", "fsdp")),
        P(None, ("dp", "fsdp")),
        P(None, ("dp", "fsdp")),
        P(("dp", "fsdp")),
        P("dp", None),
        P(("dp", "fsdp"), None, None),
        P(("dp", "fsdp"), None),
        P(("dp", "fsdp")),
        P(("dp", "fsdp")),
        P(("dp", "fsdp")),
    )
    out_specs = (
        P(("dp", "fsdp"), None),
        P(("dp", "fsdp")),
        P(("dp", "fsdp"), None),
        P(("dp", "fsdp"), None),
        P(("dp", "fsdp"), None),
        P(("dp", "fsdp"), None),
        P(("dp", "fsdp"), None),
        P(None, ("dp", "fsdp")),
        P(None, ("dp", "fsdp")),
        P(None, ("dp", "fsdp")),
        P(("dp", "fsdp")),
    )
    fused = mesh.shape["dp"] == 16 and mesh.shape["fsdp"] == 2
    return jax.shard_map(
        on_device_fused if fused else on_device, mesh=mesh, in_specs=in_specs, out_specs=out_specs, check_vma=False
    )
```

```python
import functools
import math

import jax
import jax.numpy as jnp
from jax import lax
from jax.experimental import pallas as pl
from jax.experimental.pallas import tpu as pltpu
from jax.sharding import PartitionSpec as P

HEADS = 16


EPSILON = 1e-05
MIX_WEIGHT = 0.25


def norm_rows(values, gain_row, shift_row):
    center = values - jnp.mean(values, -1, keepdims=True)
    inverse = lax.rsqrt(jnp.mean(center * center, -1, keepdims=True) + EPSILON)
    unit_rows = center * inverse
    return (unit_rows * gain_row + shift_row, unit_rows, inverse)


def norm_back(grad_rows, unit_rows, inverse, gain_row):
    scaled = grad_rows * gain_row
    first_mean = jnp.mean(scaled, -1, keepdims=True)
    second_mean = jnp.mean(scaled * unit_rows, -1, keepdims=True)
    grad_values = inverse * (scaled - first_mean - unit_rows * second_mean)
    return (grad_values, jnp.sum(grad_rows * unit_rows, 0), jnp.sum(grad_rows, 0))


def contract_rows(left, right):
    return lax.dot_general(
        left, right, (((0,), (0,)), ((), ())), preferred_element_type=jnp.float32
    )


def times_transposed(left, right):
    return lax.dot_general(
        left, right, (((1,), (1,)), ((), ())), preferred_element_type=jnp.float32
    )


def segment_of(lengths, positions):
    first_end = lengths[0]
    second_end = lengths[0] + lengths[1]
    return (positions >= first_end).astype(jnp.int32) + (positions >= second_end).astype(jnp.int32)


def on_device(
    tokens,
    head_grad,
    w_qkv,
    w_out,
    w_up,
    w_down,
    gains,
    shifts,
    biases,
    up_bias,
    seq_lengths,
    neigh_keys,
    neigh_ids,
    neigh_counts,
    targets,
    p_lm,
):
    gathered = (
        lax.all_gather(w_qkv, ("dp", "fsdp"), axis=0, tiled=True),
        lax.all_gather(w_out, ("dp", "fsdp"), axis=0, tiled=True),
        lax.all_gather(w_up, ("dp", "fsdp"), axis=0, tiled=True),
        lax.all_gather(w_down, ("dp", "fsdp"), axis=0, tiled=True),
        lax.all_gather(gains, ("dp", "fsdp"), axis=1, tiled=True),
        lax.all_gather(shifts, ("dp", "fsdp"), axis=1, tiled=True),
        lax.all_gather(biases, ("dp", "fsdp"), axis=1, tiled=True),
        lax.all_gather(up_bias, ("dp", "fsdp"), axis=0, tiled=True),
    )
    row_count, feature_width = tokens.shape
    head_count = HEADS
    head_depth = feature_width // head_count
    score_scale = 1.0 / math.sqrt(head_depth)
    gain_rows = gathered[4].astype(jnp.float32)
    shift_rows = gathered[5].astype(jnp.float32)
    bias_rows = gathered[6].astype(jnp.float32)
    tokens_f32 = tokens.astype(jnp.float32)
    normed_in, unit_in, inverse_in = norm_rows(tokens_f32, gain_rows[0], shift_rows[0])
    normed_in_low = normed_in.astype(jnp.bfloat16)
    qkv_bias = jnp.concatenate([bias_rows[0], jnp.zeros_like(bias_rows[0]), bias_rows[1]])
    qkv = (
        jnp.dot(normed_in_low, gathered[0], preferred_element_type=jnp.float32) + qkv_bias
    ).astype(jnp.bfloat16)
    query_heads = qkv[:, :feature_width].reshape(row_count, head_count, head_depth)
    kv_local = qkv[:, feature_width:]
    kv_group = lax.all_gather(kv_local, "fsdp", axis=0, tiled=True)
    group_size = kv_group.shape[0]
    part_count = lax.axis_size("fsdp")
    block_rows = row_count * min(part_count, max(1, 512 // row_count))
    block_count = group_size // block_rows
    first_row = lax.axis_index("fsdp") * row_count
    last_row = first_row + row_count - 1
    lengths = seq_lengths[0]
    query_pos = first_row + jnp.arange(row_count, dtype=jnp.int32)
    query_seg = segment_of(lengths, query_pos)

    def scores_of(source, block_start):
        key_piece = lax.dynamic_slice_in_dim(source, block_start, block_rows, 0)
        key_heads = key_piece[:, :feature_width].reshape(block_rows, head_count, head_depth)
        value_heads = key_piece[:, feature_width:].reshape(block_rows, head_count, head_depth)
        key_pos = block_start + jnp.arange(block_rows, dtype=jnp.int32)
        allowed = (segment_of(lengths, key_pos)[None, :] == query_seg[:, None]) & (
            key_pos[None, :] <= query_pos[:, None]
        )
        raw_scores = (
            jnp.einsum("qhe,khe->hqk", query_heads, key_heads, preferred_element_type=jnp.float32)
            * score_scale
        )
        return (jnp.where(allowed[None], raw_scores, -jnp.inf), key_heads, value_heads)

    def keep_same(kept_value):
        return kept_value

    def stats_step(block_index, stats):
        block_start = block_index * block_rows

        def stats_block_work(pair):
            row_top, row_total = pair
            masked, key_heads, value_heads = scores_of(kv_group, block_start)
            new_top = jnp.maximum(row_top, jnp.max(masked, -1))
            safe_top = jnp.where(new_top > -jnp.inf, new_top, 0.0)
            row_total = row_total * jnp.exp(row_top - safe_top) + jnp.sum(
                jnp.exp(masked - safe_top[..., None]), -1
            )
            return (new_top, row_total)

        return lax.cond(block_start <= last_row, stats_block_work, keep_same, stats)

    start_stats = (
        jnp.full((head_count, row_count), -jnp.inf, jnp.float32),
        jnp.zeros((head_count, row_count), jnp.float32),
    )
    row_top, row_total = lax.fori_loop(0, block_count, stats_step, start_stats)
    log_total = row_top + jnp.log(row_total)

    def value_step(block_index, value_acc):
        block_start = block_index * block_rows

        def value_block_work(value_sum):
            masked, key_heads, value_heads = scores_of(kv_group, block_start)
            prob_low = jnp.exp(masked - log_total[..., None]).astype(jnp.bfloat16)
            return value_sum + jnp.einsum(
                "hqk,khe->qhe", prob_low, value_heads, preferred_element_type=jnp.float32
            )

        return lax.cond(block_start <= last_row, value_block_work, keep_same, value_acc)

    attended = lax.fori_loop(
        0, block_count, value_step, jnp.zeros((row_count, head_count, head_depth), jnp.float32)
    )
    attended = attended.reshape(row_count, feature_width)
    attended_low = attended.astype(jnp.bfloat16)
    hidden_one = tokens_f32 + (
        jnp.dot(attended_low, gathered[1], preferred_element_type=jnp.float32) + bias_rows[2]
    )
    normed_mid, unit_mid, inverse_mid = norm_rows(hidden_one, gain_rows[1], shift_rows[1])
    normed_mid_low = normed_mid.astype(jnp.bfloat16)
    pre_act = jnp.dot(normed_mid_low, gathered[2], preferred_element_type=jnp.float32) + gathered[
        7
    ].astype(jnp.float32)
    gelu_low = jax.nn.gelu(pre_act).astype(jnp.bfloat16)
    state_f32 = hidden_one + (
        jnp.dot(gelu_low, gathered[3], preferred_element_type=jnp.float32) + bias_rows[3]
    )
    query, unit_out, inverse_out = norm_rows(state_f32, gain_rows[2], shift_rows[2])
    span_count = neigh_keys.shape[0]
    slot_count = neigh_keys.shape[1]
    knn_scale = 0.5 / math.sqrt(feature_width)
    query_low = query.astype(jnp.bfloat16).reshape(span_count, -1, feature_width)
    key_square = jnp.einsum(
        "snd,snd->sn", neigh_keys, neigh_keys, preferred_element_type=jnp.float32
    )
    raw_logits = jnp.einsum(
        "sqd,snd->sqn", query_low, neigh_keys, preferred_element_type=jnp.float32
    )
    logits = (2.0 * raw_logits - key_square[:, None, :]) * knn_scale
    slot_valid = jnp.arange(slot_count, dtype=jnp.int32)[None, :] < neigh_counts[:, None]
    masked_logits = jnp.where(slot_valid[:, None, :], logits, -jnp.inf)
    exp_values = jnp.exp(masked_logits - jnp.max(masked_logits, -1, keepdims=True))
    weights = exp_values / jnp.sum(exp_values, -1, keepdims=True)
    id_match = neigh_ids[:, None, :] == targets.reshape(span_count, -1)[:, :, None]
    knn_prob = jnp.sum(jnp.where(id_match, weights, 0.0), -1)
    mixture = MIX_WEIGHT * knn_prob + (1.0 - MIX_WEIGHT) * p_lm.reshape(span_count, -1)
    token_loss = -jnp.log(mixture).reshape(row_count)
    match_f32 = jnp.where(id_match, 1.0, 0.0)
    dlogits = (
        -(MIX_WEIGHT / mixture)[..., None] * weights * (match_f32 - knn_prob[..., None])
    ).astype(jnp.bfloat16)
    knn_grad = jnp.einsum(
        "sqn,snd->sqd", dlogits, neigh_keys, preferred_element_type=jnp.float32
    ) * (2.0 * knn_scale)
    dquery = head_grad.astype(jnp.float32) + knn_grad.reshape(row_count, feature_width)
    back_params = (
        lax.all_gather(w_qkv, ("dp", "fsdp"), axis=0, tiled=True),
        lax.all_gather(w_out, ("dp", "fsdp"), axis=0, tiled=True),
        lax.all_gather(w_up, ("dp", "fsdp"), axis=0, tiled=True),
        lax.all_gather(w_down, ("dp", "fsdp"), axis=0, tiled=True),
        lax.all_gather(gains, ("dp", "fsdp"), axis=1, tiled=True),
        lax.all_gather(shifts, ("dp", "fsdp"), axis=1, tiled=True),
        lax.all_gather(biases, ("dp", "fsdp"), axis=1, tiled=True),
        lax.all_gather(up_bias, ("dp", "fsdp"), axis=0, tiled=True),
    )
    kv_back = lax.all_gather(kv_local, "fsdp", axis=0, tiled=True)
    gain_back = back_params[4].astype(jnp.float32)
    dstate, gain_grad_out, shift_grad_out = norm_back(dquery, unit_out, inverse_out, gain_back[2])
    dstate_low = dstate.astype(jnp.bfloat16)
    grad_w_down = contract_rows(gelu_low, dstate_low)
    bias_grad_down = jnp.sum(dstate_low.astype(jnp.float32), 0)
    dgelu = times_transposed(dstate_low, back_params[3])
    gelu_value, gelu_pull = jax.vjp(jax.nn.gelu, pre_act)
    dpre_low = gelu_pull(dgelu)[0].astype(jnp.bfloat16)
    grad_w_up = contract_rows(normed_mid_low, dpre_low)
    grad_up_bias = jnp.sum(dpre_low.astype(jnp.float32), 0)
    dnormed_mid = times_transposed(dpre_low, back_params[2])
    dhidden_part, gain_grad_mid, shift_grad_mid = norm_back(
        dnormed_mid, unit_mid, inverse_mid, gain_back[1]
    )
    dhidden_one = dstate + dhidden_part
    dhidden_low = dhidden_one.astype(jnp.bfloat16)
    grad_w_out = contract_rows(attended_low, dhidden_low)
    bias_grad_out = jnp.sum(dhidden_low.astype(jnp.float32), 0)
    dattended_low = times_transposed(dhidden_low, back_params[1]).astype(jnp.bfloat16)
    dattended_heads = dattended_low.reshape(row_count, head_count, head_depth)
    delta_rows = jnp.sum(
        dattended_heads.astype(jnp.float32) * attended.reshape(row_count, head_count, head_depth),
        -1,
    ).T

    def both_grad_step(block_index, grad_pair):
        block_start = block_index * block_rows

        def both_block_work(pair):
            dquery_acc, dkv_group = pair
            masked, key_heads, value_heads = scores_of(kv_back, block_start)
            prob_values = jnp.exp(masked - log_total[..., None])
            prob_low = prob_values.astype(jnp.bfloat16)
            dprob = jnp.einsum(
                "qhe,khe->hqk", dattended_heads, value_heads, preferred_element_type=jnp.float32
            )
            dscores = (prob_values * (dprob - delta_rows[..., None])).astype(jnp.bfloat16)
            dquery_acc = dquery_acc + jnp.einsum(
                "hqk,khe->qhe", dscores, key_heads, preferred_element_type=jnp.float32
            )
            dkey_heads = (
                jnp.einsum("hqk,qhe->khe", dscores, query_heads, preferred_element_type=jnp.float32)
                * score_scale
            )
            dvalue_heads = jnp.einsum(
                "hqk,qhe->khe", prob_low, dattended_heads, preferred_element_type=jnp.float32
            )
            block_grad = jnp.concatenate(
                [
                    dkey_heads.reshape(block_rows, feature_width),
                    dvalue_heads.reshape(block_rows, feature_width),
                ],
                1,
            )
            current = lax.dynamic_slice_in_dim(dkv_group, block_start, block_rows, 0)
            return (
                dquery_acc,
                lax.dynamic_update_slice_in_dim(dkv_group, current + block_grad, block_start, 0),
            )

        return lax.cond(block_start <= last_row, both_block_work, keep_same, grad_pair)

    zero_dquery = jnp.zeros((row_count, head_count, head_depth), jnp.float32)
    start_grads = (zero_dquery, jnp.zeros((group_size, 2 * feature_width), jnp.float32))
    dquery_acc, dkv_group = lax.fori_loop(0, block_count, both_grad_step, start_grads)
    dkv_mine = lax.psum_scatter(
        dkv_group.astype(jnp.bfloat16), "fsdp", scatter_dimension=0, tiled=True
    ).astype(jnp.float32)
    dqkv_low = jnp.concatenate(
        [(dquery_acc * score_scale).reshape(row_count, feature_width), dkv_mine], 1
    ).astype(jnp.bfloat16)
    grad_w_qkv = contract_rows(normed_in_low, dqkv_low)
    column_sums = jnp.sum(dqkv_low.astype(jnp.float32), 0)
    dnormed_in = times_transposed(dqkv_low, back_params[0])
    dinput_part, gain_grad_in, shift_grad_in = norm_back(
        dnormed_in, unit_in, inverse_in, gain_back[0]
    )
    grad_input = (dhidden_one + dinput_part).astype(jnp.bfloat16)
    grad_gains = jnp.stack([gain_grad_in, gain_grad_mid, gain_grad_out])
    grad_shifts = jnp.stack([shift_grad_in, shift_grad_mid, shift_grad_out])
    grad_biases = jnp.stack(
        [
            column_sums[:feature_width],
            column_sums[2 * feature_width :],
            bias_grad_out,
            bias_grad_down,
        ]
    )
    summed = (
        lax.psum_scatter(grad_w_qkv, ("dp", "fsdp"), scatter_dimension=0, tiled=True),
        lax.psum_scatter(grad_w_out, ("dp", "fsdp"), scatter_dimension=0, tiled=True),
        lax.psum_scatter(grad_w_up, ("dp", "fsdp"), scatter_dimension=0, tiled=True),
        lax.psum_scatter(grad_w_down, ("dp", "fsdp"), scatter_dimension=0, tiled=True),
        lax.psum_scatter(grad_gains, ("dp", "fsdp"), scatter_dimension=1, tiled=True),
        lax.psum_scatter(grad_shifts, ("dp", "fsdp"), scatter_dimension=1, tiled=True),
        lax.psum_scatter(grad_biases, ("dp", "fsdp"), scatter_dimension=1, tiled=True),
        lax.psum_scatter(grad_up_bias, ("dp", "fsdp"), scatter_dimension=0, tiled=True),
    )
    return (
        state_f32.astype(jnp.bfloat16),
        token_loss,
        grad_input,
        summed[0],
        summed[1],
        summed[2],
        summed[3],
        summed[4],
        summed[5],
        summed[6],
        summed[7],
    )


VMEM_LIMIT = 63 << 20
KNN_SCALE = 0.5 / 32.0
BF = jnp.bfloat16
F32 = jnp.float32
MESH = pl.DeviceIdType.MESH
NEG = -1e30


def dot(left, right, left_dim=1, right_dim=0):
    return lax.dot_general(
        left, right, (((left_dim,), (right_dim,)), ((), ())), preferred_element_type=F32
    )


def unit_of(values):
    center = values - jnp.mean(values, -1, keepdims=True)
    inverse = lax.rsqrt(jnp.mean(center * center, -1, keepdims=True) + EPSILON)
    return center * inverse, inverse


def ln_back(grad_rows, unit_rows, inverse, gain_row):
    scaled = grad_rows * gain_row
    first_mean = jnp.mean(scaled, -1, keepdims=True)
    second_mean = jnp.mean(scaled * unit_rows, -1, keepdims=True)
    return inverse * (scaled - first_mean - unit_rows * second_mean)


def col_sum(values):
    return jnp.sum(values, 0, keepdims=True)


def gelu_pair(u):
    k0 = math.sqrt(2.0 / math.pi)
    square = u * u
    t = jnp.tanh(u * (k0 + (k0 * 0.044715) * square))
    half = 0.5 * (1.0 + t)
    slope = half + (0.5 * u) * (1.0 - t * t) * (k0 + (3.0 * k0 * 0.044715) * square)
    return u * half, slope


GATHER_X_FIRST = (7, 4)
REDUCE_Z_FIRST = (0, 7, 4)
DOWN = {7: (0, 1), 13: (1, 1), 8: (2, 2), 9: (4, 2), 10: (6, 2)}

(
    DO_Y0, DO_Z, DO_F, DO_X, DO_Y, DO_C, DO_TOK, DO_MASK, DO_COLS, DO_TABLE, DO_UNPACK, DO_NORMOWN,
    DO_NORMOTHER, DO_PROJ, DO_ATTEND, DO_ATTOUT, DO_NORMMID, DO_UP, DO_DOWN, DO_KNN, DO_STATEOUT,
    DO_DSREST, DO_RC, DO_RY, DO_RX, DO_RF, DO_RZ, DO_GD, DO_DP, DO_GU, DO_DNO, DO_DNS, DO_BACKMID,
    DO_DAO, DO_GO, DO_AB, DO_GQ, DO_DIO, DO_DIS, DO_BIO, DO_BIS, DO_GIN, DO_GP,
) = range(43)
ORDER = (
    (DO_Y0, 0), (DO_Y0, 4), (DO_Y0, 1), (DO_Z, 12), (DO_Z, 11), (DO_Y0, 5), (DO_Y0, 2), (DO_TOK,),
    (DO_Y0, 3), (DO_Y0, 6), (DO_MASK,), (DO_COLS,), (DO_TABLE, 2), (DO_TABLE, 1), (DO_Z, 0), (DO_TABLE,
    0), (DO_F, 12), (DO_Z, 1), (DO_TABLE, 3), (DO_Z, 2), (DO_Z, 5), (DO_X, 12), (DO_F, 11), (DO_X, 11),
    (DO_Y, 12), (DO_F, 0), (DO_X, 0), (DO_Y, 11), (DO_F, 1), (DO_Z, 3), (DO_Z, 6), (DO_C, 12), (DO_X,
    1), (DO_Z, 4), (DO_C, 0), (DO_F, 2), (DO_UNPACK,), (DO_NORMOTHER,), (DO_NORMOWN,), (DO_PROJ, 0, 0),
    (DO_PROJ, 0, 1), (DO_X, 2), (DO_Z, 8), (DO_F, 5), (DO_C, 1), (DO_X, 5), (DO_Z, 9), (DO_F, 3),
    (DO_PROJ, 1, 0), (DO_PROJ, 1, 1), (DO_C, 11), (DO_X, 3), (DO_Z, 7), (DO_C, 2), (DO_F, 6), (DO_F, 4),
    (DO_PROJ, 2, 0), (DO_PROJ, 2, 1), (DO_ATTEND, 0), (DO_X, 6), (DO_ATTEND, 3), (DO_C, 5), (DO_Z, 10),
    (DO_ATTEND, 2), (DO_F, 8), (DO_ATTEND, 1), (DO_F, 9), (DO_C, 3), (DO_F, 7), (DO_C, 6), (DO_X, 4),
    (DO_Z, 13), (DO_X, 8), (DO_X, 9), (DO_ATTOUT, 0), (DO_NORMMID, 0), (DO_UP, 0, 0), (DO_UP, 3, 0),
    (DO_UP, 2, 0), (DO_ATTOUT, 1), (DO_F, 10), (DO_C, 4), (DO_NORMMID, 1), (DO_UP, 2, 1), (DO_UP, 0, 1),
    (DO_C, 8), (DO_UP, 3, 1), (DO_UP, 1, 0), (DO_UP, 1, 1), (DO_X, 7), (DO_X, 10), (DO_C, 9), (DO_DOWN,
    8), (DO_F, 13), (DO_DOWN, 9), (DO_C, 7), (DO_X, 13), (DO_C, 10), (DO_DOWN, 7), (DO_C, 13), (DO_DOWN,
    10), (DO_DOWN, 13), (DO_KNN, 0), (DO_KNN, 1), (DO_DSREST,), (DO_DP, 1, 0), (DO_DP, 0, 0), (DO_DP, 3,
    0), (DO_DP, 2, 0), (DO_STATEOUT,), (DO_GD, 7), (DO_GD, 13), (DO_RC, 7), (DO_RC, 13), (DO_GD, 8),
    (DO_RF, 7), (DO_GD, 9), (DO_RC, 8), (DO_RX, 13), (DO_DP, 2, 1), (DO_DP, 3, 1), (DO_RC, 9), (DO_RF,
    13), (DO_RX, 7), (DO_DP, 1, 1), (DO_GD, 10), (DO_DP, 0, 1), (DO_DNO, 3), (DO_DNS, 2), (DO_GU, 0),
    (DO_GU, 1), (DO_DNO, 2), (DO_RX, 8), (DO_DNO, 0), (DO_DNO, 1), (DO_BACKMID, 1), (DO_DNS, 0),
    (DO_DNS, 1), (DO_RC, 4), (DO_RC, 3), (DO_RF, 8), (DO_GU, 2), (DO_GU, 3), (DO_RX, 9), (DO_DNS, 3),
    (DO_RZ, 7), (DO_BACKMID, 0), (DO_DAO, 1), (DO_DAO, 0), (DO_DAO, 3), (DO_DAO, 2), (DO_RC, 5), (DO_RC,
    6), (DO_RC, 10), (DO_RF, 9), (DO_GO,), (DO_RF, 4), (DO_RZ, 13), (DO_RX, 3), (DO_RZ, 8), (DO_AB, 1),
    (DO_RC, 11), (DO_RF, 3), (DO_AB, 0), (DO_RX, 5), (DO_RZ, 9), (DO_RX, 4), (DO_AB, 3), (DO_RF, 5),
    (DO_RX, 6), (DO_AB, 2), (DO_RZ, 3), (DO_RF, 6), (DO_GQ, 0), (DO_DIO,), (DO_RZ, 5), (DO_RX, 10),
    (DO_BIO, 0), (DO_RC, 0), (DO_RZ, 4), (DO_GQ, 1), (DO_GQ, 2), (DO_RY, 11), (DO_RF, 10), (DO_RZ, 6),
    (DO_BIO, 1), (DO_DIS,), (DO_BIS, 1), (DO_RF, 0), (DO_RC, 2), (DO_RC, 1), (DO_BIS, 0), (DO_GP,),
    (DO_RC, 12), (DO_RX, 11), (DO_GIN, 0), (DO_RZ, 10), (DO_RF, 11), (DO_RX, 0), (DO_RX, 2), (DO_RF, 2),
    (DO_RZ, 11), (DO_GIN, 1), (DO_RY, 12), (DO_RX, 1), (DO_RZ, 0), (DO_RX, 12), (DO_RZ, 2), (DO_RF, 1),
    (DO_RF, 12), (DO_RZ, 1), (DO_RZ, 12),
)


def block_kernel(
    tokens, head_grad, w_qkv, w_out, w_up, w_down, gains, shifts, biases, up_bias, seq, counts, keys_in,
    ids, targets, p_lm, state_out, loss_out, gin_out, gqkv_out, gout_out, gup_out, gdown_out, gpk_out,
    wA, wD, wO, pk, prm, ubias, tokg, ni, qkv, mask, att, h1, nmg, gelu, slope, st, prec, hgrad, ksq,
    match, dsg, tcol, pcol, lcol, lossb, dh, dhl, das, dattg, dnr2, sendb, gA, gD, gO, gP, dRA, xRA,
    zRA, dRD, xRD, zRD, dRO, yRO, xRO, zRO, dRP, yRP, xRP, zRP, finA, finD, finO, finP, xOA, xOD, pg,
    dub, lsem, ysend, yrecv, zsend, zrecv, xsend, xrecv, csend, crecv, osem, msend, mrecv, asend, arecv,
    dsend, drecv, psend, precv, rcs, rcr, rxs, rxr, rzs, rzr, rys, ryr, rfl, kn_sem,
):
    dp = lax.axis_index("dp")
    y = lax.axis_index("fsdp")
    z = dp // 4
    x = (dp // 2) % 2
    c = dp % 2
    oy = 1 - y
    ox = 1 - x
    oc = 1 - c

    def dev(zz, xx, cc, yy):
        return ((zz * 2 + xx) * 2 + cc, yy)

    z_to = [None] + [(z + j) % 4 for j in (1, 2, 3)]
    z_of = [z] + [(z - j) % 4 for j in (1, 2, 3)]
    zdev = [None] + [dev(zz, x, c, y) for zz in z_to[1:]]
    xdev = dev(z, ox, c, y)
    ydev = dev(z, x, c, oy)
    cdev = dev(z, x, oc, y)
    middle = (z == 1) | (z == 2)
    z_direct = {1: z != 3, 2: None, 3: z != 0}

    def when(cond, fn):
        if cond is None:
            fn()
        else:
            pl.when(cond)(fn)

    def rc(src, dst_ref, ss, rs, to):
        return pltpu.make_async_remote_copy(
            src_ref=src, dst_ref=dst_ref, send_sem=ss, recv_sem=rs, device_id=to, device_id_type=MESH
        )

    def lc(src, dst_ref, sem):
        return pltpu.make_async_copy(src, dst_ref, sem)

    pending = []
    finals = []
    late_recv = []
    tasks = {}

    def task(fn, name, *args):
        tasks[name] = functools.partial(fn, *args)

    def send(cp, cond=None):
        when(cond, cp.start)
        pending.append((cond, cp))

    my_rows = pl.ds(pl.multiple_of(y * 32, 32), 32)

    def up_cols(j, i, yy):
        return pl.ds(pl.multiple_of((8 * j + 2 * i + yy) * 128, 128), 128)

    def part_cols(part, yy):
        return pl.ds(pl.multiple_of(part * 1024 + yy * 512, 512), 512)

    for s in range(3):
        lc(w_qkv.at[:, part_cols(s, y)], wA.at[s, z, x, c, my_rows], lsem.at[s]).start()
    lc(w_out, wO.at[z, x, c, y], lsem.at[11]).start()
    lc(tokens, tokg.at[y], lsem.at[14]).start()
    for j in range(4):
        for i in range(4):
            lc(w_up.at[:, up_cols(j, i, y)], wA.at[3 + j, z, x, c, my_rows, pl.ds(i * 128, 128)],
               lsem.at[3 + j]).start()
    for t, (first, count) in DOWN.items():
        for h in range(first, first + count):
            lc(w_down.at[:, pl.ds(h * 128, 128)], wD.at[h, z, x, c], lsem.at[t]).start()
    for h in range(8):
        lc(keys_in.at[:, :, :, :, pl.ds(h * 128, 128)], gD.at[h], kn_sem.at[0]).start()
    lc(head_grad, hgrad, kn_sem.at[1]).start()

    quarter = (2 * dp + y) % 4
    pg[...] = jnp.zeros_like(pg)
    pg[0:3, 0:32] = gains[...].astype(F32)
    pg[3:6, 0:32] = shifts[...].astype(F32)
    pg[6:10, 0:32] = biases[...].astype(F32)
    small = pltpu.roll(pg[:, 0:128], quarter * 32, 1)
    pg[10:11, 0:128] = up_bias[...].astype(F32)
    row_id = lax.broadcasted_iota(jnp.int32, (16, 128), 0)
    pk[z, x, c, y] = jnp.where(row_id == 10, pg[:, 0:128], small).astype(BF)

    barrier = pltpu.get_barrier_semaphore()
    for to in (*zdev[1:], xdev, ydev, cdev):
        pl.semaphore_signal(barrier, inc=1, device_id=to, device_id_type=MESH)
    pl.semaphore_wait(barrier, 6)

    def weight(t, *index):
        if t < 7:
            return wA.at[(t, *index)]
        if t in DOWN:
            return wD.at[(pl.ds(*DOWN[t]), *index)]
        return (wO if t == 11 else pk).at[index]

    def z_view(t, zz):
        return weight(t, zz, x, c, y) if t in (11, 12) else weight(t, zz, x, c)

    def y_view(t):
        return wO.at[:, :, c, y] if t == 11 else pk.at[:, :, c, y]

    def c_view(t):
        return weight(t, slice(None), slice(None), c)

    def y0_full(t):
        view = wA.at[t, z, x, c, my_rows]
        return rc(view, view, ysend.at[t], yrecv.at[t], ydev)

    def start_y0(t):
        if t < 3:
            rc(w_qkv.at[:, part_cols(t, oy)], wA.at[t, z, x, c, my_rows], ysend.at[t], yrecv.at[t], ydev).start()
        else:
            for i in range(4):
                rc(w_up.at[:, up_cols(t - 3, i, oy)], wA.at[t, z, x, c, my_rows, pl.ds(i * 128, 128)],
                   ysend.at[t], yrecv.at[t], ydev).start()
        pending.append((None, y0_full(t)))

    def x_copy(t, j):
        view = z_view(t, z_of[j])
        return rc(view, view, xsend.at[t, j], xrecv.at[t, j], xdev)

    def pair_view(t, zz):
        return weight(t, zz, slice(None), c)

    def z_copy(t, j):
        view = pair_view(t, z) if t in GATHER_X_FIRST else z_view(t, z)
        return rc(view, view, zsend.at[t, j], zrecv.at[t, j], zdev[j])

    far = jnp.where(z == 1, 0, 3)
    far_sem = jnp.where(z == 1, 1, 3)

    def start_z(t):
        if t != 12:
            view = wA.at[t, z, x, c, my_rows] if t < 7 else z_view(t, z)
            lc(view, view, lsem.at[t]).wait()
        if t < 7:
            y0_full(t).wait_recv()
        if t not in GATHER_X_FIRST:
            for j in (2, 1, 3):
                send(z_copy(t, j), z_direct[j])
        send(x_copy(t, 0))

    def to_far(t, view):
        send(rc(view, view, zsend.at[t, 0], zrecv.at[t, far_sem], dev(far, x, c, y)), middle)

    def forward(t):
        if t in GATHER_X_FIRST:
            x_copy(t, 0).wait_recv()
            for j in (2, 1, 3):
                send(z_copy(t, j), z_direct[j])
        else:
            z_copy(t, 2).wait_recv()
            to_far(t, z_view(t, z_of[2]))
            send(x_copy(t, 2))

    def start_x(t):
        if t in GATHER_X_FIRST:
            z_copy(t, 2).wait_recv()
            to_far(t, pair_view(t, z_of[2]))
        else:
            for j in (1, 3):
                z_copy(t, j).wait_recv()
                send(x_copy(t, j))

    def x_done(t):
        if t in GATHER_X_FIRST:
            for j in (1, 3):
                z_copy(t, j).wait_recv()
        else:
            for j in range(4):
                x_copy(t, j).wait_recv()

    def y_copy(t):
        return rc(y_view(t), y_view(t), ysend.at[t - 4], yrecv.at[t - 4], ydev)

    def start_y(t):
        x_done(t)
        send(y_copy(t))

    def c_copy(t):
        return rc(c_view(t), c_view(t), csend.at[t], crecv.at[t], cdev)

    def start_c(t):
        if t not in (11, 12):
            x_done(t)
        else:
            y_copy(t).wait_recv()
        send(c_copy(t))

    def ready(t):
        c_copy(t).wait_recv()

    for t in range(14):
        if t < 7:
            task(start_y0, (DO_Y0, t), t)
        task(start_z, (DO_Z, t), t)
        task(forward, (DO_F, t), t)
        task(start_x, (DO_X, t), t)
        if t in (11, 12):
            task(start_y, (DO_Y, t), t)
        task(start_c, (DO_C, t), t)

    tok_copy = rc(tokens, tokg.at[y], msend.at[0], mrecv.at[0], ydev)
    task(send, (DO_TOK,), tok_copy)

    first_end = seq[0, 0]
    second_end = first_end + seq[0, 1]

    def segment(pos):
        return (pos >= first_end).astype(jnp.int32) + (pos >= second_end).astype(jnp.int32)

    def mask_rows(i, _):
        rows = pl.ds(pl.multiple_of(i * 128, 128), 128)
        qpos = i * 128 + lax.broadcasted_iota(jnp.int32, (128, 512), 0)
        kpos = lax.broadcasted_iota(jnp.int32, (128, 512), 1)
        good = (segment(qpos) == segment(kpos)) & (kpos <= qpos)
        mask[rows, :] = jnp.where(good, 0.0, NEG).astype(BF)
        return 0

    def make_mask():
        lax.fori_loop(0, 4, mask_rows, 0)

    task(make_mask, (DO_MASK,))

    def make_columns():
        wide = jnp.concatenate([targets[...].astype(F32), p_lm[...], jnp.zeros((6, 256), F32)], 0)
        cols = jnp.transpose(wide)
        tcol[...] = cols[:, 0:1]
        pcol[...] = cols[:, 1:2]
        lc(gD, gD, kn_sem.at[0]).wait()
        lc(head_grad, hgrad, kn_sem.at[1]).wait()

    task(make_columns, (DO_COLS,))

    def keys_of(s):
        return jnp.concatenate([gD[h, s // 4, (s // 2) % 2, s % 2] for h in range(8)], 1)

    def make_table(b):
        eye = lax.broadcasted_iota(jnp.int32, (128, 128), 0) == lax.broadcasted_iota(jnp.int32, (128, 128), 1)
        slot = lax.broadcasted_iota(jnp.int32, (16, 128), 1)
        for s in range(b * 4, b * 4 + 4):
            rows = slice(s * 16, s * 16 + 16)
            kk = keys_of(s)
            square = jnp.broadcast_to(col_sum(jnp.where(eye, dot(kk, kk, 1, 1), 0.0)), (16, 128))
            ksq[rows, :] = jnp.where(slot < counts[0, s], square * -KNN_SCALE, NEG)
            match[rows, :] = jnp.where(ids[s : s + 1, :].astype(F32) == tcol[rows, :], 1.0, 0.0)

    for b in range(4):
        task(make_table, (DO_TABLE, b), b)

    def unpack():
        ready(12)
        for g in range(8):
            total = None
            for i in range(4):
                piece = pk[g // 2, g % 2, i // 2, i % 2].astype(F32)
                total = piece if total is None else total + piece
            prm[:, g * 128 : (g + 1) * 128] = total
        for d in range(16):
            piece = pk[d // 4, (d // 2) % 2, d % 2, y].astype(F32)
            ubias[0:1, d * 128 : (d + 1) * 128] = piece[10:11, :]

    task(unpack, (DO_UNPACK,))

    def row(r):
        return prm[r : r + 1, :]

    def norm_in(half):
        def rows_of(i, _):
            rows = pl.ds(pl.multiple_of(i * 64, 64), 64)
            unit, _inv = unit_of(tokg[half, rows, :].astype(F32))
            ni[half, rows, :] = (unit * row(0) + row(3)).astype(BF)
            return 0

        lax.fori_loop(0, 4, rows_of, 0)

    def norm_own():
        lc(tokens, tokg.at[y], lsem.at[14]).wait()
        norm_in(y)

    def norm_other():
        tok_copy.wait_recv()
        norm_in(oy)

    task(norm_own, (DO_NORMOWN,))
    task(norm_other, (DO_NORMOTHER,))

    head_cols = pl.ds(pl.multiple_of(y * 512, 512), 512)

    def project(s, own):
        if own:
            ready(s)
        half = y if own else oy
        value = dot(ni[half], wA[s].reshape(1024, 512))
        if s != 1:
            value = value + prm[6 + s // 2 : 7 + s // 2, head_cols]
        qkv[s, half] = value.astype(BF)

    for s in range(3):
        task(project, (DO_PROJ, s, 0), s, True)
        task(project, (DO_PROJ, s, 1), s, False)

    lane = lax.broadcasted_iota(jnp.int32, (1, 128), 1)
    in_head = [lane < 64, lane >= 64]

    def probs_of(qe, k2, half):
        nk = 256 * (half + 1)
        s = dot(qe, k2[:nk], 1, 1) * 0.125 + mask[half * 256 : half * 256 + 256, :nk].astype(F32)
        ex = jnp.exp(s - jnp.max(s, -1, keepdims=True))
        return ex * (1.0 / jnp.sum(ex, -1, keepdims=True))

    def attend(p):
        cols = slice(p * 128, p * 128 + 128)
        q2 = qkv[0, :, :, cols]
        k2 = qkv[1, :, :, cols].reshape(512, 128)
        v2 = qkv[2, :, :, cols].reshape(512, 128)
        for half in range(2):
            nk = 256 * (half + 1)
            outs = []
            for e in range(2):
                qe = jnp.where(in_head[e], q2[half], jnp.zeros_like(q2[half]))
                outs.append(dot(probs_of(qe, k2, half).astype(BF), v2[:nk]))
            att[half, :, pair_cols(p)] = jnp.where(in_head[0], outs[0], outs[1]).astype(BF)
        send(att_copy(p))

    def pair_cols(p):
        return pl.ds(pl.multiple_of(y * 512 + p * 128, 128), 128)

    def att_copy(p):
        view = att.at[:, :, pair_cols(p)]
        return rc(view, view, asend.at[p], arecv.at[p], ydev)

    for p in range(4):
        task(attend, (DO_ATTEND, p), p)

    def attention_out(half):
        if half == 0:
            for p in range(4):
                att_copy(p).wait_recv()
            ready(11)
        h1[half] = dot(att[half], wO[...].reshape(1024, 1024)) + row(8)

    def norm_mid(half):
        def rows_of(k, _):
            rows = pl.ds(pl.multiple_of(k * 64, 64), 64)
            value = h1[half, rows, :] + tokg[half, rows, :].astype(F32)
            h1[half, rows, :] = value
            unit, _inv = unit_of(value)
            nmg[half, rows, :] = (unit * row(1) + row(4)).astype(BF)
            return 0

        lax.fori_loop(0, 4, rows_of, 0)

    for half in range(2):
        task(attention_out, (DO_ATTOUT, half), half)
        task(norm_mid, (DO_NORMMID, half), half)

    def up(j, half):
        if half == 0:
            ready(3 + j)
        cols = slice(j * 512, (j + 1) * 512)
        u = dot(nmg[half], wA[3 + j].reshape(1024, 512)) + ubias[0:1, cols]
        value, dvalue = gelu_pair(u)
        gelu[half, :, cols] = value.astype(BF)
        slope[half, :, cols] = dvalue.astype(BF)

    for j in range(4):
        task(up, (DO_UP, j, 0), j, 0)
        task(up, (DO_UP, j, 1), j, 1)

    def part_copy(t):
        cols = pl.ds(DOWN[t][0] * 128, DOWN[t][1] * 128)
        sem = list(DOWN).index(t)
        return rc(sendb.at[:, cols], prec.at[:, cols], psend.at[sem], precv.at[sem], ydev)

    def down_weight(first, count):
        return jnp.concatenate([wD[h].reshape(2048, 128) for h in range(first, first + count)], 1)

    def down(t):
        ready(t)
        first, count = DOWN[t]
        cols = slice(first * 128, (first + count) * 128)
        right = down_weight(first, count)
        sendb[:, cols] = dot(gelu[oy], right).astype(BF)
        send(part_copy(t))
        st[:, cols] = dot(gelu[y], right) + (h1[y, :, cols] + prm[9:10, cols])

    for t in DOWN:
        task(down, (DO_DOWN, t), t)

    def add_row(r, value):
        pg[r : r + 1, :] = pg[r : r + 1, :] + value

    def ds_copy(j, b):
        rows = pl.ds(b * 128, 128) if j < 2 else pl.ds(0, 256)
        cols = pl.ds(j * 128, 128) if j < 2 else pl.ds((j - 1) * 256, 256)
        view = dsg.at[y, rows, cols]
        sem = 2 * j + b if j < 2 else 2 + j
        return rc(view, view, dsend.at[sem], drecv.at[sem], ydev)

    ds_waited = []

    def need_ds(*columns):
        for j in columns:
            if j not in ds_waited:
                ds_waited.append(j)
                for b in range(2 if j < 2 else 1):
                    ds_copy(j, b).wait_recv()

    def neighbours(b):
        if b == 0:
            pg[...] = jnp.zeros_like(pg)
            for t in DOWN:
                part_copy(t).wait_recv()
        rows = slice(b * 128, b * 128 + 128)
        value = st[rows, :] + prec[rows, :].astype(F32)
        unit, inv = unit_of(value)
        query = (unit * row(2) + row(5)).astype(BF)
        raw = jnp.concatenate(
            [dot(query[i * 16 : i * 16 + 16], keys_of(b * 8 + i), 1, 1) for i in range(8)], 0
        )
        logits = (2.0 * KNN_SCALE) * raw + ksq[rows, :]
        ex = jnp.exp(logits - jnp.max(logits, -1, keepdims=True))
        weights = ex / jnp.sum(ex, -1, keepdims=True)
        same = match[rows, :]
        knn_prob = jnp.sum(same * weights, -1, keepdims=True)
        mixture = MIX_WEIGHT * knn_prob + (1.0 - MIX_WEIGHT) * pcol[rows, :]
        lcol[rows, :] = -jnp.log(mixture)
        dlog = (-(MIX_WEIGHT / mixture) * weights * (same - knn_prob)).astype(BF)
        kgrad = jnp.concatenate(
            [dot(dlog[i * 16 : i * 16 + 16], keys_of(b * 8 + i)) for i in range(8)], 0
        )
        dquery = hgrad[rows, :].astype(F32) + kgrad * (2.0 * KNN_SCALE)
        hgrad[rows, :] = value.astype(BF)
        add_row(2, col_sum(dquery * unit))
        add_row(5, col_sum(dquery))
        dvalue = ln_back(dquery, unit, inv, row(2))
        st[rows, :] = dvalue
        low = dvalue.astype(BF)
        add_row(9, col_sum(low.astype(F32)))
        dsg[y, rows, :] = low
        send(ds_copy(0, b))
        send(ds_copy(1, b))

    for b in range(2):
        task(neighbours, (DO_KNN, b), b)

    out_state = lc(hgrad, state_out, osem.at[0])

    def state_done():
        out_state.start()
        lossb[...] = jnp.transpose(jnp.broadcast_to(lcol[...], (256, 128)))[0:1, :]
        cp = lc(lossb, loss_out, osem.at[1])
        cp.start()
        finals.append(cp)

    task(state_done, (DO_STATEOUT,))

    def ds_rest():
        send(ds_copy(2, 0))
        send(ds_copy(3, 0))
        send(ds_copy(4, 0))

    task(ds_rest, (DO_DSREST,))

    slot_of = {3: 0, 4: 1, 5: 2, 6: 3, 0: 0, 1: 1, 2: 2}

    every = slice(None)

    def pick(refs, t, *index):
        if t < 7:
            return refs[0].at[(slot_of[t] if refs[0] is gA else t, *index)]
        if t in DOWN:
            return refs[1].at[(pl.ds(*DOWN[t]), *index)]
        return refs[2 if t == 11 else 3].at[index]

    g_refs = (gA, gD, gO, gP)
    c_refs = (dRA, dRD, dRO, dRP)
    y_refs = (None, None, yRO, yRP)
    x_refs = (xRA, xRD, xRO, xRP)
    z_refs = (zRA, zRD, zRO, zRP)

    def g_at(t, zz, xx):
        return pick(g_refs, t, zz, xx, c, y) if t in (11, 12) else pick(g_refs, t, zz, xx, c)

    def rs_c(t):
        return rc(pick(g_refs, t, every, every, oc), pick(c_refs, t, every), rcs.at[t], rcr.at[t], cdev)

    def rs_y(t):
        return rc(pick(g_refs, t, every, every, c, oy), pick(y_refs, t, every), rys.at[t], ryr.at[t], ydev)

    def x_one(t):
        k = REDUCE_Z_FIRST.index(t)
        return xOA.at[k] if t < 7 else xOD.at[k, pl.ds(0, DOWN[t][1])]

    def rs_x(t):
        if t in REDUCE_Z_FIRST:
            return rc(g_at(t, z, ox), x_one(t), rxs.at[t], rxr.at[t], xdev)
        return rc(g_at(t, every, ox), pick(x_refs, t, every), rxs.at[t], rxr.at[t], xdev)

    def z_block(t, zz):
        return g_at(t, zz, every if t in REDUCE_Z_FIRST else x)

    def z_slot(t, j):
        if t in REDUCE_Z_FIRST:
            return pick((x_refs, z_refs)[j // 2], t, pl.ds(2 * (j % 2), 2))
        return pick(z_refs, t, j)

    def rs_z(t, j):
        return rc(z_block(t, z_to[j]), z_slot(t, j), rzs.at[t, j], rzr.at[t, j], zdev[j])

    end_block = jnp.where(z == 0, 3, 0)
    end_to = dev(jnp.where(z == 0, 1, 2), x, c, y)
    is_end = (z == 0) | (z == 3)

    def rs_end(t):
        return rc(z_block(t, end_block), z_slot(t, 0), rzs.at[t, 0], rzr.at[t, 0], end_to)

    def add_to(ref, other):
        ref[...] = (ref[...].astype(F32) + other.astype(F32)).astype(ref.dtype)

    def rs_after_c(t):
        rs_c(t).wait_recv()
        for i in range(4):
            add_to(pick(g_refs, t, i, every, c), pick(c_refs, t, i)[...])
        if t in REDUCE_Z_FIRST:
            start_zs(t)
        else:
            (rs_y(t) if t in (11, 12) else rs_x(t)).start()

    def rs_after_y(t):
        rs_y(t).wait_recv()
        for i in range(4):
            add_to(pick(g_refs, t, i, every, c, y), pick(y_refs, t, i)[...])
        rs_x(t).start()

    def start_zs(t):
        when(is_end, rs_end(t).start)
        when(z_direct[1], rs_z(t, 1).start)
        when(z_direct[3], rs_z(t, 3).start)
        when(is_end, rs_z(t, 2).start)

    def z_arrived(t):
        rs_z(t, 2).wait_recv()
        pl.when(z != 0)(rs_z(t, 1).wait_recv)
        pl.when(z != 3)(rs_z(t, 3).wait_recv)

    def rs_after_x(t):
        if t in REDUCE_Z_FIRST:
            z_arrived(t)

            def add(*slots):
                total = g_at(t, z, every)[...].astype(F32)
                for j in slots:
                    total = total + z_slot(t, j)[...].astype(F32)
                g_at(t, z, every)[...] = total.astype(BF)

            pl.when(z == 0)(functools.partial(add, 2, 3))
            pl.when(z == 3)(functools.partial(add, 2, 1))
            pl.when(middle)(functools.partial(add, 2, 1, 3))
            rs_x(t).start()
        else:
            rs_x(t).wait_recv()
            for i in range(4):
                add_to(g_at(t, i, x), pick(x_refs, t, i)[...])
            start_zs(t)

    def rs_forward(t):
        def go():
            rs_end(t).wait_recv()
            add_to(z_block(t, z_to[2]), z_slot(t, 0)[...])
            rs_z(t, 2).start()

        pl.when(middle)(go)

    def rs_sends(t):
        out = [(None, rs_c(t)), (None, rs_x(t)), (None, rs_z(t, 2))]
        if t in (11, 12):
            out.append((None, rs_y(t)))
        return out + [(z_direct[1], rs_z(t, 1)), (z_direct[3], rs_z(t, 3)), (is_end, rs_end(t))]

    def out_cols(t, yy):
        if t < 3:
            return [(gqkv_out, part_cols(t, yy), pl.ds(0, 512))]
        return [(gup_out, up_cols(t - 3, i, yy), pl.ds(i * 128, 128)) for i in range(4)]

    def rs_finish(t):
        if t < 7:
            fin = finA.at[t]
        elif t in DOWN:
            fin = finD.at[pl.ds(*DOWN[t])]
        else:
            fin = finO if t == 11 else finP
        own = g_at(t, z, x)
        if t in REDUCE_Z_FIRST:
            rs_x(t).wait_recv()
            total = own[...].astype(F32) + x_one(t)[...].astype(F32)
            fin[...] = total.reshape(fin.shape)
        else:
            z_arrived(t)
            near = jnp.where(z == 0, 3, 1)
            total = own[...].astype(F32)
            for j in (2, near):
                total = total + pick(z_refs, t, j)[...].astype(F32)
            fin[...] = total.reshape(fin.shape)

            def third():
                fin[...] = fin[...] + pick(z_refs, t, 3)[...].astype(F32).reshape(fin.shape)

            pl.when(middle)(third)
        if t not in (3, 4, 5):
            pending.extend(rs_sends(t))
        if t < 7:
            for ref, cols, inner in out_cols(t, y):
                lc(finA.at[t, y, :, inner], ref.at[:, cols], rfl.at[t]).start()
                rc(finA.at[t, oy, :, inner], ref.at[:, cols], rys.at[t], ryr.at[t], ydev).start()
            full = finA.at[t, y]
            finals.append(lc(full, full, rfl.at[t]))
            both = rc(full, full, rys.at[t], ryr.at[t], ydev)
            pending.append((None, both))
            late_recv.append(both)
        else:
            if t in DOWN:
                for h in range(DOWN[t][0], sum(DOWN[t])):
                    lc(finD.at[h], gdown_out.at[:, pl.ds(h * 128, 128)], rfl.at[t]).start()
                finals.append(lc(fin, fin, rfl.at[t]))
            else:
                cp = lc(fin, gout_out if t == 11 else gpk_out, rfl.at[t])
                cp.start()
                finals.append(cp)

    for t in range(14):
        task(rs_after_c, (DO_RC, t), t)
        if t in (11, 12):
            task(rs_after_y, (DO_RY, t), t)
        task(rs_after_x, (DO_RX, t), t)
        task(rs_forward, (DO_RF, t), t)
        task(rs_finish, (DO_RZ, t), t)

    def make_down(t):
        first, count = DOWN[t]
        need_ds(first if first < 2 else first // 2 + 1)
        ds_cols = dsg[:, :, first * 128 : (first + count) * 128].reshape(512, count * 128)
        for i in range(4):
            part = gelu[:, :, i * 512 : (i + 1) * 512].reshape(512, 512)
            value = dot(part, ds_cols, 0, 0).astype(BF)
            for k in range(count):
                gD[first + k, i] = value[:, k * 128 : (k + 1) * 128].reshape(2, 2, 128, 128)
        rs_c(t).start()

    for t in DOWN:
        task(make_down, (DO_GD, t), t)

    def make_a(t, left, right):
        for i in range(4):
            part = left[:, :, i * 256 : (i + 1) * 256].reshape(512, 256)
            gA[slot_of[t], i] = dot(part, right, 0, 0).astype(BF).reshape(2, 2, 64, 512)
        rs_c(t).start()

    dub_started = []

    def make_dpre(i, own):
        if not own:
            need_ds(0, 1, 2, 3, 4)
        half = y if own else oy
        cols = slice(i * 512, (i + 1) * 512)
        acc = None
        for j in range(4):
            right = jnp.concatenate([wD[2 * j + k, i].reshape(512, 128) for k in range(2)], 1)
            part = dot(dsg[half, :, j * 256 : (j + 1) * 256], right, 1, 1)
            acc = part if acc is None else acc + part
        low = (acc * slope[half, :, cols].astype(F32)).astype(BF)
        slope[half, :, cols] = low
        total = col_sum(low.astype(F32))
        if i in dub_started:
            total = total + dub[0:1, cols]
        dub_started.append(i)
        dub[0:1, cols] = total

    def up_grad(j):
        make_a(3 + j, nmg, slope[:, :, j * 512 : (j + 1) * 512].reshape(512, 512))

    for j in range(4):
        task(make_dpre, (DO_DP, j, 0), j, True)
        task(make_dpre, (DO_DP, j, 1), j, False)
        task(up_grad, (DO_GU, j), j)

    def dnorm_mid(half, n):
        acc = None
        for j in range(4):
            part = dot(slope[half, :, j * 512 : (j + 1) * 512], wA[3 + j, n].reshape(256, 512), 1, 1)
            acc = part if acc is None else acc + part
        dh[half, :, n * 256 : (n + 1) * 256] = acc

    for n in range(4):
        task(dnorm_mid, (DO_DNO, n), oy, n)
        task(dnorm_mid, (DO_DNS, n), y, n)

    zero_row = jnp.zeros((1, 1024), F32)

    def back_mid(own):
        half = y if own else oy

        def rows_of(i, carry):
            a, b, d = carry
            rows = pl.ds(pl.multiple_of(i * 64, 64), 64)
            dy = dh[half, rows, :]
            unit, inv = unit_of(h1[half, rows, :])
            total = ln_back(dy, unit, inv, row(1))
            if own:
                total = total + st[rows, :]
            dh[half, rows, :] = total
            low = total.astype(BF)
            dhl[half, rows, :] = low
            return a + col_sum(dy * unit), b + col_sum(dy), d + col_sum(low.astype(F32))

        a, b, d = lax.fori_loop(0, 4, rows_of, (zero_row, zero_row, zero_row))
        add_row(1, a)
        add_row(4, b)
        add_row(8, d)

    task(back_mid, (DO_BACKMID, 0), True)
    task(back_mid, (DO_BACKMID, 1), False)

    def datt(yy, p):
        right = wO[2 * yy + p // 2, p % 2].reshape(128, 1024)
        return dot(dhl[...].reshape(512, 1024), right, 1, 1).reshape(2, 256, 128)

    def da_copy(p):
        cols = pl.ds(p * 128, 128)
        return rc(das.at[:, :, cols], dattg.at[:, :, cols], dsend.at[7 + p], drecv.at[7 + p], ydev)

    def datt_other(p):
        das[:, :, p * 128 : (p + 1) * 128] = datt(oy, p).astype(BF)
        send(da_copy(p))

    for p in range(4):
        task(datt_other, (DO_DAO, p), p)

    def out_grad():
        for i in range(4):
            part = att[:, :, i * 256 : (i + 1) * 256].reshape(512, 256)
            gO[i] = dot(part, dhl[...].reshape(512, 1024), 0, 0).astype(BF).reshape(2, 2, 2, 32, 1024)
        rs_c(11).start()

    task(out_grad, (DO_GO,))

    dqkv = qkv

    def attend_back(p):
        da_copy(p).wait_recv()
        cols = slice(p * 128, p * 128 + 128)
        q2 = qkv[0, :, :, cols]
        k2 = qkv[1, :, :, cols].reshape(512, 128)
        v2 = qkv[2, :, :, cols].reshape(512, 128)
        do2 = (datt(y, p) + dattg[:, :, cols].astype(F32)).astype(BF)
        zero = jnp.zeros((512, 128), BF)
        dks = [None, None]
        dvs = [None, None]
        for half in range(2):
            nk = 256 * (half + 1)
            dq = None
            for e in range(2):
                qe = jnp.where(in_head[e], q2[half], zero[:256])
                doe = jnp.where(in_head[e], do2[half], zero[:256])
                ke = jnp.where(in_head[e], k2[:nk], zero[:nk])
                probs = probs_of(qe, k2, half)
                dprob = dot(doe, v2[:nk], 1, 1)
                delta = jnp.sum(probs * dprob, -1, keepdims=True)
                ds = (probs * (dprob - delta)).astype(BF)
                part = dot(ds, ke)
                dq = part if dq is None else dq + part
                dk = dot(ds, qe, 0, 0)
                dv = dot(probs.astype(BF), doe, 0, 0)
                for kb in range(half + 1):
                    rows = slice(kb * 256, kb * 256 + 256)
                    dks[kb] = dk[rows] if dks[kb] is None else dks[kb] + dk[rows]
                    dvs[kb] = dv[rows] if dvs[kb] is None else dvs[kb] + dv[rows]
            dqkv[0, half, :, cols] = (dq * 0.125).astype(BF)
        for kb in range(2):
            dqkv[1, kb, :, cols] = (dks[kb] * 0.125).astype(BF)
            dqkv[2, kb, :, cols] = dvs[kb].astype(BF)

    for p in range(4):
        task(attend_back, (DO_AB, p), p)

    def qkv_grad(s):
        for cond, cp in rs_sends(3 + s):
            when(cond, cp.wait_send)
        make_a(s, ni, dqkv[s].reshape(512, 512))

    for s in range(3):
        task(qkv_grad, (DO_GQ, s), s)

    def di_copy(i):
        rows = pl.ds(i * 128, 128)
        return rc(prec.at[rows], dnr2.at[rows], msend.at[1 + i], mrecv.at[1 + i], ydev)

    def dnorm_in(own):
        half = y if own else oy
        for n in range(4):
            acc = None
            for s in range(3):
                part = dot(dqkv[s, half], wA[s, n].reshape(256, 512), 1, 1)
                acc = part if acc is None else acc + part
            st[:, n * 256 : (n + 1) * 256] = acc

    def back_in(own, i):
        half = y if own else oy

        def rows_of(k, carry):
            a, b = carry
            rows = pl.ds(pl.multiple_of(k * 64, 64), 64)
            dy = st[rows, :]
            unit, inv = unit_of(tokg[half, rows, :].astype(F32))
            total = dh[half, rows, :] + ln_back(dy, unit, inv, row(0))
            if own:
                dh[half, rows, :] = total
            else:
                prec[rows, :] = total.astype(BF)
            return a + col_sum(dy * unit), b + col_sum(dy)

        a, b = lax.fori_loop(2 * i, 2 * i + 2, rows_of, (zero_row, zero_row))
        add_row(0, a)
        add_row(3, b)
        if not own:
            send(di_copy(i))

    task(dnorm_in, (DO_DIO,), False)
    task(dnorm_in, (DO_DIS,), True)
    for i in range(2):
        task(back_in, (DO_BIO, i), False, i)
        task(back_in, (DO_BIS, i), True, i)

    gin_started = []

    def grad_in(i):
        di_copy(i).wait_recv()
        if not gin_started:
            out_state.wait()
        gin_started.append(i)
        rows = slice(i * 128, i * 128 + 128)
        hgrad[rows, :] = (dh[y, rows, :] + dnr2[rows, :].astype(F32)).astype(BF)
        cp = lc(hgrad.at[pl.ds(i * 128, 128)], gin_out.at[pl.ds(i * 128, 128)], osem.at[2 + i])
        cp.start()
        finals.append(cp)

    for i in range(2):
        task(grad_in, (DO_GIN, i), i)

    def small_grads():
        pg[6:7, head_cols] = col_sum(dqkv[0].reshape(512, 512).astype(F32))
        pg[7:8, head_cols] = col_sum(dqkv[2].reshape(512, 512).astype(F32))
        for d in range(32):
            piece = pg[:, (d // 4) * 128 : (d // 4) * 128 + 128]
            mine = jnp.where(y == d % 2, dub[0:1, (d // 2) * 128 : (d // 2) * 128 + 128], 0.0)
            gP[d // 8, (d // 4) % 2, (d // 2) % 2, d % 2] = jnp.where(row_id == 10, mine, piece)
        rs_c(12).start()

    task(small_grads, (DO_GP,))

    for name in ORDER:
        tasks.pop(name)()
    assert not tasks, sorted(tasks)
    for cp in late_recv:
        cp.wait_recv()
    for cond, cp in pending:
        when(cond, cp.wait_send)
    for cp in finals:
        cp.wait()


def finish_kernel(state, loss, gin, gqkv, gout, gup, gdown, gpk, *refs):
    outs, held, (sem, out_sem) = refs[:11], refs[11:18], refs[18:]
    big = [(state, 0), (loss, 1), (gin, 2), (gqkv, 3), (gout, 4), (gup, 5), (gdown, 6)]
    copies = [pltpu.make_async_copy(src, held[i], sem.at[i]) for src, i in big]
    for cp in copies:
        cp.start()
    quarter = (2 * lax.axis_index("dp") + lax.axis_index("fsdp")) % 4
    total = gpk[...]
    mine = pltpu.roll(total, ((4 - quarter) % 4) * 32, 1)
    outs[7][...] = mine[0:3, 0:32]
    outs[8][...] = mine[3:6, 0:32]
    outs[9][...] = mine[6:10, 0:32]
    outs[10][...] = total[10:11, :]
    results = [pltpu.make_async_copy(held[i], outs[i], out_sem.at[i]) for _, i in big]
    for cp, result in zip(copies, results):
        cp.wait()
        result.start()
    for result in results:
        result.wait()


SCRATCH = dict(
    wA=((7, 4, 2, 2, 64, 512), BF), wD=((8, 4, 2, 2, 128, 128), BF), wO=((4, 2, 2, 2, 32, 1024), BF),
    pk=((4, 2, 2, 2, 16, 128), BF), prm=((16, 1024), F32), ubias=((8, 2048), F32),
    tokg=((2, 256, 1024), BF), ni=((2, 256, 1024), BF), qkv=((3, 2, 256, 512), BF), mask=((512, 512), BF),
    att=((2, 256, 1024), BF), h1=((2, 256, 1024), F32), nmg=((2, 256, 1024), BF),
    gelu=((2, 256, 2048), BF), slope=((2, 256, 2048), BF), st=((256, 1024), F32), prec=((256, 1024), BF),
    hgrad=((256, 1024), BF), ksq=((256, 128), F32), match=((256, 128), F32), dsg=((2, 256, 1024), BF),
    tcol=((256, 1), F32), pcol=((256, 1), F32), lcol=((256, 1), F32), lossb=((1, 256), F32),
    dh=((2, 256, 1024), F32), dhl=((2, 256, 1024), BF), das=((2, 256, 512), BF), dattg=((2, 256, 512), BF),
    dnr2=((256, 1024), BF), sendb=((256, 1024), BF),
    gA=((4, 4, 2, 2, 64, 512), BF), gD=((8, 4, 2, 2, 128, 128), BF), gO=((4, 2, 2, 2, 32, 1024), BF),
    gP=((4, 2, 2, 2, 16, 128), F32),
    dRA=((7, 4, 2, 64, 512), BF), xRA=((7, 4, 64, 512), BF), zRA=((7, 4, 64, 512), BF),
    dRD=((8, 4, 2, 128, 128), BF), xRD=((8, 4, 128, 128), BF), zRD=((8, 4, 128, 128), BF),
    dRO=((4, 2, 2, 32, 1024), BF), yRO=((4, 2, 32, 1024), BF), xRO=((4, 32, 1024), BF), zRO=((4, 32, 1024), BF),
    dRP=((4, 2, 2, 16, 128), F32), yRP=((4, 2, 16, 128), F32), xRP=((4, 16, 128), F32), zRP=((4, 16, 128), F32),
    finA=((7, 2, 32, 512), F32), finD=((8, 128, 128), F32), finO=((32, 1024), F32), finP=((16, 128), F32),
    xOA=((3, 64, 512), BF), xOD=((3, 2, 128, 128), BF), pg=((16, 1024), F32), dub=((8, 2048), F32),
)
SEMS = dict(
    lsem=(15,), ysend=(9,), yrecv=(9,), zsend=(14, 4), zrecv=(14, 4), xsend=(14, 4), xrecv=(14, 4),
    csend=(14,), crecv=(14,), osem=(4,), msend=(3,), mrecv=(3,), asend=(4,), arecv=(4,),
    dsend=(11,), drecv=(11,), psend=(5,), precv=(5,), rcs=(14,), rcr=(14,), rxs=(14,), rxr=(14,),
    rzs=(14, 4), rzr=(14, 4), rys=(14,), ryr=(14,), rfl=(14,), kn_sem=(2,),
)


def on_device_fused(
    tokens, head_grad, w_qkv, w_out, w_up, w_down, gains, shifts, biases, up_bias, seq_lengths,
    neigh_keys, neigh_ids, neigh_counts, targets, p_lm,
):
    keys = neigh_keys.reshape(4, 2, 2, 128, 1024)
    anywhere = pl.BlockSpec(memory_space=pl.ANY)
    vmem = pl.BlockSpec(memory_space=pltpu.VMEM)
    smem = pl.BlockSpec(memory_space=pltpu.SMEM)
    shape = jax.ShapeDtypeStruct
    results = [
        shape((256, 1024), BF),
        shape((1, 256), F32),
        shape((256, 1024), BF),
        shape((32, 3072), F32),
        shape((32, 1024), F32),
        shape((32, 4096), F32),
        shape((128, 1024), F32),
    ]
    held = pl.pallas_call(
        block_kernel,
        out_shape=results + [shape((16, 128), F32)],
        in_specs=[anywhere] * 6 + [vmem] * 4 + [smem, smem, anywhere, vmem, vmem, vmem],
        out_specs=[anywhere] * 8,
        scratch_shapes=[pltpu.VMEM(*SCRATCH[k]) for k in SCRATCH]
        + [pltpu.SemaphoreType.DMA(SEMS[k]) for k in SEMS],
        compiler_params=pltpu.CompilerParams(
            collective_id=0, has_side_effects=True, vmem_limit_bytes=VMEM_LIMIT
        ),
        name="block",
    )(
        tokens, head_grad, w_qkv, w_out, w_up, w_down, gains, shifts, biases, up_bias.reshape(1, 128),
        seq_lengths, neigh_counts.reshape(1, 16), keys, neigh_ids, targets.reshape(1, 256),
        p_lm.reshape(1, 256),
    )
    small = [shape((3, 32), F32), shape((3, 32), F32), shape((4, 32), F32), shape((1, 128), F32)]
    res = pl.pallas_call(
        finish_kernel,
        out_shape=results + small,
        in_specs=[anywhere] * 7 + [vmem],
        out_specs=[anywhere] * 7 + [vmem] * 4,
        scratch_shapes=[pltpu.VMEM(r.shape, r.dtype) for r in results]
        + [pltpu.SemaphoreType.DMA((7,)), pltpu.SemaphoreType.DMA((7,))],
        name="finish",
    )(*held)
    state, loss, gin, gqkv, gout, gup, gdown, dgains, dshifts, dbiases, dub = res
    return (
        state, loss.reshape(256), gin, gqkv, gout, gup, gdown, dgains, dshifts, dbiases, dub.reshape(128),
    )


def solution(mesh):
    in_specs = (
        P(("dp", "fsdp"), None),
        P(("dp", "fsdp"), None),
        P(("dp", "fsdp"), None),
        P(("dp", "fsdp"), None),
        P(("dp", "fsdp"), None),
        P(("dp", "fsdp"), None),
        P(None, ("dp", "fsdp")),
        P(None, ("dp", "fsdp")),
        P(None, ("dp", "fsdp")),
        P(("dp", "fsdp")),
        P("dp", None),
        P(("dp", "fsdp"), None, None),
        P(("dp", "fsdp"), None),
        P(("dp", "fsdp")),
        P(("dp", "fsdp")),
        P(("dp", "fsdp")),
    )
    out_specs = (
        P(("dp", "fsdp"), None),
        P(("dp", "fsdp")),
        P(("dp", "fsdp"), None),
        P(("dp", "fsdp"), None),
        P(("dp", "fsdp"), None),
        P(("dp", "fsdp"), None),
        P(("dp", "fsdp"), None),
        P(None, ("dp", "fsdp")),
        P(None, ("dp", "fsdp")),
        P(None, ("dp", "fsdp")),
        P(("dp", "fsdp")),
    )
    fused = mesh.shape["dp"] == 16 and mesh.shape["fsdp"] == 2
    return jax.shard_map(
        on_device_fused if fused else on_device, mesh=mesh, in_specs=in_specs, out_specs=out_specs, check_vma=False
    )
```

```python
import functools
import math

import jax
import jax.numpy as jnp
from jax import lax
from jax.experimental import pallas as pl
from jax.experimental.pallas import tpu as pltpu
from jax.sharding import PartitionSpec as P

HEADS = 16


EPSILON = 1e-05
MIX_WEIGHT = 0.25


def norm_rows(values, gain_row, shift_row):
    center = values - jnp.mean(values, -1, keepdims=True)
    inverse = lax.rsqrt(jnp.mean(center * center, -1, keepdims=True) + EPSILON)
    unit_rows = center * inverse
    return (unit_rows * gain_row + shift_row, unit_rows, inverse)


def norm_back(grad_rows, unit_rows, inverse, gain_row):
    scaled = grad_rows * gain_row
    first_mean = jnp.mean(scaled, -1, keepdims=True)
    second_mean = jnp.mean(scaled * unit_rows, -1, keepdims=True)
    grad_values = inverse * (scaled - first_mean - unit_rows * second_mean)
    return (grad_values, jnp.sum(grad_rows * unit_rows, 0), jnp.sum(grad_rows, 0))


def contract_rows(left, right):
    return lax.dot_general(
        left, right, (((0,), (0,)), ((), ())), preferred_element_type=jnp.float32
    )


def times_transposed(left, right):
    return lax.dot_general(
        left, right, (((1,), (1,)), ((), ())), preferred_element_type=jnp.float32
    )


def segment_of(lengths, positions):
    first_end = lengths[0]
    second_end = lengths[0] + lengths[1]
    return (positions >= first_end).astype(jnp.int32) + (positions >= second_end).astype(jnp.int32)


def on_device(
    tokens,
    head_grad,
    w_qkv,
    w_out,
    w_up,
    w_down,
    gains,
    shifts,
    biases,
    up_bias,
    seq_lengths,
    neigh_keys,
    neigh_ids,
    neigh_counts,
    targets,
    p_lm,
):
    gathered = (
        lax.all_gather(w_qkv, ("dp", "fsdp"), axis=0, tiled=True),
        lax.all_gather(w_out, ("dp", "fsdp"), axis=0, tiled=True),
        lax.all_gather(w_up, ("dp", "fsdp"), axis=0, tiled=True),
        lax.all_gather(w_down, ("dp", "fsdp"), axis=0, tiled=True),
        lax.all_gather(gains, ("dp", "fsdp"), axis=1, tiled=True),
        lax.all_gather(shifts, ("dp", "fsdp"), axis=1, tiled=True),
        lax.all_gather(biases, ("dp", "fsdp"), axis=1, tiled=True),
        lax.all_gather(up_bias, ("dp", "fsdp"), axis=0, tiled=True),
    )
    row_count, feature_width = tokens.shape
    head_count = HEADS
    head_depth = feature_width // head_count
    score_scale = 1.0 / math.sqrt(head_depth)
    gain_rows = gathered[4].astype(jnp.float32)
    shift_rows = gathered[5].astype(jnp.float32)
    bias_rows = gathered[6].astype(jnp.float32)
    tokens_f32 = tokens.astype(jnp.float32)
    normed_in, unit_in, inverse_in = norm_rows(tokens_f32, gain_rows[0], shift_rows[0])
    normed_in_low = normed_in.astype(jnp.bfloat16)
    qkv_bias = jnp.concatenate([bias_rows[0], jnp.zeros_like(bias_rows[0]), bias_rows[1]])
    qkv = (
        jnp.dot(normed_in_low, gathered[0], preferred_element_type=jnp.float32) + qkv_bias
    ).astype(jnp.bfloat16)
    query_heads = qkv[:, :feature_width].reshape(row_count, head_count, head_depth)
    kv_local = qkv[:, feature_width:]
    kv_group = lax.all_gather(kv_local, "fsdp", axis=0, tiled=True)
    group_size = kv_group.shape[0]
    part_count = lax.axis_size("fsdp")
    block_rows = row_count * min(part_count, max(1, 512 // row_count))
    block_count = group_size // block_rows
    first_row = lax.axis_index("fsdp") * row_count
    last_row = first_row + row_count - 1
    lengths = seq_lengths[0]
    query_pos = first_row + jnp.arange(row_count, dtype=jnp.int32)
    query_seg = segment_of(lengths, query_pos)

    def scores_of(source, block_start):
        key_piece = lax.dynamic_slice_in_dim(source, block_start, block_rows, 0)
        key_heads = key_piece[:, :feature_width].reshape(block_rows, head_count, head_depth)
        value_heads = key_piece[:, feature_width:].reshape(block_rows, head_count, head_depth)
        key_pos = block_start + jnp.arange(block_rows, dtype=jnp.int32)
        allowed = (segment_of(lengths, key_pos)[None, :] == query_seg[:, None]) & (
            key_pos[None, :] <= query_pos[:, None]
        )
        raw_scores = (
            jnp.einsum("qhe,khe->hqk", query_heads, key_heads, preferred_element_type=jnp.float32)
            * score_scale
        )
        return (jnp.where(allowed[None], raw_scores, -jnp.inf), key_heads, value_heads)

    def keep_same(kept_value):
        return kept_value

    def stats_step(block_index, stats):
        block_start = block_index * block_rows

        def stats_block_work(pair):
            row_top, row_total = pair
            masked, key_heads, value_heads = scores_of(kv_group, block_start)
            new_top = jnp.maximum(row_top, jnp.max(masked, -1))
            safe_top = jnp.where(new_top > -jnp.inf, new_top, 0.0)
            row_total = row_total * jnp.exp(row_top - safe_top) + jnp.sum(
                jnp.exp(masked - safe_top[..., None]), -1
            )
            return (new_top, row_total)

        return lax.cond(block_start <= last_row, stats_block_work, keep_same, stats)

    start_stats = (
        jnp.full((head_count, row_count), -jnp.inf, jnp.float32),
        jnp.zeros((head_count, row_count), jnp.float32),
    )
    row_top, row_total = lax.fori_loop(0, block_count, stats_step, start_stats)
    log_total = row_top + jnp.log(row_total)

    def value_step(block_index, value_acc):
        block_start = block_index * block_rows

        def value_block_work(value_sum):
            masked, key_heads, value_heads = scores_of(kv_group, block_start)
            prob_low = jnp.exp(masked - log_total[..., None]).astype(jnp.bfloat16)
            return value_sum + jnp.einsum(
                "hqk,khe->qhe", prob_low, value_heads, preferred_element_type=jnp.float32
            )

        return lax.cond(block_start <= last_row, value_block_work, keep_same, value_acc)

    attended = lax.fori_loop(
        0, block_count, value_step, jnp.zeros((row_count, head_count, head_depth), jnp.float32)
    )
    attended = attended.reshape(row_count, feature_width)
    attended_low = attended.astype(jnp.bfloat16)
    hidden_one = tokens_f32 + (
        jnp.dot(attended_low, gathered[1], preferred_element_type=jnp.float32) + bias_rows[2]
    )
    normed_mid, unit_mid, inverse_mid = norm_rows(hidden_one, gain_rows[1], shift_rows[1])
    normed_mid_low = normed_mid.astype(jnp.bfloat16)
    pre_act = jnp.dot(normed_mid_low, gathered[2], preferred_element_type=jnp.float32) + gathered[
        7
    ].astype(jnp.float32)
    gelu_low = jax.nn.gelu(pre_act).astype(jnp.bfloat16)
    state_f32 = hidden_one + (
        jnp.dot(gelu_low, gathered[3], preferred_element_type=jnp.float32) + bias_rows[3]
    )
    query, unit_out, inverse_out = norm_rows(state_f32, gain_rows[2], shift_rows[2])
    span_count = neigh_keys.shape[0]
    slot_count = neigh_keys.shape[1]
    knn_scale = 0.5 / math.sqrt(feature_width)
    query_low = query.astype(jnp.bfloat16).reshape(span_count, -1, feature_width)
    key_square = jnp.einsum(
        "snd,snd->sn", neigh_keys, neigh_keys, preferred_element_type=jnp.float32
    )
    raw_logits = jnp.einsum(
        "sqd,snd->sqn", query_low, neigh_keys, preferred_element_type=jnp.float32
    )
    logits = (2.0 * raw_logits - key_square[:, None, :]) * knn_scale
    slot_valid = jnp.arange(slot_count, dtype=jnp.int32)[None, :] < neigh_counts[:, None]
    masked_logits = jnp.where(slot_valid[:, None, :], logits, -jnp.inf)
    exp_values = jnp.exp(masked_logits - jnp.max(masked_logits, -1, keepdims=True))
    weights = exp_values / jnp.sum(exp_values, -1, keepdims=True)
    id_match = neigh_ids[:, None, :] == targets.reshape(span_count, -1)[:, :, None]
    knn_prob = jnp.sum(jnp.where(id_match, weights, 0.0), -1)
    mixture = MIX_WEIGHT * knn_prob + (1.0 - MIX_WEIGHT) * p_lm.reshape(span_count, -1)
    token_loss = -jnp.log(mixture).reshape(row_count)
    match_f32 = jnp.where(id_match, 1.0, 0.0)
    dlogits = (
        -(MIX_WEIGHT / mixture)[..., None] * weights * (match_f32 - knn_prob[..., None])
    ).astype(jnp.bfloat16)
    knn_grad = jnp.einsum(
        "sqn,snd->sqd", dlogits, neigh_keys, preferred_element_type=jnp.float32
    ) * (2.0 * knn_scale)
    dquery = head_grad.astype(jnp.float32) + knn_grad.reshape(row_count, feature_width)
    back_params = (
        lax.all_gather(w_qkv, ("dp", "fsdp"), axis=0, tiled=True),
        lax.all_gather(w_out, ("dp", "fsdp"), axis=0, tiled=True),
        lax.all_gather(w_up, ("dp", "fsdp"), axis=0, tiled=True),
        lax.all_gather(w_down, ("dp", "fsdp"), axis=0, tiled=True),
        lax.all_gather(gains, ("dp", "fsdp"), axis=1, tiled=True),
        lax.all_gather(shifts, ("dp", "fsdp"), axis=1, tiled=True),
        lax.all_gather(biases, ("dp", "fsdp"), axis=1, tiled=True),
        lax.all_gather(up_bias, ("dp", "fsdp"), axis=0, tiled=True),
    )
    kv_back = lax.all_gather(kv_local, "fsdp", axis=0, tiled=True)
    gain_back = back_params[4].astype(jnp.float32)
    dstate, gain_grad_out, shift_grad_out = norm_back(dquery, unit_out, inverse_out, gain_back[2])
    dstate_low = dstate.astype(jnp.bfloat16)
    grad_w_down = contract_rows(gelu_low, dstate_low)
    bias_grad_down = jnp.sum(dstate_low.astype(jnp.float32), 0)
    dgelu = times_transposed(dstate_low, back_params[3])
    gelu_value, gelu_pull = jax.vjp(jax.nn.gelu, pre_act)
    dpre_low = gelu_pull(dgelu)[0].astype(jnp.bfloat16)
    grad_w_up = contract_rows(normed_mid_low, dpre_low)
    grad_up_bias = jnp.sum(dpre_low.astype(jnp.float32), 0)
    dnormed_mid = times_transposed(dpre_low, back_params[2])
    dhidden_part, gain_grad_mid, shift_grad_mid = norm_back(
        dnormed_mid, unit_mid, inverse_mid, gain_back[1]
    )
    dhidden_one = dstate + dhidden_part
    dhidden_low = dhidden_one.astype(jnp.bfloat16)
    grad_w_out = contract_rows(attended_low, dhidden_low)
    bias_grad_out = jnp.sum(dhidden_low.astype(jnp.float32), 0)
    dattended_low = times_transposed(dhidden_low, back_params[1]).astype(jnp.bfloat16)
    dattended_heads = dattended_low.reshape(row_count, head_count, head_depth)
    delta_rows = jnp.sum(
        dattended_heads.astype(jnp.float32) * attended.reshape(row_count, head_count, head_depth),
        -1,
    ).T

    def both_grad_step(block_index, grad_pair):
        block_start = block_index * block_rows

        def both_block_work(pair):
            dquery_acc, dkv_group = pair
            masked, key_heads, value_heads = scores_of(kv_back, block_start)
            prob_values = jnp.exp(masked - log_total[..., None])
            prob_low = prob_values.astype(jnp.bfloat16)
            dprob = jnp.einsum(
                "qhe,khe->hqk", dattended_heads, value_heads, preferred_element_type=jnp.float32
            )
            dscores = (prob_values * (dprob - delta_rows[..., None])).astype(jnp.bfloat16)
            dquery_acc = dquery_acc + jnp.einsum(
                "hqk,khe->qhe", dscores, key_heads, preferred_element_type=jnp.float32
            )
            dkey_heads = (
                jnp.einsum("hqk,qhe->khe", dscores, query_heads, preferred_element_type=jnp.float32)
                * score_scale
            )
            dvalue_heads = jnp.einsum(
                "hqk,qhe->khe", prob_low, dattended_heads, preferred_element_type=jnp.float32
            )
            block_grad = jnp.concatenate(
                [
                    dkey_heads.reshape(block_rows, feature_width),
                    dvalue_heads.reshape(block_rows, feature_width),
                ],
                1,
            )
            current = lax.dynamic_slice_in_dim(dkv_group, block_start, block_rows, 0)
            return (
                dquery_acc,
                lax.dynamic_update_slice_in_dim(dkv_group, current + block_grad, block_start, 0),
            )

        return lax.cond(block_start <= last_row, both_block_work, keep_same, grad_pair)

    zero_dquery = jnp.zeros((row_count, head_count, head_depth), jnp.float32)
    start_grads = (zero_dquery, jnp.zeros((group_size, 2 * feature_width), jnp.float32))
    dquery_acc, dkv_group = lax.fori_loop(0, block_count, both_grad_step, start_grads)
    dkv_mine = lax.psum_scatter(
        dkv_group.astype(jnp.bfloat16), "fsdp", scatter_dimension=0, tiled=True
    ).astype(jnp.float32)
    dqkv_low = jnp.concatenate(
        [(dquery_acc * score_scale).reshape(row_count, feature_width), dkv_mine], 1
    ).astype(jnp.bfloat16)
    grad_w_qkv = contract_rows(normed_in_low, dqkv_low)
    column_sums = jnp.sum(dqkv_low.astype(jnp.float32), 0)
    dnormed_in = times_transposed(dqkv_low, back_params[0])
    dinput_part, gain_grad_in, shift_grad_in = norm_back(
        dnormed_in, unit_in, inverse_in, gain_back[0]
    )
    grad_input = (dhidden_one + dinput_part).astype(jnp.bfloat16)
    grad_gains = jnp.stack([gain_grad_in, gain_grad_mid, gain_grad_out])
    grad_shifts = jnp.stack([shift_grad_in, shift_grad_mid, shift_grad_out])
    grad_biases = jnp.stack(
        [
            column_sums[:feature_width],
            column_sums[2 * feature_width :],
            bias_grad_out,
            bias_grad_down,
        ]
    )
    summed = (
        lax.psum_scatter(grad_w_qkv, ("dp", "fsdp"), scatter_dimension=0, tiled=True),
        lax.psum_scatter(grad_w_out, ("dp", "fsdp"), scatter_dimension=0, tiled=True),
        lax.psum_scatter(grad_w_up, ("dp", "fsdp"), scatter_dimension=0, tiled=True),
        lax.psum_scatter(grad_w_down, ("dp", "fsdp"), scatter_dimension=0, tiled=True),
        lax.psum_scatter(grad_gains, ("dp", "fsdp"), scatter_dimension=1, tiled=True),
        lax.psum_scatter(grad_shifts, ("dp", "fsdp"), scatter_dimension=1, tiled=True),
        lax.psum_scatter(grad_biases, ("dp", "fsdp"), scatter_dimension=1, tiled=True),
        lax.psum_scatter(grad_up_bias, ("dp", "fsdp"), scatter_dimension=0, tiled=True),
    )
    return (
        state_f32.astype(jnp.bfloat16),
        token_loss,
        grad_input,
        summed[0],
        summed[1],
        summed[2],
        summed[3],
        summed[4],
        summed[5],
        summed[6],
        summed[7],
    )


VMEM_LIMIT = 63 << 20
KNN_SCALE = 0.5 / 32.0
BF = jnp.bfloat16
F32 = jnp.float32
MESH = pl.DeviceIdType.MESH
NEG = -1e30


def dot(left, right, left_dim=1, right_dim=0):
    return lax.dot_general(
        left, right, (((left_dim,), (right_dim,)), ((), ())), preferred_element_type=F32
    )


def unit_of(values):
    center = values - jnp.mean(values, -1, keepdims=True)
    inverse = lax.rsqrt(jnp.mean(center * center, -1, keepdims=True) + EPSILON)
    return center * inverse, inverse


def ln_back(grad_rows, unit_rows, inverse, gain_row):
    scaled = grad_rows * gain_row
    first_mean = jnp.mean(scaled, -1, keepdims=True)
    second_mean = jnp.mean(scaled * unit_rows, -1, keepdims=True)
    return inverse * (scaled - first_mean - unit_rows * second_mean)


def col_sum(values):
    return jnp.sum(values, 0, keepdims=True)


def gelu_pair(u):
    k0 = math.sqrt(2.0 / math.pi)
    square = u * u
    t = jnp.tanh(u * (k0 + (k0 * 0.044715) * square))
    half = 0.5 * (1.0 + t)
    slope = half + (0.5 * u) * (1.0 - t * t) * (k0 + (3.0 * k0 * 0.044715) * square)
    return u * half, slope


GATHER_X_FIRST = (7, 6)
REDUCE_Z_FIRST = (5, 13, 1)
DOWN = {7: (0, 1), 13: (1, 1), 8: (2, 2), 9: (4, 2), 10: (6, 2)}

(
    DO_Y0, DO_Z, DO_F, DO_X, DO_Y, DO_C, DO_TOK, DO_MASK, DO_COLS, DO_TABLE, DO_UNPACK, DO_NORMOWN,
    DO_NORMOTHER, DO_PROJ, DO_ATTEND, DO_ATTOUT, DO_NORMMID, DO_UP, DO_DOWN, DO_KNN, DO_STATEOUT,
    DO_DSREST, DO_RC, DO_RY, DO_RX, DO_RF, DO_RZ, DO_GD, DO_DP, DO_GU, DO_DNO, DO_DNS, DO_BACKMID,
    DO_DAO, DO_GO, DO_AB, DO_GQ, DO_DIO, DO_DIS, DO_BIO, DO_BIS, DO_GIN, DO_GP,
) = range(43)
ORDER = (
    (DO_Z, 12), (DO_Z, 11), (DO_Y0, 1), (DO_Y0, 4), (DO_Y0, 2), (DO_Y0, 6), (DO_Y0, 3), (DO_Y0, 5),
    (DO_MASK,), (DO_Y0, 0), (DO_TOK,), (DO_COLS,), (DO_TABLE, 0), (DO_F, 12), (DO_TABLE, 2), (DO_Z, 1),
    (DO_TABLE, 1), (DO_TABLE, 3), (DO_Z, 2), (DO_X, 12), (DO_F, 11), (DO_Z, 0), (DO_Z, 5), (DO_Y, 12),
    (DO_X, 11), (DO_Z, 4), (DO_F, 1), (DO_X, 1), (DO_Z, 13), (DO_F, 2), (DO_Y, 11), (DO_X, 2), (DO_Z,
    6), (DO_C, 12), (DO_F, 0), (DO_UNPACK,), (DO_NORMOTHER,), (DO_NORMOWN,), (DO_C, 1), (DO_X, 0),
    (DO_Z, 3), (DO_F, 5), (DO_PROJ, 1, 0), (DO_PROJ, 1, 1), (DO_C, 2), (DO_X, 5), (DO_Z, 9), (DO_F, 4),
    (DO_PROJ, 2, 0), (DO_PROJ, 2, 1), (DO_F, 13), (DO_F, 6), (DO_C, 11), (DO_X, 4), (DO_Z, 8), (DO_C,
    0), (DO_X, 13), (DO_Z, 7), (DO_F, 3), (DO_PROJ, 0, 0), (DO_PROJ, 0, 1), (DO_ATTEND, 0), (DO_ATTEND,
    2), (DO_C, 5), (DO_ATTEND, 1), (DO_ATTEND, 3), (DO_F, 9), (DO_C, 4), (DO_C, 13), (DO_X, 6), (DO_Z,
    10), (DO_X, 3), (DO_X, 9), (DO_ATTOUT, 0), (DO_ATTOUT, 1), (DO_F, 8), (DO_F, 7), (DO_NORMMID, 0),
    (DO_UP, 2, 0), (DO_UP, 1, 0), (DO_C, 6), (DO_NORMMID, 1), (DO_C, 3), (DO_X, 8), (DO_F, 10), (DO_UP,
    1, 1), (DO_UP, 2, 1), (DO_UP, 3, 0), (DO_C, 9), (DO_UP, 3, 1), (DO_UP, 0, 0), (DO_UP, 0, 1),
    (DO_DOWN, 13), (DO_X, 7), (DO_X, 10), (DO_DOWN, 9), (DO_C, 8), (DO_C, 7), (DO_DOWN, 8), (DO_DOWN,
    7), (DO_C, 10), (DO_DOWN, 10), (DO_KNN, 0), (DO_KNN, 1), (DO_DSREST,), (DO_DP, 1, 0), (DO_DP, 0, 0),
    (DO_DP, 2, 0), (DO_DP, 3, 0), (DO_STATEOUT,), (DO_GD, 7), (DO_GD, 13), (DO_RC, 13), (DO_RC, 7),
    (DO_GD, 8), (DO_GD, 9), (DO_RF, 13), (DO_RC, 8), (DO_RX, 7), (DO_DP, 3, 1), (DO_RC, 9), (DO_DP, 1,
    1), (DO_GD, 10), (DO_RF, 7), (DO_DP, 0, 1), (DO_GU, 0), (DO_GU, 1), (DO_DP, 2, 1), (DO_DNO, 2),
    (DO_DNO, 0), (DO_DNO, 1), (DO_RZ, 7), (DO_RX, 8), (DO_RC, 3), (DO_GU, 2), (DO_RC, 4), (DO_GU, 3),
    (DO_DNO, 3), (DO_DNS, 0), (DO_DNS, 2), (DO_RF, 8), (DO_BACKMID, 1), (DO_RC, 5), (DO_RC, 10), (DO_RX,
    9), (DO_DNS, 1), (DO_RC, 6), (DO_RX, 13), (DO_RZ, 8), (DO_DNS, 3), (DO_BACKMID, 0), (DO_DAO, 3),
    (DO_GO,), (DO_RF, 5), (DO_DAO, 2), (DO_RX, 3), (DO_RF, 9), (DO_DAO, 0), (DO_DAO, 1), (DO_AB, 3),
    (DO_RF, 3), (DO_RX, 4), (DO_RC, 11), (DO_AB, 2), (DO_RX, 5), (DO_RF, 4), (DO_AB, 0), (DO_RZ, 9),
    (DO_RZ, 3), (DO_RX, 10), (DO_AB, 1), (DO_GQ, 0), (DO_RZ, 4), (DO_RZ, 13), (DO_RF, 10), (DO_GQ, 1),
    (DO_RX, 6), (DO_RZ, 5), (DO_GQ, 2), (DO_RC, 0), (DO_DIO,), (DO_RZ, 10), (DO_RC, 1), (DO_BIO, 1),
    (DO_RC, 2), (DO_RY, 11), (DO_RF, 6), (DO_BIO, 0), (DO_DIS,), (DO_BIS, 1), (DO_BIS, 0), (DO_RF, 1),
    (DO_GP,), (DO_RX, 0), (DO_RC, 12), (DO_RZ, 6), (DO_RF, 0), (DO_RX, 2), (DO_RX, 1), (DO_RF, 2),
    (DO_GIN, 0), (DO_GIN, 1), (DO_RZ, 0), (DO_RY, 12), (DO_RX, 11), (DO_RZ, 1), (DO_RX, 12), (DO_RZ, 2),
    (DO_RF, 11), (DO_RF, 12), (DO_RZ, 11), (DO_RZ, 12),
)


def block_kernel(
    tokens, head_grad, w_qkv, w_out, w_up, w_down, gains, shifts, biases, up_bias, seq, counts, keys_in,
    ids, targets, p_lm, state_out, loss_out, gin_out, gqkv_out, gout_out, gup_out, gdown_out, gpk_out,
    wA, wD, wO, pk, prm, ubias, tokg, ni, qkv, mask, att, h1, nmg, gelu, slope, st, prec, hgrad, ksq,
    match, dsg, tcol, pcol, lcol, lossb, dh, dhl, das, dattg, dnr2, sendb, gA, gD, gO, gP, dRA, xRA,
    zRA, dRD, xRD, zRD, dRO, yRO, xRO, zRO, dRP, yRP, xRP, zRP, finA, finD, finO, finP, xOA, xOD, pg,
    dub, lsem, ysend, yrecv, zsend, zrecv, xsend, xrecv, csend, crecv, osem, msend, mrecv, asend, arecv,
    dsend, drecv, psend, precv, rcs, rcr, rxs, rxr, rzs, rzr, rys, ryr, rfl, kn_sem,
):
    dp = lax.axis_index("dp")
    y = lax.axis_index("fsdp")
    z = dp // 4
    x = (dp // 2) % 2
    c = dp % 2
    oy = 1 - y
    ox = 1 - x
    oc = 1 - c

    def dev(zz, xx, cc, yy):
        return ((zz * 2 + xx) * 2 + cc, yy)

    z_to = [None] + [(z + j) % 4 for j in (1, 2, 3)]
    z_of = [z] + [(z - j) % 4 for j in (1, 2, 3)]
    zdev = [None] + [dev(zz, x, c, y) for zz in z_to[1:]]
    xdev = dev(z, ox, c, y)
    ydev = dev(z, x, c, oy)
    cdev = dev(z, x, oc, y)
    middle = (z == 1) | (z == 2)
    z_direct = {1: z != 3, 2: None, 3: z != 0}

    def when(cond, fn):
        if cond is None:
            fn()
        else:
            pl.when(cond)(fn)

    def rc(src, dst_ref, ss, rs, to):
        return pltpu.make_async_remote_copy(
            src_ref=src, dst_ref=dst_ref, send_sem=ss, recv_sem=rs, device_id=to, device_id_type=MESH
        )

    def lc(src, dst_ref, sem):
        return pltpu.make_async_copy(src, dst_ref, sem)

    pending = []
    finals = []
    late_recv = []
    tasks = {}

    def task(fn, name, *args):
        tasks[name] = functools.partial(fn, *args)

    def send(cp, cond=None):
        when(cond, cp.start)
        pending.append((cond, cp))

    my_rows = pl.ds(pl.multiple_of(y * 32, 32), 32)

    def up_cols(j, i, yy):
        return pl.ds(pl.multiple_of((8 * j + 2 * i + yy) * 128, 128), 128)

    def part_cols(part, yy):
        return pl.ds(pl.multiple_of(part * 1024 + yy * 512, 512), 512)

    for s in range(3):
        lc(w_qkv.at[:, part_cols(s, y)], wA.at[s, z, x, c, my_rows], lsem.at[s]).start()
    lc(w_out, wO.at[z, x, c, y], lsem.at[11]).start()
    lc(tokens, tokg.at[y], lsem.at[14]).start()
    for j in range(4):
        for i in range(4):
            lc(w_up.at[:, up_cols(j, i, y)], wA.at[3 + j, z, x, c, my_rows, pl.ds(i * 128, 128)],
               lsem.at[3 + j]).start()
    for t, (first, count) in DOWN.items():
        for h in range(first, first + count):
            lc(w_down.at[:, pl.ds(h * 128, 128)], wD.at[h, z, x, c], lsem.at[t]).start()
    for h in range(8):
        lc(keys_in.at[:, :, :, :, pl.ds(h * 128, 128)], gD.at[h], kn_sem.at[0]).start()
    lc(head_grad, hgrad, kn_sem.at[1]).start()

    quarter = (2 * dp + y) % 4
    pg[...] = jnp.zeros_like(pg)
    pg[0:3, 0:32] = gains[...].astype(F32)
    pg[3:6, 0:32] = shifts[...].astype(F32)
    pg[6:10, 0:32] = biases[...].astype(F32)
    small = pltpu.roll(pg[:, 0:128], quarter * 32, 1)
    pg[10:11, 0:128] = up_bias[...].astype(F32)
    row_id = lax.broadcasted_iota(jnp.int32, (16, 128), 0)
    pk[z, x, c, y] = jnp.where(row_id == 10, pg[:, 0:128], small).astype(BF)

    barrier = pltpu.get_barrier_semaphore()
    for to in (*zdev[1:], xdev, ydev, cdev):
        pl.semaphore_signal(barrier, inc=1, device_id=to, device_id_type=MESH)
    pl.semaphore_wait(barrier, 6)

    def weight(t, *index):
        if t < 7:
            return wA.at[(t, *index)]
        if t in DOWN:
            return wD.at[(pl.ds(*DOWN[t]), *index)]
        return (wO if t == 11 else pk).at[index]

    def z_view(t, zz):
        return weight(t, zz, x, c, y) if t in (11, 12) else weight(t, zz, x, c)

    def y_view(t):
        return wO.at[:, :, c, y] if t == 11 else pk.at[:, :, c, y]

    def c_view(t):
        return weight(t, slice(None), slice(None), c)

    def y0_full(t):
        view = wA.at[t, z, x, c, my_rows]
        return rc(view, view, ysend.at[t], yrecv.at[t], ydev)

    def start_y0(t):
        if t < 3:
            rc(w_qkv.at[:, part_cols(t, oy)], wA.at[t, z, x, c, my_rows], ysend.at[t], yrecv.at[t], ydev).start()
        else:
            for i in range(4):
                rc(w_up.at[:, up_cols(t - 3, i, oy)], wA.at[t, z, x, c, my_rows, pl.ds(i * 128, 128)],
                   ysend.at[t], yrecv.at[t], ydev).start()
        pending.append((None, y0_full(t)))

    def x_copy(t, j):
        view = z_view(t, z_of[j])
        return rc(view, view, xsend.at[t, j], xrecv.at[t, j], xdev)

    def pair_view(t, zz):
        return weight(t, zz, slice(None), c)

    def z_copy(t, j):
        view = pair_view(t, z) if t in GATHER_X_FIRST else z_view(t, z)
        return rc(view, view, zsend.at[t, j], zrecv.at[t, j], zdev[j])

    far = jnp.where(z == 1, 0, 3)
    far_sem = jnp.where(z == 1, 1, 3)

    def start_z(t):
        if t != 12:
            view = wA.at[t, z, x, c, my_rows] if t < 7 else z_view(t, z)
            lc(view, view, lsem.at[t]).wait()
        if t < 7:
            y0_full(t).wait_recv()
        if t not in GATHER_X_FIRST:
            for j in (2, 1, 3):
                send(z_copy(t, j), z_direct[j])
        send(x_copy(t, 0))

    def to_far(t, view):
        send(rc(view, view, zsend.at[t, 0], zrecv.at[t, far_sem], dev(far, x, c, y)), middle)

    def forward(t):
        if t in GATHER_X_FIRST:
            x_copy(t, 0).wait_recv()
            for j in (2, 1, 3):
                send(z_copy(t, j), z_direct[j])
        else:
            z_copy(t, 2).wait_recv()
            to_far(t, z_view(t, z_of[2]))
            send(x_copy(t, 2))

    def start_x(t):
        if t in GATHER_X_FIRST:
            z_copy(t, 2).wait_recv()
            to_far(t, pair_view(t, z_of[2]))
        else:
            for j in (1, 3):
                z_copy(t, j).wait_recv()
                send(x_copy(t, j))

    def x_done(t):
        if t in GATHER_X_FIRST:
            for j in (1, 3):
                z_copy(t, j).wait_recv()
        else:
            for j in range(4):
                x_copy(t, j).wait_recv()

    def y_copy(t):
        return rc(y_view(t), y_view(t), ysend.at[t - 4], yrecv.at[t - 4], ydev)

    def start_y(t):
        x_done(t)
        send(y_copy(t))

    def c_copy(t):
        return rc(c_view(t), c_view(t), csend.at[t], crecv.at[t], cdev)

    def start_c(t):
        if t not in (11, 12):
            x_done(t)
        else:
            y_copy(t).wait_recv()
        send(c_copy(t))

    def ready(t):
        c_copy(t).wait_recv()

    for t in range(14):
        if t < 7:
            task(start_y0, (DO_Y0, t), t)
        task(start_z, (DO_Z, t), t)
        task(forward, (DO_F, t), t)
        task(start_x, (DO_X, t), t)
        if t in (11, 12):
            task(start_y, (DO_Y, t), t)
        task(start_c, (DO_C, t), t)

    tok_copy = rc(tokens, tokg.at[y], msend.at[0], mrecv.at[0], ydev)
    task(send, (DO_TOK,), tok_copy)

    first_end = seq[0, 0]
    second_end = first_end + seq[0, 1]

    def segment(pos):
        return (pos >= first_end).astype(jnp.int32) + (pos >= second_end).astype(jnp.int32)

    def mask_rows(i, _):
        rows = pl.ds(pl.multiple_of(i * 128, 128), 128)
        qpos = i * 128 + lax.broadcasted_iota(jnp.int32, (128, 512), 0)
        kpos = lax.broadcasted_iota(jnp.int32, (128, 512), 1)
        good = (segment(qpos) == segment(kpos)) & (kpos <= qpos)
        mask[rows, :] = jnp.where(good, 0.0, NEG).astype(BF)
        return 0

    def make_mask():
        lax.fori_loop(0, 4, mask_rows, 0)

    task(make_mask, (DO_MASK,))

    def make_columns():
        wide = jnp.concatenate([targets[...].astype(F32), p_lm[...], jnp.zeros((6, 256), F32)], 0)
        cols = jnp.transpose(wide)
        tcol[...] = cols[:, 0:1]
        pcol[...] = cols[:, 1:2]
        lc(gD, gD, kn_sem.at[0]).wait()
        lc(head_grad, hgrad, kn_sem.at[1]).wait()

    task(make_columns, (DO_COLS,))

    def keys_of(s):
        return jnp.concatenate([gD[h, s // 4, (s // 2) % 2, s % 2] for h in range(8)], 1)

    def make_table(b):
        eye = lax.broadcasted_iota(jnp.int32, (128, 128), 0) == lax.broadcasted_iota(jnp.int32, (128, 128), 1)
        slot = lax.broadcasted_iota(jnp.int32, (16, 128), 1)
        for s in range(b * 4, b * 4 + 4):
            rows = slice(s * 16, s * 16 + 16)
            kk = keys_of(s)
            square = jnp.broadcast_to(col_sum(jnp.where(eye, dot(kk, kk, 1, 1), 0.0)), (16, 128))
            ksq[rows, :] = jnp.where(slot < counts[0, s], square * -KNN_SCALE, NEG)
            match[rows, :] = jnp.where(ids[s : s + 1, :].astype(F32) == tcol[rows, :], 1.0, 0.0)

    for b in range(4):
        task(make_table, (DO_TABLE, b), b)

    def unpack():
        ready(12)
        for g in range(8):
            total = None
            for i in range(4):
                piece = pk[g // 2, g % 2, i // 2, i % 2].astype(F32)
                total = piece if total is None else total + piece
            prm[:, g * 128 : (g + 1) * 128] = total
        for d in range(16):
            piece = pk[d // 4, (d // 2) % 2, d % 2, y].astype(F32)
            ubias[0:1, d * 128 : (d + 1) * 128] = piece[10:11, :]

    task(unpack, (DO_UNPACK,))

    def row(r):
        return prm[r : r + 1, :]

    def norm_in(half):
        def rows_of(i, _):
            rows = pl.ds(pl.multiple_of(i * 64, 64), 64)
            unit, _inv = unit_of(tokg[half, rows, :].astype(F32))
            ni[half, rows, :] = (unit * row(0) + row(3)).astype(BF)
            return 0

        lax.fori_loop(0, 4, rows_of, 0)

    def norm_own():
        lc(tokens, tokg.at[y], lsem.at[14]).wait()
        norm_in(y)

    def norm_other():
        tok_copy.wait_recv()
        norm_in(oy)

    task(norm_own, (DO_NORMOWN,))
    task(norm_other, (DO_NORMOTHER,))

    head_cols = pl.ds(pl.multiple_of(y * 512, 512), 512)

    def project(s, own):
        if own:
            ready(s)
        half = y if own else oy
        value = dot(ni[half], wA[s].reshape(1024, 512))
        if s != 1:
            value = value + prm[6 + s // 2 : 7 + s // 2, head_cols]
        qkv[s, half] = value.astype(BF)

    for s in range(3):
        task(project, (DO_PROJ, s, 0), s, True)
        task(project, (DO_PROJ, s, 1), s, False)

    lane = lax.broadcasted_iota(jnp.int32, (1, 128), 1)
    in_head = [lane < 64, lane >= 64]

    def probs_of(qe, k2, half):
        nk = 256 * (half + 1)
        s = dot(qe, k2[:nk], 1, 1) * 0.125 + mask[half * 256 : half * 256 + 256, :nk].astype(F32)
        ex = jnp.exp(s - jnp.max(s, -1, keepdims=True))
        return ex * (1.0 / jnp.sum(ex, -1, keepdims=True))

    def attend(p):
        cols = slice(p * 128, p * 128 + 128)
        q2 = qkv[0, :, :, cols]
        k2 = qkv[1, :, :, cols].reshape(512, 128)
        v2 = qkv[2, :, :, cols].reshape(512, 128)
        for half in range(2):
            nk = 256 * (half + 1)
            outs = []
            for e in range(2):
                qe = jnp.where(in_head[e], q2[half], jnp.zeros_like(q2[half]))
                outs.append(dot(probs_of(qe, k2, half).astype(BF), v2[:nk]))
            att[half, :, pair_cols(p)] = jnp.where(in_head[0], outs[0], outs[1]).astype(BF)
        send(att_copy(p))

    def pair_cols(p):
        return pl.ds(pl.multiple_of(y * 512 + p * 128, 128), 128)

    def att_copy(p):
        view = att.at[:, :, pair_cols(p)]
        return rc(view, view, asend.at[p], arecv.at[p], ydev)

    for p in range(4):
        task(attend, (DO_ATTEND, p), p)

    def attention_out(half):
        if half == 0:
            for p in range(4):
                att_copy(p).wait_recv()
            ready(11)
        h1[half] = dot(att[half], wO[...].reshape(1024, 1024)) + row(8)

    def norm_mid(half):
        def rows_of(k, _):
            rows = pl.ds(pl.multiple_of(k * 64, 64), 64)
            value = h1[half, rows, :] + tokg[half, rows, :].astype(F32)
            h1[half, rows, :] = value
            unit, _inv = unit_of(value)
            nmg[half, rows, :] = (unit * row(1) + row(4)).astype(BF)
            return 0

        lax.fori_loop(0, 4, rows_of, 0)

    for half in range(2):
        task(attention_out, (DO_ATTOUT, half), half)
        task(norm_mid, (DO_NORMMID, half), half)

    def up(j, half):
        if half == 0:
            ready(3 + j)
        cols = slice(j * 512, (j + 1) * 512)
        u = dot(nmg[half], wA[3 + j].reshape(1024, 512)) + ubias[0:1, cols]
        value, dvalue = gelu_pair(u)
        gelu[half, :, cols] = value.astype(BF)
        slope[half, :, cols] = dvalue.astype(BF)

    for j in range(4):
        task(up, (DO_UP, j, 0), j, 0)
        task(up, (DO_UP, j, 1), j, 1)

    def part_copy(t):
        cols = pl.ds(DOWN[t][0] * 128, DOWN[t][1] * 128)
        sem = list(DOWN).index(t)
        return rc(sendb.at[:, cols], prec.at[:, cols], psend.at[sem], precv.at[sem], ydev)

    def down_weight(first, count):
        return jnp.concatenate([wD[h].reshape(2048, 128) for h in range(first, first + count)], 1)

    def down(t):
        ready(t)
        first, count = DOWN[t]
        cols = slice(first * 128, (first + count) * 128)
        right = down_weight(first, count)
        sendb[:, cols] = dot(gelu[oy], right).astype(BF)
        send(part_copy(t))
        st[:, cols] = dot(gelu[y], right) + (h1[y, :, cols] + prm[9:10, cols])

    for t in DOWN:
        task(down, (DO_DOWN, t), t)

    def add_row(r, value):
        pg[r : r + 1, :] = pg[r : r + 1, :] + value

    def ds_copy(j, b):
        rows = pl.ds(b * 128, 128) if j < 2 else pl.ds(0, 256)
        cols = pl.ds(j * 128, 128) if j < 2 else pl.ds((j - 1) * 256, 256)
        view = dsg.at[y, rows, cols]
        sem = 2 * j + b if j < 2 else 2 + j
        return rc(view, view, dsend.at[sem], drecv.at[sem], ydev)

    ds_waited = []

    def need_ds(*columns):
        for j in columns:
            if j not in ds_waited:
                ds_waited.append(j)
                for b in range(2 if j < 2 else 1):
                    ds_copy(j, b).wait_recv()

    def neighbours(b):
        if b == 0:
            pg[...] = jnp.zeros_like(pg)
            for t in DOWN:
                part_copy(t).wait_recv()
        rows = slice(b * 128, b * 128 + 128)
        value = st[rows, :] + prec[rows, :].astype(F32)
        unit, inv = unit_of(value)
        query = (unit * row(2) + row(5)).astype(BF)
        raw = jnp.concatenate(
            [dot(query[i * 16 : i * 16 + 16], keys_of(b * 8 + i), 1, 1) for i in range(8)], 0
        )
        logits = (2.0 * KNN_SCALE) * raw + ksq[rows, :]
        ex = jnp.exp(logits - jnp.max(logits, -1, keepdims=True))
        weights = ex / jnp.sum(ex, -1, keepdims=True)
        same = match[rows, :]
        knn_prob = jnp.sum(same * weights, -1, keepdims=True)
        mixture = MIX_WEIGHT * knn_prob + (1.0 - MIX_WEIGHT) * pcol[rows, :]
        lcol[rows, :] = -jnp.log(mixture)
        dlog = (-(MIX_WEIGHT / mixture) * weights * (same - knn_prob)).astype(BF)
        kgrad = jnp.concatenate(
            [dot(dlog[i * 16 : i * 16 + 16], keys_of(b * 8 + i)) for i in range(8)], 0
        )
        dquery = hgrad[rows, :].astype(F32) + kgrad * (2.0 * KNN_SCALE)
        hgrad[rows, :] = value.astype(BF)
        add_row(2, col_sum(dquery * unit))
        add_row(5, col_sum(dquery))
        dvalue = ln_back(dquery, unit, inv, row(2))
        st[rows, :] = dvalue
        low = dvalue.astype(BF)
        add_row(9, col_sum(low.astype(F32)))
        dsg[y, rows, :] = low
        send(ds_copy(0, b))
        send(ds_copy(1, b))

    for b in range(2):
        task(neighbours, (DO_KNN, b), b)

    out_state = lc(hgrad, state_out, osem.at[0])

    def state_done():
        out_state.start()
        lossb[...] = jnp.transpose(jnp.broadcast_to(lcol[...], (256, 128)))[0:1, :]
        cp = lc(lossb, loss_out, osem.at[1])
        cp.start()
        finals.append(cp)

    task(state_done, (DO_STATEOUT,))

    def ds_rest():
        send(ds_copy(2, 0))
        send(ds_copy(3, 0))
        send(ds_copy(4, 0))

    task(ds_rest, (DO_DSREST,))

    slot_of = {3: 0, 4: 1, 5: 2, 6: 3, 0: 0, 1: 1, 2: 2}

    every = slice(None)

    def pick(refs, t, *index):
        if t < 7:
            return refs[0].at[(slot_of[t] if refs[0] is gA else t, *index)]
        if t in DOWN:
            return refs[1].at[(pl.ds(*DOWN[t]), *index)]
        return refs[2 if t == 11 else 3].at[index]

    g_refs = (gA, gD, gO, gP)
    c_refs = (dRA, dRD, dRO, dRP)
    y_refs = (None, None, yRO, yRP)
    x_refs = (xRA, xRD, xRO, xRP)
    z_refs = (zRA, zRD, zRO, zRP)

    def g_at(t, zz, xx):
        return pick(g_refs, t, zz, xx, c, y) if t in (11, 12) else pick(g_refs, t, zz, xx, c)

    def rs_c(t):
        return rc(pick(g_refs, t, every, every, oc), pick(c_refs, t, every), rcs.at[t], rcr.at[t], cdev)

    def rs_y(t):
        return rc(pick(g_refs, t, every, every, c, oy), pick(y_refs, t, every), rys.at[t], ryr.at[t], ydev)

    def x_one(t):
        k = REDUCE_Z_FIRST.index(t)
        return xOA.at[k] if t < 7 else xOD.at[k, pl.ds(0, DOWN[t][1])]

    def rs_x(t):
        if t in REDUCE_Z_FIRST:
            return rc(g_at(t, z, ox), x_one(t), rxs.at[t], rxr.at[t], xdev)
        return rc(g_at(t, every, ox), pick(x_refs, t, every), rxs.at[t], rxr.at[t], xdev)

    def z_block(t, zz):
        return g_at(t, zz, every if t in REDUCE_Z_FIRST else x)

    def z_slot(t, j):
        if t in REDUCE_Z_FIRST:
            return pick((x_refs, z_refs)[j // 2], t, pl.ds(2 * (j % 2), 2))
        return pick(z_refs, t, j)

    def rs_z(t, j):
        return rc(z_block(t, z_to[j]), z_slot(t, j), rzs.at[t, j], rzr.at[t, j], zdev[j])

    end_block = jnp.where(z == 0, 3, 0)
    end_to = dev(jnp.where(z == 0, 1, 2), x, c, y)
    is_end = (z == 0) | (z == 3)

    def rs_end(t):
        return rc(z_block(t, end_block), z_slot(t, 0), rzs.at[t, 0], rzr.at[t, 0], end_to)

    def add_to(ref, other):
        ref[...] = (ref[...].astype(F32) + other.astype(F32)).astype(ref.dtype)

    def rs_after_c(t):
        rs_c(t).wait_recv()
        for i in range(4):
            add_to(pick(g_refs, t, i, every, c), pick(c_refs, t, i)[...])
        if t in REDUCE_Z_FIRST:
            start_zs(t)
        else:
            (rs_y(t) if t in (11, 12) else rs_x(t)).start()

    def rs_after_y(t):
        rs_y(t).wait_recv()
        for i in range(4):
            add_to(pick(g_refs, t, i, every, c, y), pick(y_refs, t, i)[...])
        rs_x(t).start()

    def start_zs(t):
        when(is_end, rs_end(t).start)
        when(z_direct[1], rs_z(t, 1).start)
        when(z_direct[3], rs_z(t, 3).start)
        when(is_end, rs_z(t, 2).start)

    def z_arrived(t):
        rs_z(t, 2).wait_recv()
        pl.when(z != 0)(rs_z(t, 1).wait_recv)
        pl.when(z != 3)(rs_z(t, 3).wait_recv)

    def rs_after_x(t):
        if t in REDUCE_Z_FIRST:
            z_arrived(t)

            def add(*slots):
                total = g_at(t, z, every)[...].astype(F32)
                for j in slots:
                    total = total + z_slot(t, j)[...].astype(F32)
                g_at(t, z, every)[...] = total.astype(BF)

            pl.when(z == 0)(functools.partial(add, 2, 3))
            pl.when(z == 3)(functools.partial(add, 2, 1))
            pl.when(middle)(functools.partial(add, 2, 1, 3))
            rs_x(t).start()
        else:
            rs_x(t).wait_recv()
            for i in range(4):
                add_to(g_at(t, i, x), pick(x_refs, t, i)[...])
            start_zs(t)

    def rs_forward(t):
        def go():
            rs_end(t).wait_recv()
            add_to(z_block(t, z_to[2]), z_slot(t, 0)[...])
            rs_z(t, 2).start()

        pl.when(middle)(go)

    def rs_sends(t):
        out = [(None, rs_c(t)), (None, rs_x(t)), (None, rs_z(t, 2))]
        if t in (11, 12):
            out.append((None, rs_y(t)))
        return out + [(z_direct[1], rs_z(t, 1)), (z_direct[3], rs_z(t, 3)), (is_end, rs_end(t))]

    def out_cols(t, yy):
        if t < 3:
            return [(gqkv_out, part_cols(t, yy), pl.ds(0, 512))]
        return [(gup_out, up_cols(t - 3, i, yy), pl.ds(i * 128, 128)) for i in range(4)]

    def rs_finish(t):
        if t < 7:
            fin = finA.at[t]
        elif t in DOWN:
            fin = finD.at[pl.ds(*DOWN[t])]
        else:
            fin = finO if t == 11 else finP
        own = g_at(t, z, x)
        if t in REDUCE_Z_FIRST:
            rs_x(t).wait_recv()
            total = own[...].astype(F32) + x_one(t)[...].astype(F32)
            fin[...] = total.reshape(fin.shape)
        else:
            z_arrived(t)
            near = jnp.where(z == 0, 3, 1)
            total = own[...].astype(F32)
            for j in (2, near):
                total = total + pick(z_refs, t, j)[...].astype(F32)
            fin[...] = total.reshape(fin.shape)

            def third():
                fin[...] = fin[...] + pick(z_refs, t, 3)[...].astype(F32).reshape(fin.shape)

            pl.when(middle)(third)
        if t not in (3, 4, 5):
            pending.extend(rs_sends(t))
        if t < 7:
            for ref, cols, inner in out_cols(t, y):
                lc(finA.at[t, y, :, inner], ref.at[:, cols], rfl.at[t]).start()
                rc(finA.at[t, oy, :, inner], ref.at[:, cols], rys.at[t], ryr.at[t], ydev).start()
            full = finA.at[t, y]
            finals.append(lc(full, full, rfl.at[t]))
            both = rc(full, full, rys.at[t], ryr.at[t], ydev)
            pending.append((None, both))
            late_recv.append(both)
        else:
            if t in DOWN:
                for h in range(DOWN[t][0], sum(DOWN[t])):
                    lc(finD.at[h], gdown_out.at[:, pl.ds(h * 128, 128)], rfl.at[t]).start()
                finals.append(lc(fin, fin, rfl.at[t]))
            else:
                cp = lc(fin, gout_out if t == 11 else gpk_out, rfl.at[t])
                cp.start()
                finals.append(cp)

    for t in range(14):
        task(rs_after_c, (DO_RC, t), t)
        if t in (11, 12):
            task(rs_after_y, (DO_RY, t), t)
        task(rs_after_x, (DO_RX, t), t)
        task(rs_forward, (DO_RF, t), t)
        task(rs_finish, (DO_RZ, t), t)

    def make_down(t):
        first, count = DOWN[t]
        need_ds(first if first < 2 else first // 2 + 1)
        ds_cols = dsg[:, :, first * 128 : (first + count) * 128].reshape(512, count * 128)
        for i in range(4):
            part = gelu[:, :, i * 512 : (i + 1) * 512].reshape(512, 512)
            value = dot(part, ds_cols, 0, 0).astype(BF)
            for k in range(count):
                gD[first + k, i] = value[:, k * 128 : (k + 1) * 128].reshape(2, 2, 128, 128)
        rs_c(t).start()

    for t in DOWN:
        task(make_down, (DO_GD, t), t)

    def make_a(t, left, right):
        for i in range(4):
            part = left[:, :, i * 256 : (i + 1) * 256].reshape(512, 256)
            gA[slot_of[t], i] = dot(part, right, 0, 0).astype(BF).reshape(2, 2, 64, 512)
        rs_c(t).start()

    dub_started = []

    def make_dpre(i, own):
        if not own:
            need_ds(0, 1, 2, 3, 4)
        half = y if own else oy
        cols = slice(i * 512, (i + 1) * 512)
        acc = None
        for j in range(4):
            right = jnp.concatenate([wD[2 * j + k, i].reshape(512, 128) for k in range(2)], 1)
            part = dot(dsg[half, :, j * 256 : (j + 1) * 256], right, 1, 1)
            acc = part if acc is None else acc + part
        low = (acc * slope[half, :, cols].astype(F32)).astype(BF)
        slope[half, :, cols] = low
        total = col_sum(low.astype(F32))
        if i in dub_started:
            total = total + dub[0:1, cols]
        dub_started.append(i)
        dub[0:1, cols] = total

    def up_grad(j):
        make_a(3 + j, nmg, slope[:, :, j * 512 : (j + 1) * 512].reshape(512, 512))

    for j in range(4):
        task(make_dpre, (DO_DP, j, 0), j, True)
        task(make_dpre, (DO_DP, j, 1), j, False)
        task(up_grad, (DO_GU, j), j)

    def dnorm_mid(half, n):
        acc = None
        for j in range(4):
            part = dot(slope[half, :, j * 512 : (j + 1) * 512], wA[3 + j, n].reshape(256, 512), 1, 1)
            acc = part if acc is None else acc + part
        dh[half, :, n * 256 : (n + 1) * 256] = acc

    for n in range(4):
        task(dnorm_mid, (DO_DNO, n), oy, n)
        task(dnorm_mid, (DO_DNS, n), y, n)

    zero_row = jnp.zeros((1, 1024), F32)

    def back_mid(own):
        half = y if own else oy

        def rows_of(i, carry):
            a, b, d = carry
            rows = pl.ds(pl.multiple_of(i * 64, 64), 64)
            dy = dh[half, rows, :]
            unit, inv = unit_of(h1[half, rows, :])
            total = ln_back(dy, unit, inv, row(1))
            if own:
                total = total + st[rows, :]
            dh[half, rows, :] = total
            low = total.astype(BF)
            dhl[half, rows, :] = low
            return a + col_sum(dy * unit), b + col_sum(dy), d + col_sum(low.astype(F32))

        a, b, d = lax.fori_loop(0, 4, rows_of, (zero_row, zero_row, zero_row))
        add_row(1, a)
        add_row(4, b)
        add_row(8, d)

    task(back_mid, (DO_BACKMID, 0), True)
    task(back_mid, (DO_BACKMID, 1), False)

    def datt(yy, p):
        right = wO[2 * yy + p // 2, p % 2].reshape(128, 1024)
        return dot(dhl[...].reshape(512, 1024), right, 1, 1).reshape(2, 256, 128)

    def da_copy(p):
        cols = pl.ds(p * 128, 128)
        return rc(das.at[:, :, cols], dattg.at[:, :, cols], dsend.at[7 + p], drecv.at[7 + p], ydev)

    def datt_other(p):
        das[:, :, p * 128 : (p + 1) * 128] = datt(oy, p).astype(BF)
        send(da_copy(p))

    for p in range(4):
        task(datt_other, (DO_DAO, p), p)

    def out_grad():
        for i in range(4):
            part = att[:, :, i * 256 : (i + 1) * 256].reshape(512, 256)
            gO[i] = dot(part, dhl[...].reshape(512, 1024), 0, 0).astype(BF).reshape(2, 2, 2, 32, 1024)
        rs_c(11).start()

    task(out_grad, (DO_GO,))

    dqkv = qkv

    def attend_back(p):
        da_copy(p).wait_recv()
        cols = slice(p * 128, p * 128 + 128)
        q2 = qkv[0, :, :, cols]
        k2 = qkv[1, :, :, cols].reshape(512, 128)
        v2 = qkv[2, :, :, cols].reshape(512, 128)
        do2 = (datt(y, p) + dattg[:, :, cols].astype(F32)).astype(BF)
        zero = jnp.zeros((512, 128), BF)
        dks = [None, None]
        dvs = [None, None]
        for half in range(2):
            nk = 256 * (half + 1)
            dq = None
            for e in range(2):
                qe = jnp.where(in_head[e], q2[half], zero[:256])
                doe = jnp.where(in_head[e], do2[half], zero[:256])
                ke = jnp.where(in_head[e], k2[:nk], zero[:nk])
                probs = probs_of(qe, k2, half)
                dprob = dot(doe, v2[:nk], 1, 1)
                delta = jnp.sum(probs * dprob, -1, keepdims=True)
                ds = (probs * (dprob - delta)).astype(BF)
                part = dot(ds, ke)
                dq = part if dq is None else dq + part
                dk = dot(ds, qe, 0, 0)
                dv = dot(probs.astype(BF), doe, 0, 0)
                for kb in range(half + 1):
                    rows = slice(kb * 256, kb * 256 + 256)
                    dks[kb] = dk[rows] if dks[kb] is None else dks[kb] + dk[rows]
                    dvs[kb] = dv[rows] if dvs[kb] is None else dvs[kb] + dv[rows]
            dqkv[0, half, :, cols] = (dq * 0.125).astype(BF)
        for kb in range(2):
            dqkv[1, kb, :, cols] = (dks[kb] * 0.125).astype(BF)
            dqkv[2, kb, :, cols] = dvs[kb].astype(BF)

    for p in range(4):
        task(attend_back, (DO_AB, p), p)

    def qkv_grad(s):
        for cond, cp in rs_sends(3 + s):
            when(cond, cp.wait_send)
        make_a(s, ni, dqkv[s].reshape(512, 512))

    for s in range(3):
        task(qkv_grad, (DO_GQ, s), s)

    def di_copy(i):
        rows = pl.ds(i * 128, 128)
        return rc(prec.at[rows], dnr2.at[rows], msend.at[1 + i], mrecv.at[1 + i], ydev)

    def dnorm_in(own):
        half = y if own else oy
        for n in range(4):
            acc = None
            for s in range(3):
                part = dot(dqkv[s, half], wA[s, n].reshape(256, 512), 1, 1)
                acc = part if acc is None else acc + part
            st[:, n * 256 : (n + 1) * 256] = acc

    def back_in(own, i):
        half = y if own else oy

        def rows_of(k, carry):
            a, b = carry
            rows = pl.ds(pl.multiple_of(k * 64, 64), 64)
            dy = st[rows, :]
            unit, inv = unit_of(tokg[half, rows, :].astype(F32))
            total = dh[half, rows, :] + ln_back(dy, unit, inv, row(0))
            if own:
                dh[half, rows, :] = total
            else:
                prec[rows, :] = total.astype(BF)
            return a + col_sum(dy * unit), b + col_sum(dy)

        a, b = lax.fori_loop(2 * i, 2 * i + 2, rows_of, (zero_row, zero_row))
        add_row(0, a)
        add_row(3, b)
        if not own:
            send(di_copy(i))

    task(dnorm_in, (DO_DIO,), False)
    task(dnorm_in, (DO_DIS,), True)
    for i in range(2):
        task(back_in, (DO_BIO, i), False, i)
        task(back_in, (DO_BIS, i), True, i)

    gin_started = []

    def grad_in(i):
        di_copy(i).wait_recv()
        if not gin_started:
            out_state.wait()
        gin_started.append(i)
        rows = slice(i * 128, i * 128 + 128)
        hgrad[rows, :] = (dh[y, rows, :] + dnr2[rows, :].astype(F32)).astype(BF)
        cp = lc(hgrad.at[pl.ds(i * 128, 128)], gin_out.at[pl.ds(i * 128, 128)], osem.at[2 + i])
        cp.start()
        finals.append(cp)

    for i in range(2):
        task(grad_in, (DO_GIN, i), i)

    def small_grads():
        pg[6:7, head_cols] = col_sum(dqkv[0].reshape(512, 512).astype(F32))
        pg[7:8, head_cols] = col_sum(dqkv[2].reshape(512, 512).astype(F32))
        for d in range(32):
            piece = pg[:, (d // 4) * 128 : (d // 4) * 128 + 128]
            mine = jnp.where(y == d % 2, dub[0:1, (d // 2) * 128 : (d // 2) * 128 + 128], 0.0)
            gP[d // 8, (d // 4) % 2, (d // 2) % 2, d % 2] = jnp.where(row_id == 10, mine, piece)
        rs_c(12).start()

    task(small_grads, (DO_GP,))

    for name in ORDER:
        tasks.pop(name)()
    assert not tasks, sorted(tasks)
    for cp in late_recv:
        cp.wait_recv()
    for cond, cp in pending:
        when(cond, cp.wait_send)
    for cp in finals:
        cp.wait()


def finish_kernel(state, loss, gin, gqkv, gout, gup, gdown, gpk, *refs):
    outs, held, (sem, out_sem) = refs[:11], refs[11:18], refs[18:]
    big = [(state, 0), (loss, 1), (gin, 2), (gqkv, 3), (gout, 4), (gup, 5), (gdown, 6)]
    copies = [pltpu.make_async_copy(src, held[i], sem.at[i]) for src, i in big]
    for cp in copies:
        cp.start()
    quarter = (2 * lax.axis_index("dp") + lax.axis_index("fsdp")) % 4
    total = gpk[...]
    mine = pltpu.roll(total, ((4 - quarter) % 4) * 32, 1)
    outs[7][...] = mine[0:3, 0:32]
    outs[8][...] = mine[3:6, 0:32]
    outs[9][...] = mine[6:10, 0:32]
    outs[10][...] = total[10:11, :]
    results = [pltpu.make_async_copy(held[i], outs[i], out_sem.at[i]) for _, i in big]
    for cp, result in zip(copies, results):
        cp.wait()
        result.start()
    for result in results:
        result.wait()


SCRATCH = dict(
    wA=((7, 4, 2, 2, 64, 512), BF), wD=((8, 4, 2, 2, 128, 128), BF), wO=((4, 2, 2, 2, 32, 1024), BF),
    pk=((4, 2, 2, 2, 16, 128), BF), prm=((16, 1024), F32), ubias=((8, 2048), F32),
    tokg=((2, 256, 1024), BF), ni=((2, 256, 1024), BF), qkv=((3, 2, 256, 512), BF), mask=((512, 512), BF),
    att=((2, 256, 1024), BF), h1=((2, 256, 1024), F32), nmg=((2, 256, 1024), BF),
    gelu=((2, 256, 2048), BF), slope=((2, 256, 2048), BF), st=((256, 1024), F32), prec=((256, 1024), BF),
    hgrad=((256, 1024), BF), ksq=((256, 128), F32), match=((256, 128), F32), dsg=((2, 256, 1024), BF),
    tcol=((256, 1), F32), pcol=((256, 1), F32), lcol=((256, 1), F32), lossb=((1, 256), F32),
    dh=((2, 256, 1024), F32), dhl=((2, 256, 1024), BF), das=((2, 256, 512), BF), dattg=((2, 256, 512), BF),
    dnr2=((256, 1024), BF), sendb=((256, 1024), BF),
    gA=((4, 4, 2, 2, 64, 512), BF), gD=((8, 4, 2, 2, 128, 128), BF), gO=((4, 2, 2, 2, 32, 1024), BF),
    gP=((4, 2, 2, 2, 16, 128), F32),
    dRA=((7, 4, 2, 64, 512), BF), xRA=((7, 4, 64, 512), BF), zRA=((7, 4, 64, 512), BF),
    dRD=((8, 4, 2, 128, 128), BF), xRD=((8, 4, 128, 128), BF), zRD=((8, 4, 128, 128), BF),
    dRO=((4, 2, 2, 32, 1024), BF), yRO=((4, 2, 32, 1024), BF), xRO=((4, 32, 1024), BF), zRO=((4, 32, 1024), BF),
    dRP=((4, 2, 2, 16, 128), F32), yRP=((4, 2, 16, 128), F32), xRP=((4, 16, 128), F32), zRP=((4, 16, 128), F32),
    finA=((7, 2, 32, 512), F32), finD=((8, 128, 128), F32), finO=((32, 1024), F32), finP=((16, 128), F32),
    xOA=((3, 64, 512), BF), xOD=((3, 2, 128, 128), BF), pg=((16, 1024), F32), dub=((8, 2048), F32),
)
SEMS = dict(
    lsem=(15,), ysend=(9,), yrecv=(9,), zsend=(14, 4), zrecv=(14, 4), xsend=(14, 4), xrecv=(14, 4),
    csend=(14,), crecv=(14,), osem=(4,), msend=(3,), mrecv=(3,), asend=(4,), arecv=(4,),
    dsend=(11,), drecv=(11,), psend=(5,), precv=(5,), rcs=(14,), rcr=(14,), rxs=(14,), rxr=(14,),
    rzs=(14, 4), rzr=(14, 4), rys=(14,), ryr=(14,), rfl=(14,), kn_sem=(2,),
)


def on_device_fused(
    tokens, head_grad, w_qkv, w_out, w_up, w_down, gains, shifts, biases, up_bias, seq_lengths,
    neigh_keys, neigh_ids, neigh_counts, targets, p_lm,
):
    keys = neigh_keys.reshape(4, 2, 2, 128, 1024)
    anywhere = pl.BlockSpec(memory_space=pl.ANY)
    vmem = pl.BlockSpec(memory_space=pltpu.VMEM)
    smem = pl.BlockSpec(memory_space=pltpu.SMEM)
    shape = jax.ShapeDtypeStruct
    results = [
        shape((256, 1024), BF),
        shape((1, 256), F32),
        shape((256, 1024), BF),
        shape((32, 3072), F32),
        shape((32, 1024), F32),
        shape((32, 4096), F32),
        shape((128, 1024), F32),
    ]
    held = pl.pallas_call(
        block_kernel,
        out_shape=results + [shape((16, 128), F32)],
        in_specs=[anywhere] * 6 + [vmem] * 4 + [smem, smem, anywhere, vmem, vmem, vmem],
        out_specs=[anywhere] * 8,
        scratch_shapes=[pltpu.VMEM(*SCRATCH[k]) for k in SCRATCH]
        + [pltpu.SemaphoreType.DMA(SEMS[k]) for k in SEMS],
        compiler_params=pltpu.CompilerParams(
            collective_id=0, has_side_effects=True, vmem_limit_bytes=VMEM_LIMIT
        ),
        name="block",
    )(
        tokens, head_grad, w_qkv, w_out, w_up, w_down, gains, shifts, biases, up_bias.reshape(1, 128),
        seq_lengths, neigh_counts.reshape(1, 16), keys, neigh_ids, targets.reshape(1, 256),
        p_lm.reshape(1, 256),
    )
    small = [shape((3, 32), F32), shape((3, 32), F32), shape((4, 32), F32), shape((1, 128), F32)]
    res = pl.pallas_call(
        finish_kernel,
        out_shape=results + small,
        in_specs=[anywhere] * 7 + [vmem],
        out_specs=[anywhere] * 7 + [vmem] * 4,
        scratch_shapes=[pltpu.VMEM(r.shape, r.dtype) for r in results]
        + [pltpu.SemaphoreType.DMA((7,)), pltpu.SemaphoreType.DMA((7,))],
        name="finish",
    )(*held)
    state, loss, gin, gqkv, gout, gup, gdown, dgains, dshifts, dbiases, dub = res
    return (
        state, loss.reshape(256), gin, gqkv, gout, gup, gdown, dgains, dshifts, dbiases, dub.reshape(128),
    )


def solution(mesh):
    in_specs = (
        P(("dp", "fsdp"), None),
        P(("dp", "fsdp"), None),
        P(("dp", "fsdp"), None),
        P(("dp", "fsdp"), None),
        P(("dp", "fsdp"), None),
        P(("dp", "fsdp"), None),
        P(None, ("dp", "fsdp")),
        P(None, ("dp", "fsdp")),
        P(None, ("dp", "fsdp")),
        P(("dp", "fsdp")),
        P("dp", None),
        P(("dp", "fsdp"), None, None),
        P(("dp", "fsdp"), None),
        P(("dp", "fsdp")),
        P(("dp", "fsdp")),
        P(("dp", "fsdp")),
    )
    out_specs = (
        P(("dp", "fsdp"), None),
        P(("dp", "fsdp")),
        P(("dp", "fsdp"), None),
        P(("dp", "fsdp"), None),
        P(("dp", "fsdp"), None),
        P(("dp", "fsdp"), None),
        P(("dp", "fsdp"), None),
        P(None, ("dp", "fsdp")),
        P(None, ("dp", "fsdp")),
        P(None, ("dp", "fsdp")),
        P(("dp", "fsdp")),
    )
    fused = mesh.shape["dp"] == 16 and mesh.shape["fsdp"] == 2
    return jax.shard_map(
        on_device_fused if fused else on_device, mesh=mesh, in_specs=in_specs, out_specs=out_specs, check_vma=False
    )
```

```python
import functools
import math

import jax
import jax.numpy as jnp
from jax import lax
from jax.experimental import pallas as pl
from jax.experimental.pallas import tpu as pltpu
from jax.sharding import PartitionSpec as P

HEADS = 16


EPSILON = 1e-05
MIX_WEIGHT = 0.25


def norm_rows(values, gain_row, shift_row):
    center = values - jnp.mean(values, -1, keepdims=True)
    inverse = lax.rsqrt(jnp.mean(center * center, -1, keepdims=True) + EPSILON)
    unit_rows = center * inverse
    return (unit_rows * gain_row + shift_row, unit_rows, inverse)


def norm_back(grad_rows, unit_rows, inverse, gain_row):
    scaled = grad_rows * gain_row
    first_mean = jnp.mean(scaled, -1, keepdims=True)
    second_mean = jnp.mean(scaled * unit_rows, -1, keepdims=True)
    grad_values = inverse * (scaled - first_mean - unit_rows * second_mean)
    return (grad_values, jnp.sum(grad_rows * unit_rows, 0), jnp.sum(grad_rows, 0))


def contract_rows(left, right):
    return lax.dot_general(
        left, right, (((0,), (0,)), ((), ())), preferred_element_type=jnp.float32
    )


def times_transposed(left, right):
    return lax.dot_general(
        left, right, (((1,), (1,)), ((), ())), preferred_element_type=jnp.float32
    )


def segment_of(lengths, positions):
    first_end = lengths[0]
    second_end = lengths[0] + lengths[1]
    return (positions >= first_end).astype(jnp.int32) + (positions >= second_end).astype(jnp.int32)


def on_device(
    tokens,
    head_grad,
    w_qkv,
    w_out,
    w_up,
    w_down,
    gains,
    shifts,
    biases,
    up_bias,
    seq_lengths,
    neigh_keys,
    neigh_ids,
    neigh_counts,
    targets,
    p_lm,
):
    gathered = (
        lax.all_gather(w_qkv, ("dp", "fsdp"), axis=0, tiled=True),
        lax.all_gather(w_out, ("dp", "fsdp"), axis=0, tiled=True),
        lax.all_gather(w_up, ("dp", "fsdp"), axis=0, tiled=True),
        lax.all_gather(w_down, ("dp", "fsdp"), axis=0, tiled=True),
        lax.all_gather(gains, ("dp", "fsdp"), axis=1, tiled=True),
        lax.all_gather(shifts, ("dp", "fsdp"), axis=1, tiled=True),
        lax.all_gather(biases, ("dp", "fsdp"), axis=1, tiled=True),
        lax.all_gather(up_bias, ("dp", "fsdp"), axis=0, tiled=True),
    )
    row_count, feature_width = tokens.shape
    head_count = HEADS
    head_depth = feature_width // head_count
    score_scale = 1.0 / math.sqrt(head_depth)
    gain_rows = gathered[4].astype(jnp.float32)
    shift_rows = gathered[5].astype(jnp.float32)
    bias_rows = gathered[6].astype(jnp.float32)
    tokens_f32 = tokens.astype(jnp.float32)
    normed_in, unit_in, inverse_in = norm_rows(tokens_f32, gain_rows[0], shift_rows[0])
    normed_in_low = normed_in.astype(jnp.bfloat16)
    qkv_bias = jnp.concatenate([bias_rows[0], jnp.zeros_like(bias_rows[0]), bias_rows[1]])
    qkv = (
        jnp.dot(normed_in_low, gathered[0], preferred_element_type=jnp.float32) + qkv_bias
    ).astype(jnp.bfloat16)
    query_heads = qkv[:, :feature_width].reshape(row_count, head_count, head_depth)
    kv_local = qkv[:, feature_width:]
    kv_group = lax.all_gather(kv_local, "fsdp", axis=0, tiled=True)
    group_size = kv_group.shape[0]
    part_count = lax.axis_size("fsdp")
    block_rows = row_count * min(part_count, max(1, 512 // row_count))
    block_count = group_size // block_rows
    first_row = lax.axis_index("fsdp") * row_count
    last_row = first_row + row_count - 1
    lengths = seq_lengths[0]
    query_pos = first_row + jnp.arange(row_count, dtype=jnp.int32)
    query_seg = segment_of(lengths, query_pos)

    def scores_of(source, block_start):
        key_piece = lax.dynamic_slice_in_dim(source, block_start, block_rows, 0)
        key_heads = key_piece[:, :feature_width].reshape(block_rows, head_count, head_depth)
        value_heads = key_piece[:, feature_width:].reshape(block_rows, head_count, head_depth)
        key_pos = block_start + jnp.arange(block_rows, dtype=jnp.int32)
        allowed = (segment_of(lengths, key_pos)[None, :] == query_seg[:, None]) & (
            key_pos[None, :] <= query_pos[:, None]
        )
        raw_scores = (
            jnp.einsum("qhe,khe->hqk", query_heads, key_heads, preferred_element_type=jnp.float32)
            * score_scale
        )
        return (jnp.where(allowed[None], raw_scores, -jnp.inf), key_heads, value_heads)

    def keep_same(kept_value):
        return kept_value

    def stats_step(block_index, stats):
        block_start = block_index * block_rows

        def stats_block_work(pair):
            row_top, row_total = pair
            masked, key_heads, value_heads = scores_of(kv_group, block_start)
            new_top = jnp.maximum(row_top, jnp.max(masked, -1))
            safe_top = jnp.where(new_top > -jnp.inf, new_top, 0.0)
            row_total = row_total * jnp.exp(row_top - safe_top) + jnp.sum(
                jnp.exp(masked - safe_top[..., None]), -1
            )
            return (new_top, row_total)

        return lax.cond(block_start <= last_row, stats_block_work, keep_same, stats)

    start_stats = (
        jnp.full((head_count, row_count), -jnp.inf, jnp.float32),
        jnp.zeros((head_count, row_count), jnp.float32),
    )
    row_top, row_total = lax.fori_loop(0, block_count, stats_step, start_stats)
    log_total = row_top + jnp.log(row_total)

    def value_step(block_index, value_acc):
        block_start = block_index * block_rows

        def value_block_work(value_sum):
            masked, key_heads, value_heads = scores_of(kv_group, block_start)
            prob_low = jnp.exp(masked - log_total[..., None]).astype(jnp.bfloat16)
            return value_sum + jnp.einsum(
                "hqk,khe->qhe", prob_low, value_heads, preferred_element_type=jnp.float32
            )

        return lax.cond(block_start <= last_row, value_block_work, keep_same, value_acc)

    attended = lax.fori_loop(
        0, block_count, value_step, jnp.zeros((row_count, head_count, head_depth), jnp.float32)
    )
    attended = attended.reshape(row_count, feature_width)
    attended_low = attended.astype(jnp.bfloat16)
    hidden_one = tokens_f32 + (
        jnp.dot(attended_low, gathered[1], preferred_element_type=jnp.float32) + bias_rows[2]
    )
    normed_mid, unit_mid, inverse_mid = norm_rows(hidden_one, gain_rows[1], shift_rows[1])
    normed_mid_low = normed_mid.astype(jnp.bfloat16)
    pre_act = jnp.dot(normed_mid_low, gathered[2], preferred_element_type=jnp.float32) + gathered[
        7
    ].astype(jnp.float32)
    gelu_low = jax.nn.gelu(pre_act).astype(jnp.bfloat16)
    state_f32 = hidden_one + (
        jnp.dot(gelu_low, gathered[3], preferred_element_type=jnp.float32) + bias_rows[3]
    )
    query, unit_out, inverse_out = norm_rows(state_f32, gain_rows[2], shift_rows[2])
    span_count = neigh_keys.shape[0]
    slot_count = neigh_keys.shape[1]
    knn_scale = 0.5 / math.sqrt(feature_width)
    query_low = query.astype(jnp.bfloat16).reshape(span_count, -1, feature_width)
    key_square = jnp.einsum(
        "snd,snd->sn", neigh_keys, neigh_keys, preferred_element_type=jnp.float32
    )
    raw_logits = jnp.einsum(
        "sqd,snd->sqn", query_low, neigh_keys, preferred_element_type=jnp.float32
    )
    logits = (2.0 * raw_logits - key_square[:, None, :]) * knn_scale
    slot_valid = jnp.arange(slot_count, dtype=jnp.int32)[None, :] < neigh_counts[:, None]
    masked_logits = jnp.where(slot_valid[:, None, :], logits, -jnp.inf)
    exp_values = jnp.exp(masked_logits - jnp.max(masked_logits, -1, keepdims=True))
    weights = exp_values / jnp.sum(exp_values, -1, keepdims=True)
    id_match = neigh_ids[:, None, :] == targets.reshape(span_count, -1)[:, :, None]
    knn_prob = jnp.sum(jnp.where(id_match, weights, 0.0), -1)
    mixture = MIX_WEIGHT * knn_prob + (1.0 - MIX_WEIGHT) * p_lm.reshape(span_count, -1)
    token_loss = -jnp.log(mixture).reshape(row_count)
    match_f32 = jnp.where(id_match, 1.0, 0.0)
    dlogits = (
        -(MIX_WEIGHT / mixture)[..., None] * weights * (match_f32 - knn_prob[..., None])
    ).astype(jnp.bfloat16)
    knn_grad = jnp.einsum(
        "sqn,snd->sqd", dlogits, neigh_keys, preferred_element_type=jnp.float32
    ) * (2.0 * knn_scale)
    dquery = head_grad.astype(jnp.float32) + knn_grad.reshape(row_count, feature_width)
    back_params = (
        lax.all_gather(w_qkv, ("dp", "fsdp"), axis=0, tiled=True),
        lax.all_gather(w_out, ("dp", "fsdp"), axis=0, tiled=True),
        lax.all_gather(w_up, ("dp", "fsdp"), axis=0, tiled=True),
        lax.all_gather(w_down, ("dp", "fsdp"), axis=0, tiled=True),
        lax.all_gather(gains, ("dp", "fsdp"), axis=1, tiled=True),
        lax.all_gather(shifts, ("dp", "fsdp"), axis=1, tiled=True),
        lax.all_gather(biases, ("dp", "fsdp"), axis=1, tiled=True),
        lax.all_gather(up_bias, ("dp", "fsdp"), axis=0, tiled=True),
    )
    kv_back = lax.all_gather(kv_local, "fsdp", axis=0, tiled=True)
    gain_back = back_params[4].astype(jnp.float32)
    dstate, gain_grad_out, shift_grad_out = norm_back(dquery, unit_out, inverse_out, gain_back[2])
    dstate_low = dstate.astype(jnp.bfloat16)
    grad_w_down = contract_rows(gelu_low, dstate_low)
    bias_grad_down = jnp.sum(dstate_low.astype(jnp.float32), 0)
    dgelu = times_transposed(dstate_low, back_params[3])
    gelu_value, gelu_pull = jax.vjp(jax.nn.gelu, pre_act)
    dpre_low = gelu_pull(dgelu)[0].astype(jnp.bfloat16)
    grad_w_up = contract_rows(normed_mid_low, dpre_low)
    grad_up_bias = jnp.sum(dpre_low.astype(jnp.float32), 0)
    dnormed_mid = times_transposed(dpre_low, back_params[2])
    dhidden_part, gain_grad_mid, shift_grad_mid = norm_back(
        dnormed_mid, unit_mid, inverse_mid, gain_back[1]
    )
    dhidden_one = dstate + dhidden_part
    dhidden_low = dhidden_one.astype(jnp.bfloat16)
    grad_w_out = contract_rows(attended_low, dhidden_low)
    bias_grad_out = jnp.sum(dhidden_low.astype(jnp.float32), 0)
    dattended_low = times_transposed(dhidden_low, back_params[1]).astype(jnp.bfloat16)
    dattended_heads = dattended_low.reshape(row_count, head_count, head_depth)
    delta_rows = jnp.sum(
        dattended_heads.astype(jnp.float32) * attended.reshape(row_count, head_count, head_depth),
        -1,
    ).T

    def both_grad_step(block_index, grad_pair):
        block_start = block_index * block_rows

        def both_block_work(pair):
            dquery_acc, dkv_group = pair
            masked, key_heads, value_heads = scores_of(kv_back, block_start)
            prob_values = jnp.exp(masked - log_total[..., None])
            prob_low = prob_values.astype(jnp.bfloat16)
            dprob = jnp.einsum(
                "qhe,khe->hqk", dattended_heads, value_heads, preferred_element_type=jnp.float32
            )
            dscores = (prob_values * (dprob - delta_rows[..., None])).astype(jnp.bfloat16)
            dquery_acc = dquery_acc + jnp.einsum(
                "hqk,khe->qhe", dscores, key_heads, preferred_element_type=jnp.float32
            )
            dkey_heads = (
                jnp.einsum("hqk,qhe->khe", dscores, query_heads, preferred_element_type=jnp.float32)
                * score_scale
            )
            dvalue_heads = jnp.einsum(
                "hqk,qhe->khe", prob_low, dattended_heads, preferred_element_type=jnp.float32
            )
            block_grad = jnp.concatenate(
                [
                    dkey_heads.reshape(block_rows, feature_width),
                    dvalue_heads.reshape(block_rows, feature_width),
                ],
                1,
            )
            current = lax.dynamic_slice_in_dim(dkv_group, block_start, block_rows, 0)
            return (
                dquery_acc,
                lax.dynamic_update_slice_in_dim(dkv_group, current + block_grad, block_start, 0),
            )

        return lax.cond(block_start <= last_row, both_block_work, keep_same, grad_pair)

    zero_dquery = jnp.zeros((row_count, head_count, head_depth), jnp.float32)
    start_grads = (zero_dquery, jnp.zeros((group_size, 2 * feature_width), jnp.float32))
    dquery_acc, dkv_group = lax.fori_loop(0, block_count, both_grad_step, start_grads)
    dkv_mine = lax.psum_scatter(
        dkv_group.astype(jnp.bfloat16), "fsdp", scatter_dimension=0, tiled=True
    ).astype(jnp.float32)
    dqkv_low = jnp.concatenate(
        [(dquery_acc * score_scale).reshape(row_count, feature_width), dkv_mine], 1
    ).astype(jnp.bfloat16)
    grad_w_qkv = contract_rows(normed_in_low, dqkv_low)
    column_sums = jnp.sum(dqkv_low.astype(jnp.float32), 0)
    dnormed_in = times_transposed(dqkv_low, back_params[0])
    dinput_part, gain_grad_in, shift_grad_in = norm_back(
        dnormed_in, unit_in, inverse_in, gain_back[0]
    )
    grad_input = (dhidden_one + dinput_part).astype(jnp.bfloat16)
    grad_gains = jnp.stack([gain_grad_in, gain_grad_mid, gain_grad_out])
    grad_shifts = jnp.stack([shift_grad_in, shift_grad_mid, shift_grad_out])
    grad_biases = jnp.stack(
        [
            column_sums[:feature_width],
            column_sums[2 * feature_width :],
            bias_grad_out,
            bias_grad_down,
        ]
    )
    summed = (
        lax.psum_scatter(grad_w_qkv, ("dp", "fsdp"), scatter_dimension=0, tiled=True),
        lax.psum_scatter(grad_w_out, ("dp", "fsdp"), scatter_dimension=0, tiled=True),
        lax.psum_scatter(grad_w_up, ("dp", "fsdp"), scatter_dimension=0, tiled=True),
        lax.psum_scatter(grad_w_down, ("dp", "fsdp"), scatter_dimension=0, tiled=True),
        lax.psum_scatter(grad_gains, ("dp", "fsdp"), scatter_dimension=1, tiled=True),
        lax.psum_scatter(grad_shifts, ("dp", "fsdp"), scatter_dimension=1, tiled=True),
        lax.psum_scatter(grad_biases, ("dp", "fsdp"), scatter_dimension=1, tiled=True),
        lax.psum_scatter(grad_up_bias, ("dp", "fsdp"), scatter_dimension=0, tiled=True),
    )
    return (
        state_f32.astype(jnp.bfloat16),
        token_loss,
        grad_input,
        summed[0],
        summed[1],
        summed[2],
        summed[3],
        summed[4],
        summed[5],
        summed[6],
        summed[7],
    )


VMEM_LIMIT = 63 << 20
KNN_SCALE = 0.5 / 32.0
BF = jnp.bfloat16
F32 = jnp.float32
MESH = pl.DeviceIdType.MESH
NEG = -1e30


def dot(left, right, left_dim=1, right_dim=0):
    return lax.dot_general(
        left, right, (((left_dim,), (right_dim,)), ((), ())), preferred_element_type=F32
    )


def unit_of(values):
    center = values - jnp.mean(values, -1, keepdims=True)
    inverse = lax.rsqrt(jnp.mean(center * center, -1, keepdims=True) + EPSILON)
    return center * inverse, inverse


def ln_back(grad_rows, unit_rows, inverse, gain_row):
    scaled = grad_rows * gain_row
    first_mean = jnp.mean(scaled, -1, keepdims=True)
    second_mean = jnp.mean(scaled * unit_rows, -1, keepdims=True)
    return inverse * (scaled - first_mean - unit_rows * second_mean)


def col_sum(values):
    return jnp.sum(values, 0, keepdims=True)


def gelu_pair(u):
    k0 = math.sqrt(2.0 / math.pi)
    square = u * u
    t = jnp.tanh(u * (k0 + (k0 * 0.044715) * square))
    half = 0.5 * (1.0 + t)
    slope = half + (0.5 * u) * (1.0 - t * t) * (k0 + (3.0 * k0 * 0.044715) * square)
    return u * half, slope


GATHER_X_FIRST = (13, 2, 7)
REDUCE_Z_FIRST = (1, 9)
DOWN = {7: (0, 1), 13: (1, 1), 8: (2, 2), 9: (4, 2), 10: (6, 2)}

(
    DO_Y0, DO_Z, DO_F, DO_X, DO_Y, DO_C, DO_TOK, DO_MASK, DO_COLS, DO_TABLE, DO_UNPACK, DO_NORMOWN,
    DO_NORMOTHER, DO_PROJ, DO_ATTEND, DO_ATTOUT, DO_NORMMID, DO_UP, DO_DOWN, DO_KNN, DO_STATEOUT,
    DO_DSREST, DO_RC, DO_RY, DO_RX, DO_RF, DO_RZ, DO_GD, DO_DP, DO_GU, DO_DNO, DO_DNS, DO_BACKMID,
    DO_DAO, DO_GO, DO_AB, DO_GQ, DO_DIO, DO_DIS, DO_BIO, DO_BIS, DO_GIN, DO_GP,
) = range(43)
ORDER = (
    (DO_Y0, 2), (DO_Z, 12), (DO_Z, 11), (DO_Y0, 1), (DO_Y0, 6), (DO_Y0, 5), (DO_Y0, 0), (DO_TOK,),
    (DO_Y0, 4), (DO_COLS,), (DO_TABLE, 3), (DO_TABLE, 1), (DO_F, 12), (DO_TABLE, 2), (DO_Y0, 3), (DO_Z,
    1), (DO_TABLE, 0), (DO_MASK,), (DO_X, 12), (DO_Z, 0), (DO_Z, 2), (DO_Z, 8), (DO_Y, 12), (DO_F, 11),
    (DO_X, 11), (DO_F, 1), (DO_X, 1), (DO_F, 0), (DO_F, 2), (DO_Y, 11), (DO_Z, 4), (DO_Z, 3), (DO_Z, 6),
    (DO_C, 12), (DO_X, 0), (DO_Z, 5), (DO_F, 8), (DO_UNPACK,), (DO_C, 1), (DO_NORMOTHER,),
    (DO_NORMOWN,), (DO_PROJ, 1, 0), (DO_PROJ, 1, 1), (DO_X, 2), (DO_X, 8), (DO_Z, 10), (DO_C, 0), (DO_Z,
    13), (DO_C, 11), (DO_PROJ, 0, 0), (DO_PROJ, 0, 1), (DO_F, 4), (DO_C, 2), (DO_C, 8), (DO_PROJ, 2, 0),
    (DO_X, 4), (DO_Z, 9), (DO_PROJ, 2, 1), (DO_ATTEND, 1), (DO_ATTEND, 0), (DO_F, 3), (DO_ATTEND, 3),
    (DO_C, 4), (DO_F, 6), (DO_ATTEND, 2), (DO_X, 3), (DO_Z, 7), (DO_X, 6), (DO_F, 5), (DO_C, 3), (DO_X,
    5), (DO_F, 10), (DO_F, 13), (DO_ATTOUT, 0), (DO_ATTOUT, 1), (DO_NORMMID, 1), (DO_X, 10), (DO_C, 6),
    (DO_NORMMID, 0), (DO_UP, 1, 0), (DO_UP, 1, 1), (DO_F, 9), (DO_F, 7), (DO_C, 5), (DO_UP, 3, 0),
    (DO_UP, 3, 1), (DO_UP, 0, 0), (DO_UP, 0, 1), (DO_X, 13), (DO_UP, 2, 0), (DO_UP, 2, 1), (DO_C, 10),
    (DO_DOWN, 8), (DO_X, 9), (DO_C, 13), (DO_X, 7), (DO_DOWN, 10), (DO_DOWN, 13), (DO_C, 7), (DO_C, 9),
    (DO_DOWN, 7), (DO_DOWN, 9), (DO_KNN, 0), (DO_KNN, 1), (DO_DSREST,), (DO_DP, 1, 0), (DO_DP, 2, 0),
    (DO_DP, 3, 0), (DO_DP, 0, 0), (DO_STATEOUT,), (DO_GD, 7), (DO_GD, 13), (DO_RC, 7), (DO_RC, 13),
    (DO_GD, 8), (DO_GD, 9), (DO_RC, 8), (DO_RX, 7), (DO_DP, 1, 1), (DO_DP, 2, 1), (DO_GD, 10), (DO_DP,
    3, 1), (DO_RC, 9), (DO_RX, 13), (DO_DP, 0, 1), (DO_GU, 0), (DO_DNO, 0), (DO_RC, 10), (DO_GU, 1),
    (DO_GU, 2), (DO_GU, 3), (DO_RC, 3), (DO_RF, 9), (DO_DNO, 1), (DO_RC, 4), (DO_DNO, 3), (DO_DNS, 0),
    (DO_DNS, 1), (DO_RC, 5), (DO_DNS, 2), (DO_RF, 7), (DO_DNS, 3), (DO_BACKMID, 0), (DO_RC, 6), (DO_RX,
    10), (DO_DNO, 2), (DO_RF, 13), (DO_RX, 8), (DO_BACKMID, 1), (DO_DAO, 1), (DO_DAO, 2), (DO_RZ, 7),
    (DO_RX, 9), (DO_RF, 10), (DO_DAO, 3), (DO_GO,), (DO_RF, 8), (DO_RX, 3), (DO_DAO, 0), (DO_RZ, 13),
    (DO_AB, 1), (DO_RF, 3), (DO_RC, 11), (DO_RZ, 10), (DO_RX, 4), (DO_AB, 2), (DO_RZ, 8), (DO_RF, 4),
    (DO_AB, 3), (DO_RX, 5), (DO_RZ, 3), (DO_AB, 0), (DO_GQ, 0), (DO_RF, 5), (DO_RZ, 4), (DO_GQ, 1),
    (DO_RX, 6), (DO_DIO,), (DO_RZ, 9), (DO_RC, 0), (DO_BIO, 0), (DO_RC, 1), (DO_RZ, 5), (DO_GQ, 2),
    (DO_RY, 11), (DO_RF, 6), (DO_BIO, 1), (DO_DIS,), (DO_BIS, 0), (DO_RC, 2), (DO_RF, 1), (DO_BIS, 1),
    (DO_GP,), (DO_RX, 0), (DO_RC, 12), (DO_RZ, 6), (DO_GIN, 0), (DO_RF, 0), (DO_RX, 1), (DO_RX, 11),
    (DO_RF, 11), (DO_RZ, 0), (DO_GIN, 1), (DO_RY, 12), (DO_RX, 2), (DO_RZ, 1), (DO_RX, 12), (DO_RZ, 11),
    (DO_RF, 2), (DO_RF, 12), (DO_RZ, 2), (DO_RZ, 12),
)


def block_kernel(
    tokens, head_grad, w_qkv, w_out, w_up, w_down, gains, shifts, biases, up_bias, seq, counts, keys_in,
    ids, targets, p_lm, state_out, loss_out, gin_out, gqkv_out, gout_out, gup_out, gdown_out, gpk_out,
    wA, wD, wO, pk, prm, ubias, tokg, ni, qkv, mask, att, h1, nmg, gelu, slope, st, prec, hgrad, ksq,
    match, dsg, tcol, pcol, lcol, lossb, dh, dhl, das, dattg, dnr2, sendb, gA, gD, gO, gP, dRA, xRA,
    zRA, dRD, xRD, zRD, dRO, yRO, xRO, zRO, dRP, yRP, xRP, zRP, finA, finD, finO, finP, xOA, xOD, pg,
    dub, lsem, ysend, yrecv, zsend, zrecv, xsend, xrecv, csend, crecv, osem, msend, mrecv, asend, arecv,
    dsend, drecv, psend, precv, rcs, rcr, rxs, rxr, rzs, rzr, rys, ryr, rfl, kn_sem,
):
    dp = lax.axis_index("dp")
    y = lax.axis_index("fsdp")
    z = dp // 4
    x = (dp // 2) % 2
    c = dp % 2
    oy = 1 - y
    ox = 1 - x
    oc = 1 - c

    def dev(zz, xx, cc, yy):
        return ((zz * 2 + xx) * 2 + cc, yy)

    z_to = [None] + [(z + j) % 4 for j in (1, 2, 3)]
    z_of = [z] + [(z - j) % 4 for j in (1, 2, 3)]
    zdev = [None] + [dev(zz, x, c, y) for zz in z_to[1:]]
    xdev = dev(z, ox, c, y)
    ydev = dev(z, x, c, oy)
    cdev = dev(z, x, oc, y)
    middle = (z == 1) | (z == 2)
    z_direct = {1: z != 3, 2: None, 3: z != 0}

    def when(cond, fn):
        if cond is None:
            fn()
        else:
            pl.when(cond)(fn)

    def rc(src, dst_ref, ss, rs, to):
        return pltpu.make_async_remote_copy(
            src_ref=src, dst_ref=dst_ref, send_sem=ss, recv_sem=rs, device_id=to, device_id_type=MESH
        )

    def lc(src, dst_ref, sem):
        return pltpu.make_async_copy(src, dst_ref, sem)

    pending = []
    finals = []
    late_recv = []
    tasks = {}

    def task(fn, name, *args):
        tasks[name] = functools.partial(fn, *args)

    def send(cp, cond=None):
        when(cond, cp.start)
        pending.append((cond, cp))

    my_rows = pl.ds(pl.multiple_of(y * 32, 32), 32)

    def up_cols(j, i, yy):
        return pl.ds(pl.multiple_of((8 * j + 2 * i + yy) * 128, 128), 128)

    def part_cols(part, yy):
        return pl.ds(pl.multiple_of(part * 1024 + yy * 512, 512), 512)

    for s in range(3):
        lc(w_qkv.at[:, part_cols(s, y)], wA.at[s, z, x, c, my_rows], lsem.at[s]).start()
    lc(w_out, wO.at[z, x, c, y], lsem.at[11]).start()
    lc(tokens, tokg.at[y], lsem.at[14]).start()
    for j in range(4):
        for i in range(4):
            lc(w_up.at[:, up_cols(j, i, y)], wA.at[3 + j, z, x, c, my_rows, pl.ds(i * 128, 128)],
               lsem.at[3 + j]).start()
    for t, (first, count) in DOWN.items():
        for h in range(first, first + count):
            lc(w_down.at[:, pl.ds(h * 128, 128)], wD.at[h, z, x, c], lsem.at[t]).start()
    for h in range(8):
        lc(keys_in.at[:, :, :, :, pl.ds(h * 128, 128)], gD.at[h], kn_sem.at[0]).start()
    lc(head_grad, hgrad, kn_sem.at[1]).start()

    quarter = (2 * dp + y) % 4
    pg[...] = jnp.zeros_like(pg)
    pg[0:3, 0:32] = gains[...].astype(F32)
    pg[3:6, 0:32] = shifts[...].astype(F32)
    pg[6:10, 0:32] = biases[...].astype(F32)
    small = pltpu.roll(pg[:, 0:128], quarter * 32, 1)
    pg[10:11, 0:128] = up_bias[...].astype(F32)
    row_id = lax.broadcasted_iota(jnp.int32, (16, 128), 0)
    pk[z, x, c, y] = jnp.where(row_id == 10, pg[:, 0:128], small).astype(BF)

    barrier = pltpu.get_barrier_semaphore()
    for to in (*zdev[1:], xdev, ydev, cdev):
        pl.semaphore_signal(barrier, inc=1, device_id=to, device_id_type=MESH)
    pl.semaphore_wait(barrier, 6)

    def weight(t, *index):
        if t < 7:
            return wA.at[(t, *index)]
        if t in DOWN:
            return wD.at[(pl.ds(*DOWN[t]), *index)]
        return (wO if t == 11 else pk).at[index]

    def z_view(t, zz):
        return weight(t, zz, x, c, y) if t in (11, 12) else weight(t, zz, x, c)

    def y_view(t):
        return wO.at[:, :, c, y] if t == 11 else pk.at[:, :, c, y]

    def c_view(t):
        return weight(t, slice(None), slice(None), c)

    def y0_full(t):
        view = wA.at[t, z, x, c, my_rows]
        return rc(view, view, ysend.at[t], yrecv.at[t], ydev)

    def start_y0(t):
        if t < 3:
            rc(w_qkv.at[:, part_cols(t, oy)], wA.at[t, z, x, c, my_rows], ysend.at[t], yrecv.at[t], ydev).start()
        else:
            for i in range(4):
                rc(w_up.at[:, up_cols(t - 3, i, oy)], wA.at[t, z, x, c, my_rows, pl.ds(i * 128, 128)],
                   ysend.at[t], yrecv.at[t], ydev).start()
        pending.append((None, y0_full(t)))

    def x_copy(t, j):
        view = z_view(t, z_of[j])
        return rc(view, view, xsend.at[t, j], xrecv.at[t, j], xdev)

    def pair_view(t, zz):
        return weight(t, zz, slice(None), c)

    def z_copy(t, j):
        view = pair_view(t, z) if t in GATHER_X_FIRST else z_view(t, z)
        return rc(view, view, zsend.at[t, j], zrecv.at[t, j], zdev[j])

    far = jnp.where(z == 1, 0, 3)
    far_sem = jnp.where(z == 1, 1, 3)

    def start_z(t):
        if t != 12:
            view = wA.at[t, z, x, c, my_rows] if t < 7 else z_view(t, z)
            lc(view, view, lsem.at[t]).wait()
        if t < 7:
            y0_full(t).wait_recv()
        if t not in GATHER_X_FIRST:
            for j in (2, 1, 3):
                send(z_copy(t, j), z_direct[j])
        send(x_copy(t, 0))

    def to_far(t, view):
        send(rc(view, view, zsend.at[t, 0], zrecv.at[t, far_sem], dev(far, x, c, y)), middle)

    def forward(t):
        if t in GATHER_X_FIRST:
            x_copy(t, 0).wait_recv()
            for j in (2, 1, 3):
                send(z_copy(t, j), z_direct[j])
        else:
            z_copy(t, 2).wait_recv()
            to_far(t, z_view(t, z_of[2]))
            send(x_copy(t, 2))

    def start_x(t):
        if t in GATHER_X_FIRST:
            z_copy(t, 2).wait_recv()
            to_far(t, pair_view(t, z_of[2]))
        else:
            for j in (1, 3):
                z_copy(t, j).wait_recv()
                send(x_copy(t, j))

    def x_done(t):
        if t in GATHER_X_FIRST:
            for j in (1, 3):
                z_copy(t, j).wait_recv()
        else:
            for j in range(4):
                x_copy(t, j).wait_recv()

    def y_copy(t):
        return rc(y_view(t), y_view(t), ysend.at[t - 4], yrecv.at[t - 4], ydev)

    def start_y(t):
        x_done(t)
        send(y_copy(t))

    def c_copy(t):
        return rc(c_view(t), c_view(t), csend.at[t], crecv.at[t], cdev)

    def start_c(t):
        if t not in (11, 12):
            x_done(t)
        else:
            y_copy(t).wait_recv()
        send(c_copy(t))

    def ready(t):
        c_copy(t).wait_recv()

    for t in range(14):
        if t < 7:
            task(start_y0, (DO_Y0, t), t)
        task(start_z, (DO_Z, t), t)
        task(forward, (DO_F, t), t)
        task(start_x, (DO_X, t), t)
        if t in (11, 12):
            task(start_y, (DO_Y, t), t)
        task(start_c, (DO_C, t), t)

    tok_copy = rc(tokens, tokg.at[y], msend.at[0], mrecv.at[0], ydev)
    task(send, (DO_TOK,), tok_copy)

    first_end = seq[0, 0]
    second_end = first_end + seq[0, 1]

    def segment(pos):
        return (pos >= first_end).astype(jnp.int32) + (pos >= second_end).astype(jnp.int32)

    def mask_rows(i, _):
        rows = pl.ds(pl.multiple_of(i * 128, 128), 128)
        qpos = i * 128 + lax.broadcasted_iota(jnp.int32, (128, 512), 0)
        kpos = lax.broadcasted_iota(jnp.int32, (128, 512), 1)
        good = (segment(qpos) == segment(kpos)) & (kpos <= qpos)
        mask[rows, :] = jnp.where(good, 0.0, NEG).astype(BF)
        return 0

    def make_mask():
        lax.fori_loop(0, 4, mask_rows, 0)

    task(make_mask, (DO_MASK,))

    def make_columns():
        wide = jnp.concatenate([targets[...].astype(F32), p_lm[...], jnp.zeros((6, 256), F32)], 0)
        cols = jnp.transpose(wide)
        tcol[...] = cols[:, 0:1]
        pcol[...] = cols[:, 1:2]
        lc(gD, gD, kn_sem.at[0]).wait()
        lc(head_grad, hgrad, kn_sem.at[1]).wait()

    task(make_columns, (DO_COLS,))

    def keys_of(s):
        return jnp.concatenate([gD[h, s // 4, (s // 2) % 2, s % 2] for h in range(8)], 1)

    def make_table(b):
        eye = lax.broadcasted_iota(jnp.int32, (128, 128), 0) == lax.broadcasted_iota(jnp.int32, (128, 128), 1)
        slot = lax.broadcasted_iota(jnp.int32, (16, 128), 1)
        for s in range(b * 4, b * 4 + 4):
            rows = slice(s * 16, s * 16 + 16)
            kk = keys_of(s)
            square = jnp.broadcast_to(col_sum(jnp.where(eye, dot(kk, kk, 1, 1), 0.0)), (16, 128))
            ksq[rows, :] = jnp.where(slot < counts[0, s], square * -KNN_SCALE, NEG)
            match[rows, :] = jnp.where(ids[s : s + 1, :].astype(F32) == tcol[rows, :], 1.0, 0.0)

    for b in range(4):
        task(make_table, (DO_TABLE, b), b)

    def unpack():
        ready(12)
        for g in range(8):
            total = None
            for i in range(4):
                piece = pk[g // 2, g % 2, i // 2, i % 2].astype(F32)
                total = piece if total is None else total + piece
            prm[:, g * 128 : (g + 1) * 128] = total
        for d in range(16):
            piece = pk[d // 4, (d // 2) % 2, d % 2, y].astype(F32)
            ubias[0:1, d * 128 : (d + 1) * 128] = piece[10:11, :]

    task(unpack, (DO_UNPACK,))

    def row(r):
        return prm[r : r + 1, :]

    def norm_in(half):
        def rows_of(i, _):
            rows = pl.ds(pl.multiple_of(i * 64, 64), 64)
            unit, _inv = unit_of(tokg[half, rows, :].astype(F32))
            ni[half, rows, :] = (unit * row(0) + row(3)).astype(BF)
            return 0

        lax.fori_loop(0, 4, rows_of, 0)

    def norm_own():
        lc(tokens, tokg.at[y], lsem.at[14]).wait()
        norm_in(y)

    def norm_other():
        tok_copy.wait_recv()
        norm_in(oy)

    task(norm_own, (DO_NORMOWN,))
    task(norm_other, (DO_NORMOTHER,))

    head_cols = pl.ds(pl.multiple_of(y * 512, 512), 512)

    def project(s, own):
        if own:
            ready(s)
        half = y if own else oy
        value = dot(ni[half], wA[s].reshape(1024, 512))
        if s != 1:
            value = value + prm[6 + s // 2 : 7 + s // 2, head_cols]
        qkv[s, half] = value.astype(BF)

    for s in range(3):
        task(project, (DO_PROJ, s, 0), s, True)
        task(project, (DO_PROJ, s, 1), s, False)

    lane = lax.broadcasted_iota(jnp.int32, (1, 128), 1)
    in_head = [lane < 64, lane >= 64]

    def probs_of(qe, k2, half):
        nk = 256 * (half + 1)
        s = dot(qe, k2[:nk], 1, 1) * 0.125 + mask[half * 256 : half * 256 + 256, :nk].astype(F32)
        ex = jnp.exp(s - jnp.max(s, -1, keepdims=True))
        return ex * (1.0 / jnp.sum(ex, -1, keepdims=True))

    def attend(p):
        cols = slice(p * 128, p * 128 + 128)
        q2 = qkv[0, :, :, cols]
        k2 = qkv[1, :, :, cols].reshape(512, 128)
        v2 = qkv[2, :, :, cols].reshape(512, 128)
        for half in range(2):
            nk = 256 * (half + 1)
            outs = []
            for e in range(2):
                qe = jnp.where(in_head[e], q2[half], jnp.zeros_like(q2[half]))
                outs.append(dot(probs_of(qe, k2, half).astype(BF), v2[:nk]))
            att[half, :, pair_cols(p)] = jnp.where(in_head[0], outs[0], outs[1]).astype(BF)
        send(att_copy(p))

    def pair_cols(p):
        return pl.ds(pl.multiple_of(y * 512 + p * 128, 128), 128)

    def att_copy(p):
        view = att.at[:, :, pair_cols(p)]
        return rc(view, view, asend.at[p], arecv.at[p], ydev)

    for p in range(4):
        task(attend, (DO_ATTEND, p), p)

    def attention_out(half):
        if half == 0:
            for p in range(4):
                att_copy(p).wait_recv()
            ready(11)
        h1[half] = dot(att[half], wO[...].reshape(1024, 1024)) + row(8)

    def norm_mid(half):
        def rows_of(k, _):
            rows = pl.ds(pl.multiple_of(k * 64, 64), 64)
            value = h1[half, rows, :] + tokg[half, rows, :].astype(F32)
            h1[half, rows, :] = value
            unit, _inv = unit_of(value)
            nmg[half, rows, :] = (unit * row(1) + row(4)).astype(BF)
            return 0

        lax.fori_loop(0, 4, rows_of, 0)

    for half in range(2):
        task(attention_out, (DO_ATTOUT, half), half)
        task(norm_mid, (DO_NORMMID, half), half)

    def up(j, half):
        if half == 0:
            ready(3 + j)
        cols = slice(j * 512, (j + 1) * 512)
        u = dot(nmg[half], wA[3 + j].reshape(1024, 512)) + ubias[0:1, cols]
        value, dvalue = gelu_pair(u)
        gelu[half, :, cols] = value.astype(BF)
        slope[half, :, cols] = dvalue.astype(BF)

    for j in range(4):
        task(up, (DO_UP, j, 0), j, 0)
        task(up, (DO_UP, j, 1), j, 1)

    def part_copy(t):
        cols = pl.ds(DOWN[t][0] * 128, DOWN[t][1] * 128)
        sem = list(DOWN).index(t)
        return rc(sendb.at[:, cols], prec.at[:, cols], psend.at[sem], precv.at[sem], ydev)

    def down_weight(first, count):
        return jnp.concatenate([wD[h].reshape(2048, 128) for h in range(first, first + count)], 1)

    def down(t):
        ready(t)
        first, count = DOWN[t]
        cols = slice(first * 128, (first + count) * 128)
        right = down_weight(first, count)
        sendb[:, cols] = dot(gelu[oy], right).astype(BF)
        send(part_copy(t))
        st[:, cols] = dot(gelu[y], right) + (h1[y, :, cols] + prm[9:10, cols])

    for t in DOWN:
        task(down, (DO_DOWN, t), t)

    def add_row(r, value):
        pg[r : r + 1, :] = pg[r : r + 1, :] + value

    def ds_copy(j, b):
        rows = pl.ds(b * 128, 128) if j < 2 else pl.ds(0, 256)
        cols = pl.ds(j * 128, 128) if j < 2 else pl.ds((j - 1) * 256, 256)
        view = dsg.at[y, rows, cols]
        sem = 2 * j + b if j < 2 else 2 + j
        return rc(view, view, dsend.at[sem], drecv.at[sem], ydev)

    ds_waited = []

    def need_ds(*columns):
        for j in columns:
            if j not in ds_waited:
                ds_waited.append(j)
                for b in range(2 if j < 2 else 1):
                    ds_copy(j, b).wait_recv()

    def neighbours(b):
        if b == 0:
            pg[...] = jnp.zeros_like(pg)
            for t in DOWN:
                part_copy(t).wait_recv()
        rows = slice(b * 128, b * 128 + 128)
        value = st[rows, :] + prec[rows, :].astype(F32)
        unit, inv = unit_of(value)
        query = (unit * row(2) + row(5)).astype(BF)
        raw = jnp.concatenate(
            [dot(query[i * 16 : i * 16 + 16], keys_of(b * 8 + i), 1, 1) for i in range(8)], 0
        )
        logits = (2.0 * KNN_SCALE) * raw + ksq[rows, :]
        ex = jnp.exp(logits - jnp.max(logits, -1, keepdims=True))
        weights = ex / jnp.sum(ex, -1, keepdims=True)
        same = match[rows, :]
        knn_prob = jnp.sum(same * weights, -1, keepdims=True)
        mixture = MIX_WEIGHT * knn_prob + (1.0 - MIX_WEIGHT) * pcol[rows, :]
        lcol[rows, :] = -jnp.log(mixture)
        dlog = (-(MIX_WEIGHT / mixture) * weights * (same - knn_prob)).astype(BF)
        kgrad = jnp.concatenate(
            [dot(dlog[i * 16 : i * 16 + 16], keys_of(b * 8 + i)) for i in range(8)], 0
        )
        dquery = hgrad[rows, :].astype(F32) + kgrad * (2.0 * KNN_SCALE)
        hgrad[rows, :] = value.astype(BF)
        add_row(2, col_sum(dquery * unit))
        add_row(5, col_sum(dquery))
        dvalue = ln_back(dquery, unit, inv, row(2))
        st[rows, :] = dvalue
        low = dvalue.astype(BF)
        add_row(9, col_sum(low.astype(F32)))
        dsg[y, rows, :] = low
        send(ds_copy(0, b))
        send(ds_copy(1, b))

    for b in range(2):
        task(neighbours, (DO_KNN, b), b)

    out_state = lc(hgrad, state_out, osem.at[0])

    def state_done():
        out_state.start()
        lossb[...] = jnp.transpose(jnp.broadcast_to(lcol[...], (256, 128)))[0:1, :]
        cp = lc(lossb, loss_out, osem.at[1])
        cp.start()
        finals.append(cp)

    task(state_done, (DO_STATEOUT,))

    def ds_rest():
        send(ds_copy(2, 0))
        send(ds_copy(3, 0))
        send(ds_copy(4, 0))

    task(ds_rest, (DO_DSREST,))

    slot_of = {3: 0, 4: 1, 5: 2, 6: 3, 0: 0, 1: 1, 2: 2}

    every = slice(None)

    def pick(refs, t, *index):
        if t < 7:
            return refs[0].at[(slot_of[t] if refs[0] is gA else t, *index)]
        if t in DOWN:
            return refs[1].at[(pl.ds(*DOWN[t]), *index)]
        return refs[2 if t == 11 else 3].at[index]

    g_refs = (gA, gD, gO, gP)
    c_refs = (dRA, dRD, dRO, dRP)
    y_refs = (None, None, yRO, yRP)
    x_refs = (xRA, xRD, xRO, xRP)
    z_refs = (zRA, zRD, zRO, zRP)

    def g_at(t, zz, xx):
        return pick(g_refs, t, zz, xx, c, y) if t in (11, 12) else pick(g_refs, t, zz, xx, c)

    def rs_c(t):
        return rc(pick(g_refs, t, every, every, oc), pick(c_refs, t, every), rcs.at[t], rcr.at[t], cdev)

    def rs_y(t):
        return rc(pick(g_refs, t, every, every, c, oy), pick(y_refs, t, every), rys.at[t], ryr.at[t], ydev)

    def x_one(t):
        k = REDUCE_Z_FIRST.index(t)
        return xOA.at[k] if t < 7 else xOD.at[k, pl.ds(0, DOWN[t][1])]

    def rs_x(t):
        if t in REDUCE_Z_FIRST:
            return rc(g_at(t, z, ox), x_one(t), rxs.at[t], rxr.at[t], xdev)
        return rc(g_at(t, every, ox), pick(x_refs, t, every), rxs.at[t], rxr.at[t], xdev)

    def z_block(t, zz):
        return g_at(t, zz, every if t in REDUCE_Z_FIRST else x)

    def z_slot(t, j):
        if t in REDUCE_Z_FIRST:
            return pick((x_refs, z_refs)[j // 2], t, pl.ds(2 * (j % 2), 2))
        return pick(z_refs, t, j)

    def rs_z(t, j):
        return rc(z_block(t, z_to[j]), z_slot(t, j), rzs.at[t, j], rzr.at[t, j], zdev[j])

    end_block = jnp.where(z == 0, 3, 0)
    end_to = dev(jnp.where(z == 0, 1, 2), x, c, y)
    is_end = (z == 0) | (z == 3)

    def rs_end(t):
        return rc(z_block(t, end_block), z_slot(t, 0), rzs.at[t, 0], rzr.at[t, 0], end_to)

    def add_to(ref, other):
        ref[...] = (ref[...].astype(F32) + other.astype(F32)).astype(ref.dtype)

    def rs_after_c(t):
        rs_c(t).wait_recv()
        for i in range(4):
            add_to(pick(g_refs, t, i, every, c), pick(c_refs, t, i)[...])
        if t in REDUCE_Z_FIRST:
            start_zs(t)
        else:
            (rs_y(t) if t in (11, 12) else rs_x(t)).start()

    def rs_after_y(t):
        rs_y(t).wait_recv()
        for i in range(4):
            add_to(pick(g_refs, t, i, every, c, y), pick(y_refs, t, i)[...])
        rs_x(t).start()

    def start_zs(t):
        when(is_end, rs_end(t).start)
        when(z_direct[1], rs_z(t, 1).start)
        when(z_direct[3], rs_z(t, 3).start)
        when(is_end, rs_z(t, 2).start)

    def z_arrived(t):
        rs_z(t, 2).wait_recv()
        pl.when(z != 0)(rs_z(t, 1).wait_recv)
        pl.when(z != 3)(rs_z(t, 3).wait_recv)

    def rs_after_x(t):
        if t in REDUCE_Z_FIRST:
            z_arrived(t)

            def add(*slots):
                total = g_at(t, z, every)[...].astype(F32)
                for j in slots:
                    total = total + z_slot(t, j)[...].astype(F32)
                g_at(t, z, every)[...] = total.astype(BF)

            pl.when(z == 0)(functools.partial(add, 2, 3))
            pl.when(z == 3)(functools.partial(add, 2, 1))
            pl.when(middle)(functools.partial(add, 2, 1, 3))
            rs_x(t).start()
        else:
            rs_x(t).wait_recv()
            for i in range(4):
                add_to(g_at(t, i, x), pick(x_refs, t, i)[...])
            start_zs(t)

    def rs_forward(t):
        def go():
            rs_end(t).wait_recv()
            add_to(z_block(t, z_to[2]), z_slot(t, 0)[...])
            rs_z(t, 2).start()

        pl.when(middle)(go)

    def rs_sends(t):
        out = [(None, rs_c(t)), (None, rs_x(t)), (None, rs_z(t, 2))]
        if t in (11, 12):
            out.append((None, rs_y(t)))
        return out + [(z_direct[1], rs_z(t, 1)), (z_direct[3], rs_z(t, 3)), (is_end, rs_end(t))]

    def out_cols(t, yy):
        if t < 3:
            return [(gqkv_out, part_cols(t, yy), pl.ds(0, 512))]
        return [(gup_out, up_cols(t - 3, i, yy), pl.ds(i * 128, 128)) for i in range(4)]

    def rs_finish(t):
        if t < 7:
            fin = finA.at[t]
        elif t in DOWN:
            fin = finD.at[pl.ds(*DOWN[t])]
        else:
            fin = finO if t == 11 else finP
        own = g_at(t, z, x)
        if t in REDUCE_Z_FIRST:
            rs_x(t).wait_recv()
            total = own[...].astype(F32) + x_one(t)[...].astype(F32)
            fin[...] = total.reshape(fin.shape)
        else:
            z_arrived(t)
            near = jnp.where(z == 0, 3, 1)
            total = own[...].astype(F32)
            for j in (2, near):
                total = total + pick(z_refs, t, j)[...].astype(F32)
            fin[...] = total.reshape(fin.shape)

            def third():
                fin[...] = fin[...] + pick(z_refs, t, 3)[...].astype(F32).reshape(fin.shape)

            pl.when(middle)(third)
        if t not in (3, 4, 5):
            pending.extend(rs_sends(t))
        if t < 7:
            for ref, cols, inner in out_cols(t, y):
                lc(finA.at[t, y, :, inner], ref.at[:, cols], rfl.at[t]).start()
                rc(finA.at[t, oy, :, inner], ref.at[:, cols], rys.at[t], ryr.at[t], ydev).start()
            full = finA.at[t, y]
            finals.append(lc(full, full, rfl.at[t]))
            both = rc(full, full, rys.at[t], ryr.at[t], ydev)
            pending.append((None, both))
            late_recv.append(both)
        else:
            if t in DOWN:
                for h in range(DOWN[t][0], sum(DOWN[t])):
                    lc(finD.at[h], gdown_out.at[:, pl.ds(h * 128, 128)], rfl.at[t]).start()
                finals.append(lc(fin, fin, rfl.at[t]))
            else:
                cp = lc(fin, gout_out if t == 11 else gpk_out, rfl.at[t])
                cp.start()
                finals.append(cp)

    for t in range(14):
        task(rs_after_c, (DO_RC, t), t)
        if t in (11, 12):
            task(rs_after_y, (DO_RY, t), t)
        task(rs_after_x, (DO_RX, t), t)
        task(rs_forward, (DO_RF, t), t)
        task(rs_finish, (DO_RZ, t), t)

    def make_down(t):
        first, count = DOWN[t]
        need_ds(first if first < 2 else first // 2 + 1)
        ds_cols = dsg[:, :, first * 128 : (first + count) * 128].reshape(512, count * 128)
        for i in range(4):
            part = gelu[:, :, i * 512 : (i + 1) * 512].reshape(512, 512)
            value = dot(part, ds_cols, 0, 0).astype(BF)
            for k in range(count):
                gD[first + k, i] = value[:, k * 128 : (k + 1) * 128].reshape(2, 2, 128, 128)
        rs_c(t).start()

    for t in DOWN:
        task(make_down, (DO_GD, t), t)

    def make_a(t, left, right):
        for i in range(4):
            part = left[:, :, i * 256 : (i + 1) * 256].reshape(512, 256)
            gA[slot_of[t], i] = dot(part, right, 0, 0).astype(BF).reshape(2, 2, 64, 512)
        rs_c(t).start()

    dub_started = []

    def make_dpre(i, own):
        if not own:
            need_ds(0, 1, 2, 3, 4)
        half = y if own else oy
        cols = slice(i * 512, (i + 1) * 512)
        acc = None
        for j in range(4):
            right = jnp.concatenate([wD[2 * j + k, i].reshape(512, 128) for k in range(2)], 1)
            part = dot(dsg[half, :, j * 256 : (j + 1) * 256], right, 1, 1)
            acc = part if acc is None else acc + part
        low = (acc * slope[half, :, cols].astype(F32)).astype(BF)
        slope[half, :, cols] = low
        total = col_sum(low.astype(F32))
        if i in dub_started:
            total = total + dub[0:1, cols]
        dub_started.append(i)
        dub[0:1, cols] = total

    def up_grad(j):
        make_a(3 + j, nmg, slope[:, :, j * 512 : (j + 1) * 512].reshape(512, 512))

    for j in range(4):
        task(make_dpre, (DO_DP, j, 0), j, True)
        task(make_dpre, (DO_DP, j, 1), j, False)
        task(up_grad, (DO_GU, j), j)

    def dnorm_mid(half, n):
        acc = None
        for j in range(4):
            part = dot(slope[half, :, j * 512 : (j + 1) * 512], wA[3 + j, n].reshape(256, 512), 1, 1)
            acc = part if acc is None else acc + part
        dh[half, :, n * 256 : (n + 1) * 256] = acc

    for n in range(4):
        task(dnorm_mid, (DO_DNO, n), oy, n)
        task(dnorm_mid, (DO_DNS, n), y, n)

    zero_row = jnp.zeros((1, 1024), F32)

    def back_mid(own):
        half = y if own else oy

        def rows_of(i, carry):
            a, b, d = carry
            rows = pl.ds(pl.multiple_of(i * 64, 64), 64)
            dy = dh[half, rows, :]
            unit, inv = unit_of(h1[half, rows, :])
            total = ln_back(dy, unit, inv, row(1))
            if own:
                total = total + st[rows, :]
            dh[half, rows, :] = total
            low = total.astype(BF)
            dhl[half, rows, :] = low
            return a + col_sum(dy * unit), b + col_sum(dy), d + col_sum(low.astype(F32))

        a, b, d = lax.fori_loop(0, 4, rows_of, (zero_row, zero_row, zero_row))
        add_row(1, a)
        add_row(4, b)
        add_row(8, d)

    task(back_mid, (DO_BACKMID, 0), True)
    task(back_mid, (DO_BACKMID, 1), False)

    def datt(yy, p):
        right = wO[2 * yy + p // 2, p % 2].reshape(128, 1024)
        return dot(dhl[...].reshape(512, 1024), right, 1, 1).reshape(2, 256, 128)

    def da_copy(p):
        cols = pl.ds(p * 128, 128)
        return rc(das.at[:, :, cols], dattg.at[:, :, cols], dsend.at[7 + p], drecv.at[7 + p], ydev)

    def datt_other(p):
        das[:, :, p * 128 : (p + 1) * 128] = datt(oy, p).astype(BF)
        send(da_copy(p))

    for p in range(4):
        task(datt_other, (DO_DAO, p), p)

    def out_grad():
        for i in range(4):
            part = att[:, :, i * 256 : (i + 1) * 256].reshape(512, 256)
            gO[i] = dot(part, dhl[...].reshape(512, 1024), 0, 0).astype(BF).reshape(2, 2, 2, 32, 1024)
        rs_c(11).start()

    task(out_grad, (DO_GO,))

    dqkv = qkv

    def attend_back(p):
        da_copy(p).wait_recv()
        cols = slice(p * 128, p * 128 + 128)
        q2 = qkv[0, :, :, cols]
        k2 = qkv[1, :, :, cols].reshape(512, 128)
        v2 = qkv[2, :, :, cols].reshape(512, 128)
        do2 = (datt(y, p) + dattg[:, :, cols].astype(F32)).astype(BF)
        zero = jnp.zeros((512, 128), BF)
        dks = [None, None]
        dvs = [None, None]
        for half in range(2):
            nk = 256 * (half + 1)
            dq = None
            for e in range(2):
                qe = jnp.where(in_head[e], q2[half], zero[:256])
                doe = jnp.where(in_head[e], do2[half], zero[:256])
                ke = jnp.where(in_head[e], k2[:nk], zero[:nk])
                probs = probs_of(qe, k2, half)
                dprob = dot(doe, v2[:nk], 1, 1)
                delta = jnp.sum(probs * dprob, -1, keepdims=True)
                ds = (probs * (dprob - delta)).astype(BF)
                part = dot(ds, ke)
                dq = part if dq is None else dq + part
                dk = dot(ds, qe, 0, 0)
                dv = dot(probs.astype(BF), doe, 0, 0)
                for kb in range(half + 1):
                    rows = slice(kb * 256, kb * 256 + 256)
                    dks[kb] = dk[rows] if dks[kb] is None else dks[kb] + dk[rows]
                    dvs[kb] = dv[rows] if dvs[kb] is None else dvs[kb] + dv[rows]
            dqkv[0, half, :, cols] = (dq * 0.125).astype(BF)
        for kb in range(2):
            dqkv[1, kb, :, cols] = (dks[kb] * 0.125).astype(BF)
            dqkv[2, kb, :, cols] = dvs[kb].astype(BF)

    for p in range(4):
        task(attend_back, (DO_AB, p), p)

    def qkv_grad(s):
        for cond, cp in rs_sends(3 + s):
            when(cond, cp.wait_send)
        make_a(s, ni, dqkv[s].reshape(512, 512))

    for s in range(3):
        task(qkv_grad, (DO_GQ, s), s)

    def di_copy(i):
        rows = pl.ds(i * 128, 128)
        return rc(prec.at[rows], dnr2.at[rows], msend.at[1 + i], mrecv.at[1 + i], ydev)

    def dnorm_in(own):
        half = y if own else oy
        for n in range(4):
            acc = None
            for s in range(3):
                part = dot(dqkv[s, half], wA[s, n].reshape(256, 512), 1, 1)
                acc = part if acc is None else acc + part
            st[:, n * 256 : (n + 1) * 256] = acc

    def back_in(own, i):
        half = y if own else oy

        def rows_of(k, carry):
            a, b = carry
            rows = pl.ds(pl.multiple_of(k * 64, 64), 64)
            dy = st[rows, :]
            unit, inv = unit_of(tokg[half, rows, :].astype(F32))
            total = dh[half, rows, :] + ln_back(dy, unit, inv, row(0))
            if own:
                dh[half, rows, :] = total
            else:
                prec[rows, :] = total.astype(BF)
            return a + col_sum(dy * unit), b + col_sum(dy)

        a, b = lax.fori_loop(2 * i, 2 * i + 2, rows_of, (zero_row, zero_row))
        add_row(0, a)
        add_row(3, b)
        if not own:
            send(di_copy(i))

    task(dnorm_in, (DO_DIO,), False)
    task(dnorm_in, (DO_DIS,), True)
    for i in range(2):
        task(back_in, (DO_BIO, i), False, i)
        task(back_in, (DO_BIS, i), True, i)

    gin_started = []

    def grad_in(i):
        di_copy(i).wait_recv()
        if not gin_started:
            out_state.wait()
        gin_started.append(i)
        rows = slice(i * 128, i * 128 + 128)
        hgrad[rows, :] = (dh[y, rows, :] + dnr2[rows, :].astype(F32)).astype(BF)
        cp = lc(hgrad.at[pl.ds(i * 128, 128)], gin_out.at[pl.ds(i * 128, 128)], osem.at[2 + i])
        cp.start()
        finals.append(cp)

    for i in range(2):
        task(grad_in, (DO_GIN, i), i)

    def small_grads():
        pg[6:7, head_cols] = col_sum(dqkv[0].reshape(512, 512).astype(F32))
        pg[7:8, head_cols] = col_sum(dqkv[2].reshape(512, 512).astype(F32))
        for d in range(32):
            piece = pg[:, (d // 4) * 128 : (d // 4) * 128 + 128]
            mine = jnp.where(y == d % 2, dub[0:1, (d // 2) * 128 : (d // 2) * 128 + 128], 0.0)
            gP[d // 8, (d // 4) % 2, (d // 2) % 2, d % 2] = jnp.where(row_id == 10, mine, piece)
        rs_c(12).start()

    task(small_grads, (DO_GP,))

    for name in ORDER:
        tasks.pop(name)()
    assert not tasks, sorted(tasks)
    for cp in late_recv:
        cp.wait_recv()
    for cond, cp in pending:
        when(cond, cp.wait_send)
    for cp in finals:
        cp.wait()


def finish_kernel(state, loss, gin, gqkv, gout, gup, gdown, gpk, *refs):
    outs, held, (sem, out_sem) = refs[:11], refs[11:18], refs[18:]
    big = [(state, 0), (loss, 1), (gin, 2), (gqkv, 3), (gout, 4), (gup, 5), (gdown, 6)]
    copies = [pltpu.make_async_copy(src, held[i], sem.at[i]) for src, i in big]
    for cp in copies:
        cp.start()
    quarter = (2 * lax.axis_index("dp") + lax.axis_index("fsdp")) % 4
    total = gpk[...]
    mine = pltpu.roll(total, ((4 - quarter) % 4) * 32, 1)
    outs[7][...] = mine[0:3, 0:32]
    outs[8][...] = mine[3:6, 0:32]
    outs[9][...] = mine[6:10, 0:32]
    outs[10][...] = total[10:11, :]
    results = [pltpu.make_async_copy(held[i], outs[i], out_sem.at[i]) for _, i in big]
    for cp, result in zip(copies, results):
        cp.wait()
        result.start()
    for result in results:
        result.wait()


SCRATCH = dict(
    wA=((7, 4, 2, 2, 64, 512), BF), wD=((8, 4, 2, 2, 128, 128), BF), wO=((4, 2, 2, 2, 32, 1024), BF),
    pk=((4, 2, 2, 2, 16, 128), BF), prm=((16, 1024), F32), ubias=((8, 2048), F32),
    tokg=((2, 256, 1024), BF), ni=((2, 256, 1024), BF), qkv=((3, 2, 256, 512), BF), mask=((512, 512), BF),
    att=((2, 256, 1024), BF), h1=((2, 256, 1024), F32), nmg=((2, 256, 1024), BF),
    gelu=((2, 256, 2048), BF), slope=((2, 256, 2048), BF), st=((256, 1024), F32), prec=((256, 1024), BF),
    hgrad=((256, 1024), BF), ksq=((256, 128), F32), match=((256, 128), F32), dsg=((2, 256, 1024), BF),
    tcol=((256, 1), F32), pcol=((256, 1), F32), lcol=((256, 1), F32), lossb=((1, 256), F32),
    dh=((2, 256, 1024), F32), dhl=((2, 256, 1024), BF), das=((2, 256, 512), BF), dattg=((2, 256, 512), BF),
    dnr2=((256, 1024), BF), sendb=((256, 1024), BF),
    gA=((4, 4, 2, 2, 64, 512), BF), gD=((8, 4, 2, 2, 128, 128), BF), gO=((4, 2, 2, 2, 32, 1024), BF),
    gP=((4, 2, 2, 2, 16, 128), F32),
    dRA=((7, 4, 2, 64, 512), BF), xRA=((7, 4, 64, 512), BF), zRA=((7, 4, 64, 512), BF),
    dRD=((8, 4, 2, 128, 128), BF), xRD=((8, 4, 128, 128), BF), zRD=((8, 4, 128, 128), BF),
    dRO=((4, 2, 2, 32, 1024), BF), yRO=((4, 2, 32, 1024), BF), xRO=((4, 32, 1024), BF), zRO=((4, 32, 1024), BF),
    dRP=((4, 2, 2, 16, 128), F32), yRP=((4, 2, 16, 128), F32), xRP=((4, 16, 128), F32), zRP=((4, 16, 128), F32),
    finA=((7, 2, 32, 512), F32), finD=((8, 128, 128), F32), finO=((32, 1024), F32), finP=((16, 128), F32),
    xOA=((3, 64, 512), BF), xOD=((3, 2, 128, 128), BF), pg=((16, 1024), F32), dub=((8, 2048), F32),
)
SEMS = dict(
    lsem=(15,), ysend=(9,), yrecv=(9,), zsend=(14, 4), zrecv=(14, 4), xsend=(14, 4), xrecv=(14, 4),
    csend=(14,), crecv=(14,), osem=(4,), msend=(3,), mrecv=(3,), asend=(4,), arecv=(4,),
    dsend=(11,), drecv=(11,), psend=(5,), precv=(5,), rcs=(14,), rcr=(14,), rxs=(14,), rxr=(14,),
    rzs=(14, 4), rzr=(14, 4), rys=(14,), ryr=(14,), rfl=(14,), kn_sem=(2,),
)


def on_device_fused(
    tokens, head_grad, w_qkv, w_out, w_up, w_down, gains, shifts, biases, up_bias, seq_lengths,
    neigh_keys, neigh_ids, neigh_counts, targets, p_lm,
):
    keys = neigh_keys.reshape(4, 2, 2, 128, 1024)
    anywhere = pl.BlockSpec(memory_space=pl.ANY)
    vmem = pl.BlockSpec(memory_space=pltpu.VMEM)
    smem = pl.BlockSpec(memory_space=pltpu.SMEM)
    shape = jax.ShapeDtypeStruct
    results = [
        shape((256, 1024), BF),
        shape((1, 256), F32),
        shape((256, 1024), BF),
        shape((32, 3072), F32),
        shape((32, 1024), F32),
        shape((32, 4096), F32),
        shape((128, 1024), F32),
    ]
    held = pl.pallas_call(
        block_kernel,
        out_shape=results + [shape((16, 128), F32)],
        in_specs=[anywhere] * 6 + [vmem] * 4 + [smem, smem, anywhere, vmem, vmem, vmem],
        out_specs=[anywhere] * 8,
        scratch_shapes=[pltpu.VMEM(*SCRATCH[k]) for k in SCRATCH]
        + [pltpu.SemaphoreType.DMA(SEMS[k]) for k in SEMS],
        compiler_params=pltpu.CompilerParams(
            collective_id=0, has_side_effects=True, vmem_limit_bytes=VMEM_LIMIT
        ),
        name="block",
    )(
        tokens, head_grad, w_qkv, w_out, w_up, w_down, gains, shifts, biases, up_bias.reshape(1, 128),
        seq_lengths, neigh_counts.reshape(1, 16), keys, neigh_ids, targets.reshape(1, 256),
        p_lm.reshape(1, 256),
    )
    small = [shape((3, 32), F32), shape((3, 32), F32), shape((4, 32), F32), shape((1, 128), F32)]
    res = pl.pallas_call(
        finish_kernel,
        out_shape=results + small,
        in_specs=[anywhere] * 7 + [vmem],
        out_specs=[anywhere] * 7 + [vmem] * 4,
        scratch_shapes=[pltpu.VMEM(r.shape, r.dtype) for r in results]
        + [pltpu.SemaphoreType.DMA((7,)), pltpu.SemaphoreType.DMA((7,))],
        name="finish",
    )(*held)
    state, loss, gin, gqkv, gout, gup, gdown, dgains, dshifts, dbiases, dub = res
    return (
        state, loss.reshape(256), gin, gqkv, gout, gup, gdown, dgains, dshifts, dbiases, dub.reshape(128),
    )


def solution(mesh):
    in_specs = (
        P(("dp", "fsdp"), None),
        P(("dp", "fsdp"), None),
        P(("dp", "fsdp"), None),
        P(("dp", "fsdp"), None),
        P(("dp", "fsdp"), None),
        P(("dp", "fsdp"), None),
        P(None, ("dp", "fsdp")),
        P(None, ("dp", "fsdp")),
        P(None, ("dp", "fsdp")),
        P(("dp", "fsdp")),
        P("dp", None),
        P(("dp", "fsdp"), None, None),
        P(("dp", "fsdp"), None),
        P(("dp", "fsdp")),
        P(("dp", "fsdp")),
        P(("dp", "fsdp")),
    )
    out_specs = (
        P(("dp", "fsdp"), None),
        P(("dp", "fsdp")),
        P(("dp", "fsdp"), None),
        P(("dp", "fsdp"), None),
        P(("dp", "fsdp"), None),
        P(("dp", "fsdp"), None),
        P(("dp", "fsdp"), None),
        P(None, ("dp", "fsdp")),
        P(None, ("dp", "fsdp")),
        P(None, ("dp", "fsdp")),
        P(("dp", "fsdp")),
    )
    fused = mesh.shape["dp"] == 16 and mesh.shape["fsdp"] == 2
    return jax.shard_map(
        on_device_fused if fused else on_device, mesh=mesh, in_specs=in_specs, out_specs=out_specs, check_vma=False
    )
```
